32 devices in a mesh: groups: 2 (over y), fsdp: 4 (over z), tp: 4 (over x, core).
Axes of the slice: x: 2, y: 2, z: 4, core: 2. Of those that a mesh axis runs over, the one named last changes fastest.
Arguments:
- activations: bfloat16 [4096, 7168], P(('groups', 'fsdp'), 'tp'), parts along dimension 0, may hold values from -6 to 6
- key_grads: bfloat16 [4096, 512], P(('groups', 'fsdp'), 'tp'), parts along dimension 0, may hold values from -0.125 to 0.125
- momentum: float32 [4, 1792, 512], P('tp', 'fsdp')
- second_moment: float32 [4, 1792, 512], P('tp', 'fsdp'), may hold values from 0.05 to 0.5
- left_roots: bfloat16 [4, 4, 896, 896], P('fsdp', 'tp'), as said below
- right_roots: bfloat16 [4, 4, 512, 512], P('fsdp', 'tp'), as said below
- owners: int32 [4, 2], replicated, may hold values from 0 to 3, as said below
Outputs:
- update: float32 [8, 1792, 512], P(('groups', 'tp'), 'fsdp'), parts along dimension 0
- new_momentum: float32 [8, 1792, 512], P(('groups', 'tp'), 'fsdp'), parts along dimension 0
- new_second_moment: float32 [8, 1792, 512], P(('groups', 'tp'), 'fsdp'), parts along dimension 0
The draws below stay inside these ranges and needn't reach their ends.
There are 2 independent parts, one for each index of `groups`. The reference program is written for one: setup_inputs(seed, part) draws one part's arguments, and reference() takes and returns one part's arrays. A program takes and returns all parts, laid end to end along the dimension named above; an argument that names none is the same for every part. Nothing has to cross between parts.
Inputs may be any that keep to these rules, and one draw needn't show every extreme that they name: `owners`: entry [t, b] is the fsdp index whose factors in left_roots and right_roots belong to block b of panel t; the entries of a row differ. `left_roots`: symmetric in the last two dimensions; only the entries named by owners are read. `right_roots`: symmetric in the last two dimensions; only the entries named by owners are read.
All inputs are finite; a program needn't handle non-finite values.
Results may differ from the reference program's by a relative error of at most 0.005.
Values may be sent and summed in bfloat16 or wider, within the bound.
No kernel may reach another device: no remote copies, remote signals or barrier semaphores. Data moves between devices by JAX's collectives and lax.ppermute only.
A program may use at most 64 MiB of HBM per device.

```python
import math
import jax
import jax.numpy as jnp
from jax import lax

D = 7168
BR = 896
STEP = 20
KW = 512
DT = 1792
NBLK = 2
TOKENS = 2048
N_FSDP = 4
N_TP = 4


def root_factor(key, order, span, rise):
    diag_key, off_key = jax.random.split(key)
    positions = jnp.arange(order, dtype=jnp.float32)
    diagonal = jnp.exp(jax.random.uniform(diag_key, (N_FSDP, N_TP, order), minval=0.0, maxval=math.log(span)))
    diagonal = diagonal * (1.0 + rise * positions / (order - 1))
    normal_draw = jax.random.normal(off_key, (N_FSDP, N_TP, order, order), dtype=jnp.float32)
    symmetric = (normal_draw + jnp.swapaxes(normal_draw, 2, 3)) * (0.35 / math.sqrt(2.0 * order))
    unit_core = jnp.eye(order, dtype=jnp.float32) + symmetric
    return (jnp.sqrt(diagonal[..., :, None] * diagonal[..., None, :]) * unit_core).astype(jnp.bfloat16)


def draw_left_roots(key, part):
    key = jax.random.fold_in(key, 5)
    return root_factor(key, BR, 4.0, 2.0)


def draw_right_roots(key, part):
    key = jax.random.fold_in(key, 7)
    return root_factor(key, KW, 10.0, 0.0)


def draw_owners(key, part):
    key = jax.random.fold_in(key, 11)
    score_key, row_key = jax.random.split(key)
    col_ids = jnp.arange(N_FSDP, dtype=jnp.int32)[None, :]
    row_ids = jnp.arange(N_TP, dtype=jnp.int32)[:, None]
    scores = jax.random.randint(score_key, (N_TP, N_FSDP), 0, 1 << 20, dtype=jnp.int32) * N_FSDP + col_ids
    high_row = jax.random.randint(row_key, (), 0, N_TP, dtype=jnp.int32)
    low_row = (high_row + 1) % N_TP
    scores = jnp.where((row_ids == high_row) & (col_ids == N_FSDP - 1), -1, scores)
    scores = jnp.where((row_ids == low_row) & (col_ids == 0), -2, scores)
    ranking = jnp.argsort(scores, axis=1)
    return ranking[:, :NBLK].astype(jnp.int32)


def draw_momentum(key, part):
    key = jax.random.fold_in(key, 23)
    row_key, col_key, noise_key = jax.random.split(key, 3)
    rising = 1.0 + 2.0 * jnp.arange(DT, dtype=jnp.float32) / (DT - 1)
    row_scale = rising[None, :, None] * jnp.exp(jax.random.uniform(row_key, (N_TP, DT, 1), minval=0.0, maxval=math.log(4.0)))
    col_scale = jnp.exp(jax.random.uniform(col_key, (1, 1, KW), minval=0.0, maxval=math.log(10.0)))
    noise = jnp.clip(jax.random.normal(noise_key, (N_TP, DT, KW)), -4.0, 4.0)
    return (0.1 * row_scale * col_scale * noise).astype(jnp.float32)


def strengthened(entries, stream_key, source, target, blocks, factor):
    def block_of(position):
        return (jnp.arange(entries.shape[position]) // (entries.shape[position] // blocks)).reshape((-1,) + (1,) * (entries.ndim - 1 - position))

    one_side = jax.random.permutation(stream_key, blocks)[block_of(target)]
    second = (block_of(target) + blocks // 2) % blocks
    return jnp.where((block_of(source) == one_side) | (block_of(source) == second), factor * entries, entries)


def level_of(rng, extent, cuts, least, top_value):
    factor_of = 1.0
    for dim, shards_of in cuts:
        steps = jax.random.uniform(jax.random.fold_in(jax.random.fold_in(rng, 6), dim), (shards_of,), jnp.float32, least / len(cuts), top_value / len(cuts))
        factor_of = factor_of * jnp.repeat(jnp.exp(steps), extent[dim] // shards_of).reshape((-1,) + (1,) * (len(extent) - 1 - dim))
    return factor_of


def gaussian(stream_key, extent, spread, bound, pieces=(), held_as=jnp.bfloat16):
    factor_of = level_of(stream_key, extent, pieces, -0.22, 0.18) if pieces else 1.0
    drawn = jax.random.normal(stream_key, extent, jnp.float32) * spread * factor_of
    return jnp.minimum(jnp.maximum(drawn, -bound), bound).astype(held_as)


def noise_with(own_key, extent, deviation, reach, cuts, heavy, kind=jnp.bfloat16):
    array = deviation * jax.random.normal(own_key, extent, jnp.float32)
    if cuts:
        array = array * level_of(own_key, extent, cuts, -0.22, 0.18)
    return jnp.clip(strengthened(array, jax.random.fold_in(own_key, 3), *heavy), -reach, reach).astype(kind)


def setup_inputs(seed: int = 0, part: int = 0) -> dict:
    streams_of = jax.random.split(jax.random.key(seed), 8)
    own_keys = jax.random.split(jax.random.fold_in(streams_of[7], part), 8)
    activations = noise_with(own_keys[0], (TOKENS, D), 1.0, 6.0, ((0, 4), (1, 4)), (0, 1, 4, 2.0))
    key_grads = gaussian(own_keys[1], (TOKENS, KW), (TOKENS ** -0.5), 0.125, ((0, 4), (1, 4)))
    momentum = draw_momentum(jax.random.fold_in(streams_of[7], 71), part)
    second_moment = jnp.clip(jnp.exp(math.log(0.5) - 2.3025851 * jax.random.uniform(streams_of[3], (N_TP, DT, KW), jnp.float32) ** level_of(streams_of[3], (N_TP, DT, KW), ((0, 4), (1, 4)), -0.2, 0.2)), 0.05, 0.5)
    left_roots = draw_left_roots(jax.random.fold_in(streams_of[7], 71), part)
    right_roots = draw_right_roots(jax.random.fold_in(streams_of[7], 71), part)
    owners = draw_owners(jax.random.fold_in(streams_of[7], 71), part)
    return dict(activations=activations, key_grads=key_grads, momentum=momentum, second_moment=second_moment, left_roots=left_roots, right_roots=right_roots, owners=owners)


beta_one = 0.9
beta_two = 0.99
adam_eps = 1e-08
norm_eps = 1e-06

def contract_tokens(left_side, right_side):
    return lax.dot_general(left_side, right_side, (((0,), (0,)), ((), ())), preferred_element_type=jnp.float32)

def reference(activations, key_grads, momentum, second_moment, left_roots, right_roots, owners):
    gradient = jnp.stack([contract_tokens(activations[:, tp_index * DT:(tp_index + 1) * DT], key_grads) for tp_index in range(N_TP)])
    new_momentum = beta_one * momentum + (1.0 - beta_one) * gradient
    new_second = beta_two * second_moment + (1.0 - beta_two) * gradient * gradient
    adam_dir = new_momentum / (1.0 - beta_one ** STEP) / (jnp.sqrt(new_second / (1.0 - beta_two ** STEP)) + adam_eps)
    gradient_low = gradient.astype(jnp.bfloat16)
    blocks_low = gradient_low.reshape(N_TP, NBLK, BR, KW)
    updates = []
    for tp_index in range(N_TP):
        adam_sq = jnp.sum(adam_dir[tp_index] * adam_dir[tp_index])
        for block_index in range(NBLK):
            block_owner = owners[tp_index, block_index]
            left_factor = left_roots[block_owner, tp_index]
            right_factor = right_roots[block_owner, tp_index]
            left_product = jnp.dot(left_factor, blocks_low[tp_index, block_index], preferred_element_type=jnp.float32).astype(jnp.bfloat16)
            precond = jnp.dot(left_product, right_factor, preferred_element_type=jnp.float32).astype(jnp.bfloat16)
            widened = lax.optimization_barrier(precond).astype(jnp.float32)
            pre_sq = jnp.sum(widened * widened)
            updates.append(widened * jnp.sqrt(adam_sq / (pre_sq + norm_eps)))
    update = jnp.stack(updates).reshape(N_TP, DT, KW)
    return (update, new_momentum, new_second)
```

```python
import jax
import jax.numpy as jnp
from jax import lax
from jax.sharding import PartitionSpec as P

BR = 896
STEP = 20


beta_one = 0.9
beta_two = 0.99
adam_eps = 1e-08
norm_eps = 1e-06


def spread(value, axis, source):
    kept = jnp.where(lax.axis_index(axis) == source, value, 0).astype(value.dtype)
    return lax.psum(kept, axis)


def contract_tokens(left_side, right_side):
    return lax.dot_general(
        left_side, right_side, (((0,), (0,)), ((), ())), preferred_element_type=jnp.float32
    )


def moments(momentum, second_moment, gradient):
    new_mom = beta_one * momentum + (1.0 - beta_one) * gradient
    new_sec = beta_two * second_moment + (1.0 - beta_two) * gradient * gradient
    adam_dir = (
        new_mom / (1.0 - beta_one**STEP) / (jnp.sqrt(new_sec / (1.0 - beta_two**STEP)) + adam_eps)
    )
    return new_mom, new_sec, jnp.sum(adam_dir * adam_dir)


def general(activations, key_grads, momentum, second_moment, left_roots, right_roots, owners):
    all_heads = lax.all_gather(key_grads, "tp", axis=1, tiled=True)
    panel_rows = activations.shape[1]
    shard_rows = momentum.shape[1]
    columns = all_heads.shape[1]
    blocks = panel_rows // BR
    fsdp_index = lax.axis_index("fsdp")
    tp_index = lax.axis_index("tp")
    first_row = fsdp_index * shard_rows
    my_block = first_row // BR
    offset = first_row - my_block * BR
    summed = lax.psum(contract_tokens(activations, all_heads), "fsdp")
    gradient = lax.dynamic_slice_in_dim(summed, first_row, shard_rows, 0)
    panel_low = summed.astype(jnp.bfloat16)
    new_mom, new_sec, adam_sq = moments(momentum[0], second_moment[0], gradient)
    own_adam = lax.psum(adam_sq, "fsdp")
    owner_row = owners[tp_index]
    owned_slots = owner_row == fsdp_index
    own_block = jnp.sum(jnp.where(owned_slots, jnp.arange(blocks), 0))

    def precondition():
        grad_block = lax.dynamic_slice_in_dim(panel_low, own_block * BR, BR, 0)
        left_product = jnp.dot(
            left_roots[0, 0], grad_block, preferred_element_type=jnp.float32
        ).astype(jnp.bfloat16)
        return jnp.dot(left_product, right_roots[0, 0], preferred_element_type=jnp.float32).astype(
            jnp.bfloat16
        )

    def not_owner():
        return jnp.zeros((BR, columns), jnp.bfloat16)

    result_block = lax.cond(jnp.any(owned_slots), precondition, not_owner)
    update = jnp.zeros((shard_rows, columns), jnp.float32)
    for block_index in range(blocks):
        arrived = spread(result_block, "fsdp", owner_row[block_index])
        widened = lax.optimization_barrier(arrived).astype(jnp.float32)
        pre_sq = jnp.sum(widened * widened)
        my_rows = lax.dynamic_slice_in_dim(widened, offset, shard_rows, 0)
        scaled = my_rows * jnp.sqrt(own_adam / (pre_sq + norm_eps))
        update = jnp.where(my_block == block_index, scaled, update)
    return (update[None], new_mom[None], new_sec[None])


END_TO_INNER = [(0, 1), (3, 2)]
INNER_TO_END = [(1, 0), (2, 3)]
MIDDLE = [(1, 2), (2, 1)]
PAIR = [(0, 1), (1, 0), (2, 3), (3, 2)]
ACROSS = [(0, 2), (2, 0), (1, 3), (3, 1)]
OTHER_GROUP = [(0, 1), (1, 0)]


def line_of_four(activations, key_grads, momentum, second_moment, left_roots, right_roots, owners):
    low = jnp.bfloat16
    group = lax.axis_index("groups")
    z = lax.axis_index("fsdp")
    tp_index = lax.axis_index("tp")
    side = z // 2
    is_end = (z == 0) | (z == 3)
    shard_rows, columns = momentum.shape[1:]
    half_columns = columns // 2
    send = lambda value, perm: lax.ppermute(value, "fsdp", perm)

    own_key = key_grads
    core_key = lax.ppermute(own_key, "tp", [(i, i ^ 1) for i in range(4)])
    far_key = lax.ppermute(own_key, "tp", [(i, i ^ 2) for i in range(4)])
    far_core_key = lax.ppermute(far_key, "tp", [(i, i ^ 1) for i in range(4)])
    odd = tp_index % 2 == 1
    joined = lambda one, two: jnp.where(
        odd, jnp.concatenate([two, one], 1), jnp.concatenate([one, two], 1)
    )
    keys = [joined(own_key, core_key), joined(far_key, far_core_key)]
    chunk_index = [tp_index // 2, 1 - tp_index // 2]

    left = left_roots[0, 0]
    right = right_roots[0, 0]
    halves = [
        lax.dynamic_slice_in_dim(root, group * (root.shape[0] // 2), root.shape[0] // 2, 0)
        for root in (right, left)
    ]
    owner_row = owners[tp_index]
    near_owner = owner_row[side]
    far_owner = owner_row[1 - side]
    end_z = jnp.where(side == 0, 0, 3)
    gathered = []
    for half in halves:
        from_end = send(half, END_TO_INNER)
        across = send(jnp.where(far_owner == z, half, from_end), MIDDLE)
        gathered.append(
            jnp.where(near_owner == z, half, jnp.where(near_owner == end_z, from_end, across))
        )
    right_half, left_half = gathered
    left_other = lax.ppermute(left_half, "groups", OTHER_GROUP)
    right_half = jnp.where(is_end, send(right_half, INNER_TO_END), right_half)
    right_other = lax.ppermute(right_half, "groups", OTHER_GROUP)
    end_left = jnp.where(group == side, left_half, left_other)
    inner_left = jnp.where(group == side, left_other, left_half)

    far_part = lax.dynamic_slice_in_dim(activations, (1 - side) * BR, BR, 1)
    near_part = lax.dynamic_slice_in_dim(activations, side * BR, BR, 1)
    product = jnp.zeros((shard_rows, columns), jnp.float32)
    grads = []
    for keys_c, index_c in zip(keys, chunk_index):
        far = contract_tokens(far_part, keys_c)
        far_sum = (far + send(far.astype(low), END_TO_INNER).astype(jnp.float32)).astype(low)
        arrived = send(far_sum, MIDDLE)
        near = contract_tokens(near_part, keys_c)
        from_end = send(near.astype(low), END_TO_INNER)
        grad = near + from_end.astype(jnp.float32) + arrived.astype(jnp.float32)
        grad_low = grad.astype(low)
        end_grad = send(
            lax.dynamic_slice_in_dim(grad_low, side * shard_rows, shard_rows, 0), INNER_TO_END
        )
        inner_grad = lax.dynamic_slice_in_dim(grad, (1 - side) * shard_rows, shard_rows, 0)
        grads.append(jnp.where(is_end, end_grad.astype(jnp.float32), inner_grad))
        end_product = jnp.dot(end_left, grad_low, preferred_element_type=jnp.float32).astype(low)
        inner_product = jnp.dot(inner_left, grad_low, preferred_element_type=jnp.float32).astype(low)
        left_product = jnp.where(is_end, send(end_product, INNER_TO_END), inner_product)
        right_c = jnp.where(group == index_c, right_half, right_other)
        product = product + jnp.dot(left_product, right_c, preferred_element_type=jnp.float32)

    swapped = tp_index >= 2
    gradient = jnp.where(
        swapped, jnp.concatenate(grads[::-1], 1), jnp.concatenate(grads, 1)
    )
    new_mom, new_sec, adam_sq = moments(momentum[0], second_moment[0], gradient)
    adam_sq = adam_sq + send(adam_sq, PAIR)
    adam_sq = adam_sq + send(adam_sq, ACROSS)
    pre_sq = jnp.sum(product * product)
    pre_sq = pre_sq + send(pre_sq, PAIR)
    update = product * jnp.sqrt(adam_sq / (pre_sq + norm_eps))
    return (update[None], new_mom[None], new_sec[None])


def solution(mesh):
    def per_device(activations, key_grads, momentum, *rest):
        fits = (
            mesh.shape["fsdp"] == 4
            and mesh.shape["tp"] == 4
            and mesh.shape["groups"] == 2
            and momentum.shape[1] * 2 == BR
            and activations.shape[1] == 2 * BR
        )
        return (line_of_four if fits else general)(activations, key_grads, momentum, *rest)

    return jax.shard_map(
        per_device,
        mesh=mesh,
        in_specs=(
            P(("groups", "fsdp"), "tp"),
            P(("groups", "fsdp"), "tp"),
            P("tp", "fsdp", None),
            P("tp", "fsdp", None),
            P("fsdp", "tp", None, None),
            P("fsdp", "tp", None, None),
            P(),
        ),
        out_specs=(
            P(("groups", "tp"), "fsdp", None),
            P(("groups", "tp"), "fsdp", None),
            P(("groups", "tp"), "fsdp", None),
        ),
        check_vma=False,
    )
```

```python
import jax
import jax.numpy as jnp
from jax import lax
from jax.sharding import PartitionSpec as P

BR = 896
STEP = 20


beta_one = 0.9
beta_two = 0.99
adam_eps = 1e-08
norm_eps = 1e-06


def spread(value, axis, source):
    kept = jnp.where(lax.axis_index(axis) == source, value, 0).astype(value.dtype)
    return lax.psum(kept, axis)


def contract_tokens(left_side, right_side):
    return lax.dot_general(
        left_side, right_side, (((0,), (0,)), ((), ())), preferred_element_type=jnp.float32
    )


def moments(momentum, second_moment, gradient):
    new_mom = beta_one * momentum + (1.0 - beta_one) * gradient
    new_sec = beta_two * second_moment + (1.0 - beta_two) * gradient * gradient
    adam_dir = (
        new_mom / (1.0 - beta_one**STEP) / (jnp.sqrt(new_sec / (1.0 - beta_two**STEP)) + adam_eps)
    )
    return new_mom, new_sec, jnp.sum(adam_dir * adam_dir)


def general(activations, key_grads, momentum, second_moment, left_roots, right_roots, owners):
    all_heads = lax.all_gather(key_grads, "tp", axis=1, tiled=True)
    panel_rows = activations.shape[1]
    shard_rows = momentum.shape[1]
    columns = all_heads.shape[1]
    blocks = panel_rows // BR
    fsdp_index = lax.axis_index("fsdp")
    tp_index = lax.axis_index("tp")
    first_row = fsdp_index * shard_rows
    my_block = first_row // BR
    offset = first_row - my_block * BR
    summed = lax.psum(contract_tokens(activations, all_heads), "fsdp")
    gradient = lax.dynamic_slice_in_dim(summed, first_row, shard_rows, 0)
    panel_low = summed.astype(jnp.bfloat16)
    new_mom, new_sec, adam_sq = moments(momentum[0], second_moment[0], gradient)
    own_adam = lax.psum(adam_sq, "fsdp")
    owner_row = owners[tp_index]
    owned_slots = owner_row == fsdp_index
    own_block = jnp.sum(jnp.where(owned_slots, jnp.arange(blocks), 0))

    def precondition():
        grad_block = lax.dynamic_slice_in_dim(panel_low, own_block * BR, BR, 0)
        left_product = jnp.dot(
            left_roots[0, 0], grad_block, preferred_element_type=jnp.float32
        ).astype(jnp.bfloat16)
        return jnp.dot(left_product, right_roots[0, 0], preferred_element_type=jnp.float32).astype(
            jnp.bfloat16
        )

    def not_owner():
        return jnp.zeros((BR, columns), jnp.bfloat16)

    result_block = lax.cond(jnp.any(owned_slots), precondition, not_owner)
    update = jnp.zeros((shard_rows, columns), jnp.float32)
    for block_index in range(blocks):
        arrived = spread(result_block, "fsdp", owner_row[block_index])
        widened = lax.optimization_barrier(arrived).astype(jnp.float32)
        pre_sq = jnp.sum(widened * widened)
        my_rows = lax.dynamic_slice_in_dim(widened, offset, shard_rows, 0)
        scaled = my_rows * jnp.sqrt(own_adam / (pre_sq + norm_eps))
        update = jnp.where(my_block == block_index, scaled, update)
    return (update[None], new_mom[None], new_sec[None])


def after(value, *others):
    return lax.optimization_barrier((value, *others))[0]


END_TO_INNER = [(0, 1), (3, 2)]
INNER_TO_END = [(1, 0), (2, 3)]
MIDDLE = [(1, 2), (2, 1)]
PAIR = [(0, 1), (1, 0), (2, 3), (3, 2)]
ACROSS = [(0, 2), (2, 0), (1, 3), (3, 1)]
OTHER_GROUP = [(0, 1), (1, 0)]


def line_of_four(activations, key_grads, momentum, second_moment, left_roots, right_roots, owners):
    low = jnp.bfloat16
    group = lax.axis_index("groups")
    z = lax.axis_index("fsdp")
    tp_index = lax.axis_index("tp")
    side = z // 2
    is_end = (z == 0) | (z == 3)
    shard_rows, columns = momentum.shape[1:]
    half_columns = columns // 2
    send = lambda value, perm: lax.ppermute(value, "fsdp", perm)

    own_key = key_grads
    core_key = lax.ppermute(own_key, "tp", [(i, i ^ 1) for i in range(4)])
    far_key = lax.ppermute(own_key, "tp", [(i, i ^ 2) for i in range(4)])
    far_core_key = lax.ppermute(far_key, "tp", [(i, i ^ 1) for i in range(4)])
    odd = tp_index % 2 == 1
    joined = lambda one, two: jnp.where(
        odd, jnp.concatenate([two, one], 1), jnp.concatenate([one, two], 1)
    )
    keys = [joined(own_key, core_key), joined(far_key, far_core_key)]
    chunk_index = [tp_index // 2, 1 - tp_index // 2]

    left = left_roots[0, 0]
    right = right_roots[0, 0]
    quarter = left.shape[0] // 4
    pieces = [
        lax.dynamic_slice_in_dim(left, group * 2 * quarter, quarter, 0),
        lax.dynamic_slice_in_dim(left, group * 2 * quarter + quarter, quarter, 0),
        lax.dynamic_slice_in_dim(right, group * half_columns, half_columns, 0),
    ]
    owner_row = owners[tp_index]
    near_owner = owner_row[side]
    far_owner = owner_row[1 - side]
    end_z = jnp.where(side == 0, 0, 3)
    far_part = lax.dynamic_slice_in_dim(activations, (1 - side) * BR, BR, 1)
    near_part = lax.dynamic_slice_in_dim(activations, side * BR, BR, 1)

    sent = []

    def end_to_inner(value):
        if len(sent) >= 2:
            value = after(value, sent[-2])
        sent.append(send(value, END_TO_INNER))
        return sent[-1]

    from_end = [end_to_inner(piece) for piece in pieces]
    far_sums, far_arrived = [], []
    for keys_c in keys:
        far = contract_tokens(far_part, keys_c)
        far_sums.append((far + end_to_inner(far.astype(low)).astype(jnp.float32)).astype(low))
    nears = []
    for keys_c in keys:
        near = contract_tokens(near_part, keys_c)
        nears.append(near + end_to_inner(near.astype(low)).astype(jnp.float32))
    crossed = []

    def middle(value):
        if len(crossed) >= 2:
            value = after(value, crossed[-2])
        crossed.append(send(value, MIDDLE))
        return crossed[-1]

    gathered = []
    for piece, got in zip(pieces, from_end):
        across = middle(jnp.where(far_owner == z, piece, got))
        gathered.append(
            jnp.where(near_owner == z, piece, jnp.where(near_owner == end_z, got, across))
        )
    far_arrived = [middle(value) for value in far_sums]
    others = [lax.ppermute(piece, "groups", OTHER_GROUP) for piece in gathered[:2]]
    right_half = jnp.where(is_end, send(gathered[2], INNER_TO_END), gathered[2])
    right_other = lax.ppermute(right_half, "groups", OTHER_GROUP)
    end_left = [jnp.where(group == side, a, b) for a, b in zip(gathered, others)]
    inner_left = [jnp.where(group == side, b, a) for a, b in zip(gathered, others)]
    times = lambda rows, grad_low: jnp.concatenate(
        [jnp.dot(r, grad_low, preferred_element_type=jnp.float32).astype(low) for r in rows], 0
    )

    product = jnp.zeros((shard_rows, columns), jnp.float32)
    grads = []
    for near, arrived, index_c in zip(nears, far_arrived, chunk_index):
        grad = near + arrived.astype(jnp.float32)
        grad_low = grad.astype(low)
        end_grad = send(
            lax.dynamic_slice_in_dim(grad_low, side * shard_rows, shard_rows, 0), INNER_TO_END
        )
        inner_grad = lax.dynamic_slice_in_dim(grad, (1 - side) * shard_rows, shard_rows, 0)
        grads.append(jnp.where(is_end, end_grad.astype(jnp.float32), inner_grad))
        end_product = times(end_left, grad_low)
        inner_product = times(inner_left, grad_low)
        left_product = jnp.where(is_end, send(end_product, INNER_TO_END), inner_product)
        right_c = jnp.where(group == index_c, right_half, right_other)
        product = product + jnp.dot(left_product, right_c, preferred_element_type=jnp.float32)

    swapped = tp_index >= 2
    gradient = jnp.where(
        swapped, jnp.concatenate(grads[::-1], 1), jnp.concatenate(grads, 1)
    )
    new_mom, new_sec, adam_sq = moments(momentum[0], second_moment[0], gradient)
    adam_sq = adam_sq + send(adam_sq, PAIR)
    adam_sq = adam_sq + send(adam_sq, ACROSS)
    pre_sq = jnp.sum(product * product)
    pre_sq = pre_sq + send(pre_sq, PAIR)
    update = product * jnp.sqrt(adam_sq / (pre_sq + norm_eps))
    return (update[None], new_mom[None], new_sec[None])


def solution(mesh):
    def per_device(activations, key_grads, momentum, *rest):
        fits = (
            mesh.shape["fsdp"] == 4
            and mesh.shape["tp"] == 4
            and mesh.shape["groups"] == 2
            and momentum.shape[1] * 2 == BR
            and activations.shape[1] == 2 * BR
        )
        return (line_of_four if fits else general)(activations, key_grads, momentum, *rest)

    return jax.shard_map(
        per_device,
        mesh=mesh,
        in_specs=(
            P(("groups", "fsdp"), "tp"),
            P(("groups", "fsdp"), "tp"),
            P("tp", "fsdp", None),
            P("tp", "fsdp", None),
            P("fsdp", "tp", None, None),
            P("fsdp", "tp", None, None),
            P(),
        ),
        out_specs=(
            P(("groups", "tp"), "fsdp", None),
            P(("groups", "tp"), "fsdp", None),
            P(("groups", "tp"), "fsdp", None),
        ),
        check_vma=False,
    )
```

```python
import functools

import jax
import jax.numpy as jnp
from jax import lax
from jax.experimental import pallas as pl
from jax.experimental.pallas import tpu as pltpu
from jax.sharding import PartitionSpec as P

BR = 896
STEP = 20


beta_one = 0.9
beta_two = 0.99
adam_eps = 1e-08
norm_eps = 1e-06


def spread(value, axis, source):
    kept = jnp.where(lax.axis_index(axis) == source, value, 0).astype(value.dtype)
    return lax.psum(kept, axis)


def contract_tokens(left_side, right_side):
    return lax.dot_general(
        left_side, right_side, (((0,), (0,)), ((), ())), preferred_element_type=jnp.float32
    )


def moments(momentum, second_moment, gradient):
    new_mom = beta_one * momentum + (1.0 - beta_one) * gradient
    new_sec = beta_two * second_moment + (1.0 - beta_two) * gradient * gradient
    adam_dir = (
        new_mom / (1.0 - beta_one**STEP) / (jnp.sqrt(new_sec / (1.0 - beta_two**STEP)) + adam_eps)
    )
    return new_mom, new_sec, jnp.sum(adam_dir * adam_dir)


def general(activations, key_grads, momentum, second_moment, left_roots, right_roots, owners):
    all_heads = lax.all_gather(key_grads, "tp", axis=1, tiled=True)
    panel_rows = activations.shape[1]
    shard_rows = momentum.shape[1]
    columns = all_heads.shape[1]
    blocks = panel_rows // BR
    fsdp_index = lax.axis_index("fsdp")
    tp_index = lax.axis_index("tp")
    first_row = fsdp_index * shard_rows
    my_block = first_row // BR
    offset = first_row - my_block * BR
    summed = lax.psum(contract_tokens(activations, all_heads), "fsdp")
    gradient = lax.dynamic_slice_in_dim(summed, first_row, shard_rows, 0)
    panel_low = summed.astype(jnp.bfloat16)
    new_mom, new_sec, adam_sq = moments(momentum[0], second_moment[0], gradient)
    own_adam = lax.psum(adam_sq, "fsdp")
    owner_row = owners[tp_index]
    owned_slots = owner_row == fsdp_index
    own_block = jnp.sum(jnp.where(owned_slots, jnp.arange(blocks), 0))

    def precondition():
        grad_block = lax.dynamic_slice_in_dim(panel_low, own_block * BR, BR, 0)
        left_product = jnp.dot(
            left_roots[0, 0], grad_block, preferred_element_type=jnp.float32
        ).astype(jnp.bfloat16)
        return jnp.dot(left_product, right_roots[0, 0], preferred_element_type=jnp.float32).astype(
            jnp.bfloat16
        )

    def not_owner():
        return jnp.zeros((BR, columns), jnp.bfloat16)

    result_block = lax.cond(jnp.any(owned_slots), precondition, not_owner)
    update = jnp.zeros((shard_rows, columns), jnp.float32)
    for block_index in range(blocks):
        arrived = spread(result_block, "fsdp", owner_row[block_index])
        widened = lax.optimization_barrier(arrived).astype(jnp.float32)
        pre_sq = jnp.sum(widened * widened)
        my_rows = lax.dynamic_slice_in_dim(widened, offset, shard_rows, 0)
        scaled = my_rows * jnp.sqrt(own_adam / (pre_sq + norm_eps))
        update = jnp.where(my_block == block_index, scaled, update)
    return (update[None], new_mom[None], new_sec[None])


def after(value, *others):
    return lax.optimization_barrier((value, *others))[0]


END_TO_INNER = [(0, 1), (3, 2)]
INNER_TO_END = [(1, 0), (2, 3)]
MIDDLE = [(1, 2), (2, 1)]
PAIR = [(0, 1), (1, 0), (2, 3), (3, 2)]
ACROSS = [(0, 2), (2, 0), (1, 3), (3, 1)]
MIRROR = [(0, 3), (3, 0), (1, 2), (2, 1)]
INNER_GROUPS = [(1, 5), (5, 1), (2, 6), (6, 2)]

TILE = 128
MIB = 1024 * 1024
COSTS = (0, 0, 0, 0, 0, 0, 0, 20, 0, 0, 0, 0, 0, 0)
SCALARS = pl.BlockSpec(memory_space=pltpu.SMEM)
IN_PLACE = pl.BlockSpec(memory_space=pl.ANY)
GROUP, SIDE, IS_END, CHUNK = 0, 1, 2, 3
ACROSS_OWN, PICK = 0, 1


def spec_of(array):
    if len(array.shape) == 1:
        return SCALARS
    return pl.BlockSpec(array.shape, lambda i: (0,) * len(array.shape))


def on_device(kernel, scalars, inputs, outputs, scratch=(), in_place=(), aliases=None, flops=1):
    return pl.pallas_call(
        kernel,
        grid=(1,),
        in_specs=[SCALARS]
        + [IN_PLACE if k in in_place else spec_of(array) for k, array in enumerate(inputs)],
        out_specs=[spec_of(shape) for shape in outputs],
        out_shape=list(outputs),
        scratch_shapes=list(scratch),
        input_output_aliases=aliases or {},
        cost_estimate=pl.CostEstimate(flops=flops, bytes_accessed=1, transcendentals=0),
        compiler_params=pltpu.CompilerParams(vmem_limit_bytes=32 * MIB),
    )(scalars, *inputs)


def packing(left_rows, right_rows):
    upper = lambda root, rows: [
        (root, i, j) for i in range(rows // TILE) for j in range(i, rows // TILE)
    ]
    lefts, rights = upper(0, left_rows), upper(1, right_rows)
    first, second = len(lefts) // 2, len(rights) // 2
    return [lefts[:first] + rights[:second], lefts[first:] + rights[second:]]


def spots(pieces):
    return [(piece, pl.ds(row, TILE)) for piece in pieces for row in range(0, piece.shape[0], TILE)]


def pack_kernel(lists, left_ref, right_ref, *refs):
    *pieces, copied = refs
    for group, places in enumerate(lists):

        @pl.when(lax.axis_index("groups") == group)
        def _():
            copies = [
                pltpu.make_async_copy(
                    (left_ref, right_ref)[root].at[
                        pl.ds(i * TILE, TILE), pl.ds(j * TILE, TILE)
                    ],
                    piece.at[rows, :],
                    copied.at[k],
                )
                for k, ((root, i, j), (piece, rows)) in enumerate(zip(places, spots(pieces)))
            ]
            for copy in copies:
                copy.start()
            for copy in copies:
                copy.wait()


def unpack_kernel(lists, place_ref, *refs):
    *pieces, left_ref, right_ref = refs
    count = len(pieces) // 2

    def fill(places, held):
        for (root, i, j), (piece, rows) in zip(places, spots(held)):
            target = (left_ref, right_ref)[root]
            tile = piece[rows, :]
            target[pl.ds(i * TILE, TILE), pl.ds(j * TILE, TILE)] = tile
            if i != j:
                target[pl.ds(j * TILE, TILE), pl.ds(i * TILE, TILE)] = tile.T

    for group in range(2):

        @pl.when((place_ref[GROUP] == group) & (place_ref[IS_END] == 0))
        def _():
            fill(lists[group], pieces[:count])
            fill(lists[1 - group], pieces[count:])


def choose_kernel(which, count, choice_ref, *refs):
    *sources, out_ref, copied = refs
    choices = len(sources) // count
    for k in range(choices):

        @pl.when(choice_ref[which] == k)
        def _():
            copies, row = [], 0
            for n, source in enumerate(sources[k::choices]):
                target = out_ref.at[pl.ds(row, source.shape[0]), :]
                copies.append(pltpu.make_async_copy(source, target, copied.at[n]))
                row += source.shape[0]
            for copy in copies:
                copy.start()
            for copy in copies:
                copy.wait()


def partial_kernel(place_ref, keys_ref, activations_ref, far_low_ref, near_ref, near_low_ref):
    def block_of(index):
        own = activations_ref[:, pl.ds(pl.multiple_of(index * BR, TILE), BR)]
        return contract_tokens(own, keys_ref[...])

    near = block_of(place_ref[SIDE])
    near_ref[...] = near

    @pl.when(place_ref[IS_END] == 1)
    def _():
        near_low_ref[...] = near.astype(jnp.bfloat16)
        far_low_ref[...] = block_of(1 - place_ref[SIDE]).astype(jnp.bfloat16)


def far_kernel(place_ref, from_end_ref, keys_ref, activations_ref, sum_ref):
    @pl.when(place_ref[IS_END] == 0)
    def _():
        columns = pl.ds(pl.multiple_of((1 - place_ref[SIDE]) * BR, TILE), BR)
        far = contract_tokens(activations_ref[:, columns], keys_ref[...])
        sum_ref[...] = (far + wide(from_end_ref)).astype(jnp.bfloat16)


def rows_of(place_ref, end, rows):
    index = place_ref[SIDE] if end else 1 - place_ref[SIDE]
    return pl.ds(pl.multiple_of(index * rows, 64), rows)


def wide(ref, which=slice(None)):
    return ref[which, :].astype(jnp.float32)


def rest_kernel(place_ref, arrived_b_ref, arrived_a_ref, near_b_ref, near_a_ref, rest_ref):
    @pl.when(place_ref[IS_END] == 0)
    def _():
        which = rows_of(place_ref, True, rest_ref.shape[0])
        width = near_a_ref.shape[1]
        for c, (near_ref, arrived_ref) in enumerate(
            ((near_a_ref, arrived_a_ref), (near_b_ref, arrived_b_ref))
        ):
            rest_ref[:, c * width : (c + 1) * width] = (
                near_ref[which, :] + wide(arrived_ref, which)
            ).astype(jnp.bfloat16)


def near_gradient(place_ref, from_end_ref, near_ref, arrived_ref, grad_ref, low_ref):
    rows = grad_ref.shape[0]
    for end in (False, True):
        which = rows_of(place_ref, end, rows)
        grad = near_ref[which, :] + wide(from_end_ref, which) + wide(arrived_ref, which)
        low_ref[which, :] = grad.astype(jnp.bfloat16)
        if not end:
            grad_ref[...] = grad


def gradient_kernel(place_ref, from_end_ref, near_ref, arrived_ref, grad_ref, low_ref):
    @pl.when(place_ref[IS_END] == 0)
    def _():
        near_gradient(place_ref, from_end_ref, near_ref, arrived_ref, grad_ref, low_ref)


def left_product(low_ref, left_ref, product_ref):
    product_ref[...] = jnp.dot(
        left_ref[...], low_ref[...], preferred_element_type=jnp.float32
    ).astype(jnp.bfloat16)


def left_kernel(place_ref, low_ref, left_ref, product_ref):
    @pl.when(place_ref[IS_END] == 0)
    def _():
        left_product(low_ref, left_ref, product_ref)


def chunk_columns(place_ref, chunk, width):
    return pl.ds(pl.multiple_of(place_ref[CHUNK + chunk] * width, TILE), width)


def last_kernel(
    place_ref, from_end_ref, near_ref, arrived_ref, left_ref, before_ref, right_ref,
    grad_ref, end_ref, own_ref, square_ref, low_ref, product_ref,
):
    @pl.when(place_ref[IS_END] == 0)
    def _():
        near_gradient(place_ref, from_end_ref, near_ref, arrived_ref, grad_ref, low_ref)
        left_product(low_ref, left_ref, product_ref)
        square = 0.0
        for end, out_ref in ((True, end_ref), (False, own_ref)):
            rows = rows_of(place_ref, end, out_ref.shape[0])
            total = 0.0
            for c, ref in enumerate((before_ref, product_ref)):
                which = chunk_columns(place_ref, c, ref.shape[1])
                total = total + jnp.dot(
                    ref[rows, :], right_ref[which, :], preferred_element_type=jnp.float32
                )
            square = square + jnp.sum(total * total)
            out_ref[...] = total.astype(out_ref.dtype)
        square_ref[0] = square

    @pl.when(place_ref[IS_END] == 1)
    def _():
        square_ref[0] = 0.0


def moments_kernel(inner, place_ref, *refs):
    if inner:
        grad_ref, mom_ref, sec_ref, new_mom_ref, new_sec_ref, sums_ref = refs
    else:
        (
            grad_ref, mom_ref, sec_ref, rest_ref, near_a_ref, near_b_ref, square_ref,
            before_mom_ref, before_sec_ref, before_ref, new_mom_ref, new_sec_ref, sums_ref,
        ) = refs
    rows, width = grad_ref.shape

    def finish(chunk, grad):
        columns = chunk_columns(place_ref, chunk, width)
        new_mom, new_sec, adam_sq = moments(mom_ref[0, :, columns], sec_ref[0, :, columns], grad)
        new_mom_ref[0, :, columns] = new_mom
        new_sec_ref[0, :, columns] = new_sec
        return adam_sq

    @pl.when(place_ref[IS_END] == 0)
    def _():
        if inner:
            sums_ref[0] = finish(0, grad_ref[...])
            sums_ref[1] = 0.0
        else:
            columns = chunk_columns(place_ref, 0, width)
            new_mom_ref[0, :, columns] = before_mom_ref[0, :, columns]
            new_sec_ref[0, :, columns] = before_sec_ref[0, :, columns]
            sums_ref[0] = finish(1, grad_ref[...]) + before_ref[0]
            sums_ref[1] = square_ref[0]

    if not inner:

        @pl.when(place_ref[IS_END] == 1)
        def _():
            which = rows_of(place_ref, True, rows)
            total = 0.0
            for c, near_ref in enumerate((near_a_ref, near_b_ref)):
                rest = rest_ref[:, c * width : (c + 1) * width].astype(jnp.float32)
                total = total + finish(c, near_ref[which, :] + rest)
            sums_ref[0] = total
            sums_ref[1] = 0.0


def update_kernel(place_ref, end_ref, own_ref, sums_ref, pair_ref, across_ref, mirror_ref, update_ref):
    adam_sq = sums_ref[0] + pair_ref[0] + across_ref[0] + mirror_ref[0]
    pre_sq = sums_ref[1] + pair_ref[1]
    ones = jnp.ones((1, TILE), jnp.float32)
    scale = jnp.sqrt((adam_sq * ones) / (pre_sq * ones + norm_eps))[:, :1]

    @pl.when(place_ref[IS_END] == 0)
    def _():
        update_ref[0] = own_ref[...] * scale

    @pl.when(place_ref[IS_END] == 1)
    def _():
        update_ref[0] = wide(end_ref) * scale


def line_of_four(activations, key_grads, momentum, second_moment, left_roots, right_roots, owners):
    low = jnp.bfloat16
    group = lax.axis_index("groups")
    z = lax.axis_index("fsdp")
    tp_index = lax.axis_index("tp")
    side = z // 2
    is_end = (z == 0) | (z == 3)
    rows, columns = momentum.shape[1:]
    width = columns // 2
    stacked = lambda *values: jnp.stack(values).astype(jnp.int32)
    place = stacked(group, side, is_end.astype(jnp.int32), tp_index // 2, 1 - tp_index // 2)
    owner_row = owners[tp_index]
    near_owner = owner_row[side]
    far_owner = owner_row[1 - side]
    choice = stacked(
        jnp.where(far_owner == z, 0, 1),
        jnp.where(near_owner == z, 0, jnp.where(near_owner == jnp.where(side == 0, 0, 3), 1, 2)),
    )
    send = lambda value, perm: lax.ppermute(value, "fsdp", perm)
    shape = jax.ShapeDtypeStruct
    history = []

    def step(kernel, inputs, outputs, scalars=place, **kwargs):
        if history:
            inputs = [after(inputs[0], history[-1]), *inputs[1:]]
        flops = 1 + 115_000_000 * COSTS[len(history) - 1]
        out = on_device(kernel, scalars, inputs, outputs, flops=flops, **kwargs)
        history.append(out[0])
        return out

    left = left_roots[0, 0]
    right = right_roots[0, 0]
    lists = packing(left.shape[0], right.shape[0])
    count = len(lists[0])
    piece_shapes = [
        shape((tiles * TILE, TILE), low) for tiles in ((count + 1) // 2, count // 2)
    ]
    pieces = pl.pallas_call(
        functools.partial(pack_kernel, lists),
        in_specs=[IN_PLACE] * 2,
        out_specs=[pl.BlockSpec(memory_space=pltpu.VMEM)] * 2,
        out_shape=piece_shapes,
        scratch_shapes=[pltpu.SemaphoreType.DMA((count,))],
        compiler_params=pltpu.CompilerParams(vmem_limit_bytes=56 * MIB),
    )(left, right)
    history.append(pieces[0])
    root_end = [send(piece, END_TO_INNER) for piece in pieces]

    first_key = after(key_grads, history[-1])
    far_key = lax.ppermute(first_key, "tp", [(i, i ^ 2) for i in range(4)])
    core_key = lax.ppermute(first_key, "tp", [(i, i ^ 1) for i in range(4)])
    far_core_key = lax.ppermute(far_key, "tp", [(i, i ^ 1) for i in range(4)])
    odd = tp_index % 2 == 1
    joined = lambda one, two: jnp.where(
        odd, jnp.concatenate([two, one], 1), jnp.concatenate([one, two], 1)
    )
    keys_a, keys_b = joined(key_grads, core_key), joined(far_key, far_core_key)
    half = shape((rows, width), jnp.float32)
    block = shape((2 * rows, width), low)

    def partials(keys):
        return step(
            partial_kernel, [keys, activations], [block, shape(block.shape, jnp.float32), block]
        )

    def choose(which, *sources):
        rows = sum(options[0].shape[0] for options in sources)
        (out,) = step(
            functools.partial(choose_kernel, which, len(sources)),
            [array for options in sources for array in options],
            [shape((rows, TILE), low)],
            scalars=choice,
            scratch=[pltpu.SemaphoreType.DMA((len(sources),))],
            in_place=range(len(sources) * len(sources[0])),
        )
        return out

    def far_sum(from_end, keys):
        (out,) = step(far_kernel, [from_end, keys, activations], [block])
        return out

    def cross(k):
        return send(choose(ACROSS_OWN, [pieces[k], root_end[k]]), MIDDLE)

    other_group = lambda value: lax.ppermute(value, ("groups", "fsdp"), INNER_GROUPS)
    far_low_a, near_a, near_low_a = partials(keys_a)
    far_end_a = send(far_low_a, END_TO_INNER)
    far_low_b, near_b, near_low_b = partials(keys_b)
    across = [cross(0)]
    far_end_b = send(after(far_low_b, root_end[1]), END_TO_INNER)
    across.append(cross(1))
    far_sum_a = far_sum(far_end_a, keys_a)
    near_end_a = send(after(near_low_a, far_end_a), END_TO_INNER)
    arrived_a = send(far_sum_a, MIDDLE)
    picked = choose(PICK, *zip(pieces, root_end, across))
    other = other_group(picked)
    far_sum_b = far_sum(far_end_b, keys_b)
    near_end_b = send(after(near_low_b, far_end_b), END_TO_INNER)
    arrived_b = send(far_sum_b, MIDDLE)
    full = shape((rows, columns), jnp.float32)
    sums_shape = shape((2,), jnp.float32)
    grad_a, low_a = step(
        gradient_kernel, [near_end_a, near_a, arrived_a], [half, block]
    )
    block_left, block_right = step(
        functools.partial(unpack_kernel, lists),
        [picked, other],
        [shape(left.shape, low), shape(right.shape, low)],
    )
    (rest,) = step(
        rest_kernel, [arrived_b, arrived_a, near_b, near_a], [shape((rows, columns), low)]
    )
    rest = send(rest, INNER_TO_END)
    (left_a,) = step(left_kernel, [low_a, block_left], [block])
    state_shapes = [shape(momentum.shape, jnp.float32)] * 2 + [sums_shape]
    before = step(
        functools.partial(moments_kernel, True),
        [grad_a, momentum, second_moment],
        state_shapes,
    )
    scratch = pltpu.VMEM(block.shape, low)
    grad_b, end_product, own_product, square = step(
        last_kernel,
        [near_end_b, near_b, arrived_b, block_left, left_a, block_right],
        [half, shape((rows, columns), low), full, shape((1,), jnp.float32)],
        scratch=[scratch, scratch],
    )
    end_product = send(end_product, INNER_TO_END)
    new_mom, new_sec, sums = step(
        functools.partial(moments_kernel, False),
        [grad_b, momentum, second_moment, rest, near_a, near_b, square, *before],
        state_shapes,
    )
    (update,) = on_device(
        update_kernel,
        place,
        [end_product, own_product, sums, send(sums, PAIR), send(sums, ACROSS), send(sums, MIRROR)],
        [shape(momentum.shape, jnp.float32)],
    )
    return (update, new_mom, new_sec)


def solution(mesh):
    def per_device(activations, key_grads, momentum, *rest):
        fits = (
            mesh.shape["fsdp"] == 4
            and mesh.shape["tp"] == 4
            and mesh.shape["groups"] == 2
            and momentum.shape[1] * 2 == BR
            and momentum.shape[2] == 4 * TILE
            and activations.shape[1] == 2 * BR
        )
        return (line_of_four if fits else general)(activations, key_grads, momentum, *rest)

    return jax.shard_map(
        per_device,
        mesh=mesh,
        in_specs=(
            P(("groups", "fsdp"), "tp"),
            P(("groups", "fsdp"), "tp"),
            P("tp", "fsdp", None),
            P("tp", "fsdp", None),
            P("fsdp", "tp", None, None),
            P("fsdp", "tp", None, None),
            P(),
        ),
        out_specs=(
            P(("groups", "tp"), "fsdp", None),
            P(("groups", "tp"), "fsdp", None),
            P(("groups", "tp"), "fsdp", None),
        ),
        check_vma=False,
    )
```

```python
import functools

import jax
import jax.numpy as jnp
from jax import lax
from jax.experimental import pallas as pl
from jax.experimental.pallas import tpu as pltpu
from jax.sharding import PartitionSpec as P

BR = 896
STEP = 20


beta_one = 0.9
beta_two = 0.99
adam_eps = 1e-08
norm_eps = 1e-06


def moments_scaled(momentum, second_moment, gradient):
    new_mom = beta_one * momentum + (1.0 - beta_one) * gradient
    new_sec = beta_two * second_moment + (1.0 - beta_two) * gradient * gradient
    adam_dir = (
        new_mom
        * (1.0 / (1.0 - beta_one**STEP))
        / (jnp.sqrt(new_sec * (1.0 / (1.0 - beta_two**STEP))) + adam_eps)
    )
    return new_mom, new_sec, adam_dir


def spread(value, axis, source):
    kept = jnp.where(lax.axis_index(axis) == source, value, 0).astype(value.dtype)
    return lax.psum(kept, axis)


def contract_tokens(left_side, right_side):
    return lax.dot_general(
        left_side, right_side, (((0,), (0,)), ((), ())), preferred_element_type=jnp.float32
    )


def moments(momentum, second_moment, gradient):
    new_mom = beta_one * momentum + (1.0 - beta_one) * gradient
    new_sec = beta_two * second_moment + (1.0 - beta_two) * gradient * gradient
    adam_dir = (
        new_mom / (1.0 - beta_one**STEP) / (jnp.sqrt(new_sec / (1.0 - beta_two**STEP)) + adam_eps)
    )
    return new_mom, new_sec, jnp.sum(adam_dir * adam_dir)


def general(activations, key_grads, momentum, second_moment, left_roots, right_roots, owners):
    all_heads = lax.all_gather(key_grads, "tp", axis=1, tiled=True)
    panel_rows = activations.shape[1]
    shard_rows = momentum.shape[1]
    columns = all_heads.shape[1]
    blocks = panel_rows // BR
    fsdp_index = lax.axis_index("fsdp")
    tp_index = lax.axis_index("tp")
    first_row = fsdp_index * shard_rows
    my_block = first_row // BR
    offset = first_row - my_block * BR
    summed = lax.psum(contract_tokens(activations, all_heads), "fsdp")
    gradient = lax.dynamic_slice_in_dim(summed, first_row, shard_rows, 0)
    panel_low = summed.astype(jnp.bfloat16)
    new_mom, new_sec, adam_sq = moments(momentum[0], second_moment[0], gradient)
    own_adam = lax.psum(adam_sq, "fsdp")
    owner_row = owners[tp_index]
    owned_slots = owner_row == fsdp_index
    own_block = jnp.sum(jnp.where(owned_slots, jnp.arange(blocks), 0))

    def precondition():
        grad_block = lax.dynamic_slice_in_dim(panel_low, own_block * BR, BR, 0)
        left_product = jnp.dot(
            left_roots[0, 0], grad_block, preferred_element_type=jnp.float32
        ).astype(jnp.bfloat16)
        return jnp.dot(left_product, right_roots[0, 0], preferred_element_type=jnp.float32).astype(
            jnp.bfloat16
        )

    def not_owner():
        return jnp.zeros((BR, columns), jnp.bfloat16)

    result_block = lax.cond(jnp.any(owned_slots), precondition, not_owner)
    update = jnp.zeros((shard_rows, columns), jnp.float32)
    for block_index in range(blocks):
        arrived = spread(result_block, "fsdp", owner_row[block_index])
        widened = lax.optimization_barrier(arrived).astype(jnp.float32)
        pre_sq = jnp.sum(widened * widened)
        my_rows = lax.dynamic_slice_in_dim(widened, offset, shard_rows, 0)
        scaled = my_rows * jnp.sqrt(own_adam / (pre_sq + norm_eps))
        update = jnp.where(my_block == block_index, scaled, update)
    return (update[None], new_mom[None], new_sec[None])


def after(value, *others):
    return lax.optimization_barrier((value, *others))[0]


END_TO_INNER = [(0, 1), (3, 2)]
INNER_TO_END = [(1, 0), (2, 3)]
MIDDLE = [(1, 2), (2, 1)]
PAIR = [(0, 1), (1, 0), (2, 3), (3, 2)]
ACROSS = [(0, 2), (2, 0), (1, 3), (3, 1)]
MIRROR = [(0, 3), (3, 0), (1, 2), (2, 1)]
INNER_GROUPS = [(1, 5), (5, 1), (2, 6), (6, 2)]

TILE = 128
MIB = 1024 * 1024
MOMENT_TILE = 64
COSTS = (0, 0, 0, 0, 0, 0, 0, 20, 0, 0, 0, 0, 40)
SCALARS = pl.BlockSpec(memory_space=pltpu.SMEM)
VECTORS = pl.BlockSpec(memory_space=pltpu.VMEM)
IN_PLACE = pl.BlockSpec(memory_space=pl.ANY)
GROUP, SIDE, IS_END, CHUNK = 0, 1, 2, 3
ACROSS_OWN, PICK = 0, 1


def spec_of(array):
    if len(array.shape) == 1:
        return SCALARS
    return pl.BlockSpec(array.shape, lambda i: (0,) * len(array.shape))


def on_device(kernel, scalars, inputs, outputs, scratch=(), in_place=(), resident=False, flops=1):
    spec = lambda array: VECTORS if resident and len(array.shape) > 1 else spec_of(array)
    return pl.pallas_call(
        kernel,
        **({} if resident else {"grid": (1,)}),
        in_specs=[SCALARS]
        + [IN_PLACE if k in in_place else spec(array) for k, array in enumerate(inputs)],
        out_specs=[spec(shape) for shape in outputs],
        out_shape=list(outputs),
        scratch_shapes=list(scratch),
        cost_estimate=pl.CostEstimate(flops=flops, bytes_accessed=1, transcendentals=0),
        compiler_params=pltpu.CompilerParams(vmem_limit_bytes=(8 if resident else 32) * MIB),
    )(scalars, *inputs)


def packing(left_rows, right_rows):
    upper = lambda root, rows: [
        (root, i, j) for i in range(rows // TILE) for j in range(i, rows // TILE)
    ]
    lefts, rights = upper(0, left_rows), upper(1, right_rows)
    first, second = len(lefts) // 2, len(rights) // 2
    return [lefts[:first] + rights[:second], lefts[first:] + rights[second:]]


def spots(pieces):
    return [(piece, pl.ds(row, TILE)) for piece in pieces for row in range(0, piece.shape[0], TILE)]


def pack_kernel(lists, left_ref, right_ref, *refs):
    *pieces, copied = refs
    for group, places in enumerate(lists):

        @pl.when(lax.axis_index("groups") == group)
        def _():
            copies = [
                pltpu.make_async_copy(
                    (left_ref, right_ref)[root].at[
                        pl.ds(i * TILE, TILE), pl.ds(j * TILE, TILE)
                    ],
                    piece.at[rows, :],
                    copied.at[k],
                )
                for k, ((root, i, j), (piece, rows)) in enumerate(zip(places, spots(pieces)))
            ]
            for copy in copies:
                copy.start()
            for copy in copies:
                copy.wait()


def unpack_kernel(lists, place_ref, *refs):
    *pieces, left_ref, right_ref = refs
    count = len(pieces) // 2

    def fill(places, held):
        for (root, i, j), (piece, rows) in zip(places, spots(held)):
            target = (left_ref, right_ref)[root]
            tile = piece[rows, :]
            target[pl.ds(i * TILE, TILE), pl.ds(j * TILE, TILE)] = tile
            if i != j:
                target[pl.ds(j * TILE, TILE), pl.ds(i * TILE, TILE)] = tile.T

    for group in range(2):

        @pl.when((place_ref[GROUP] == group) & (place_ref[IS_END] == 0))
        def _():
            fill(lists[group], pieces[:count])
            fill(lists[1 - group], pieces[count:])


def choose_kernel(which, count, choice_ref, *refs):
    *sources, out_ref, copied = refs
    choices = len(sources) // count
    for k in range(choices):

        @pl.when(choice_ref[which] == k)
        def _():
            copies, row = [], 0
            for n, source in enumerate(sources[k::choices]):
                target = out_ref.at[pl.ds(row, source.shape[0]), :]
                copies.append(pltpu.make_async_copy(source, target, copied.at[n]))
                row += source.shape[0]
            for copy in copies:
                copy.start()
            for copy in copies:
                copy.wait()


def partial_kernel(place_ref, keys_ref, activations_ref, far_low_ref, near_ref, near_low_ref):
    def block_of(index):
        own = activations_ref[:, pl.ds(pl.multiple_of(index * BR, TILE), BR)]
        return contract_tokens(own, keys_ref[...])

    near = block_of(place_ref[SIDE])
    near_ref[...] = near

    @pl.when(place_ref[IS_END] == 1)
    def _():
        near_low_ref[...] = near.astype(jnp.bfloat16)
        far_low_ref[...] = block_of(1 - place_ref[SIDE]).astype(jnp.bfloat16)


def far_kernel(place_ref, from_end_ref, keys_ref, activations_ref, sum_ref):
    @pl.when(place_ref[IS_END] == 0)
    def _():
        columns = pl.ds(pl.multiple_of((1 - place_ref[SIDE]) * BR, TILE), BR)
        far = contract_tokens(activations_ref[:, columns], keys_ref[...])
        sum_ref[...] = (far + wide(from_end_ref)).astype(jnp.bfloat16)


def rows_of(place_ref, end, rows):
    index = place_ref[SIDE] if end else 1 - place_ref[SIDE]
    return pl.ds(pl.multiple_of(index * rows, 64), rows)


def wide(ref, which=slice(None)):
    return ref[which, :].astype(jnp.float32)


def rest_kernel(place_ref, arrived_ref, near_ref, rest_ref):
    @pl.when(place_ref[IS_END] == 0)
    def _():
        which = rows_of(place_ref, True, rest_ref.shape[0])
        rest_ref[...] = (near_ref[which, :] + wide(arrived_ref, which)).astype(jnp.bfloat16)


def near_gradient(place_ref, from_end_ref, near_ref, arrived_ref, grad_ref, low_ref):
    rows = grad_ref.shape[0]
    for end in (False, True):
        which = rows_of(place_ref, end, rows)
        grad = near_ref[which, :] + wide(from_end_ref, which) + wide(arrived_ref, which)
        low_ref[which, :] = grad.astype(jnp.bfloat16)
        if not end:
            grad_ref[...] = grad


def gradient_kernel(place_ref, from_end_ref, near_ref, arrived_ref, rest_ref, grad_ref, low_ref):
    rest_kernel(place_ref, arrived_ref, near_ref, rest_ref)

    @pl.when(place_ref[IS_END] == 0)
    def _():
        near_gradient(place_ref, from_end_ref, near_ref, arrived_ref, grad_ref, low_ref)


def left_product(low_ref, left_ref, product_ref):
    product_ref[...] = jnp.dot(
        left_ref[...], low_ref[...], preferred_element_type=jnp.float32
    ).astype(jnp.bfloat16)


def left_kernel(place_ref, low_ref, left_ref, product_ref):
    @pl.when(place_ref[IS_END] == 0)
    def _():
        left_product(low_ref, left_ref, product_ref)


def chunk_columns(place_ref, chunk, width):
    return pl.ds(pl.multiple_of(place_ref[CHUNK + chunk] * width, TILE), width)


def right_product(place_ref, end, rows, held_refs, right_ref):
    rows = rows_of(place_ref, end, rows)
    total = 0.0
    for c, ref in enumerate(held_refs):
        which = chunk_columns(place_ref, c, ref.shape[1])
        total = total + jnp.dot(
            ref[rows, :], right_ref[which, :], preferred_element_type=jnp.float32
        )
    return total


def end_kernel(
    place_ref, from_end_ref, near_ref, arrived_ref, left_ref, before_ref, right_ref,
    grad_ref, product_ref, end_ref, square_ref, low_ref,
):
    @pl.when(place_ref[IS_END] == 0)
    def _():
        near_gradient(place_ref, from_end_ref, near_ref, arrived_ref, grad_ref, low_ref)
        left_product(low_ref, left_ref, product_ref)
        held = (before_ref, product_ref)
        total = right_product(place_ref, True, end_ref.shape[0], held, right_ref)
        end_ref[...] = total.astype(jnp.bfloat16)
        square_ref[0] = jnp.sum(total * total)

    @pl.when(place_ref[IS_END] == 1)
    def _():
        square_ref[0] = 0.0


def over_rows(rows, tile, body, start=None):
    step = lambda i, carried: body(pl.multiple_of(i * tile, tile), carried)
    return lax.fori_loop(0, rows // tile, step, start)


def folded(values):
    squares = values * values
    return jnp.sum(squares.reshape(-1, 8, squares.shape[1]), axis=0)


def finish_kernel(
    place_ref, product_ref, before_ref, right_ref, grad_b_ref, grad_a_ref, rest_a_ref, rest_b_ref,
    near_a_ref, near_b_ref, mom_ref, sec_ref, square_ref, own_ref, new_mom_ref, new_sec_ref, sums_ref,
):
    rows, width = grad_a_ref.shape

    def state(grad_of):
        def body(row, squares):
            which = pl.ds(row, MOMENT_TILE)
            for c in range(2):
                columns = chunk_columns(place_ref, c, width)
                new_mom, new_sec, adam_dir = moments_scaled(
                    mom_ref[0, which, columns], sec_ref[0, which, columns], grad_of(c, row)
                )
                new_mom_ref[0, which, columns] = new_mom
                new_sec_ref[0, which, columns] = new_sec
                squares = squares + folded(adam_dir)
            return squares

        squares = over_rows(rows, MOMENT_TILE, body, jnp.zeros((8, width), jnp.float32))
        sums_ref[0] = jnp.sum(squares)

    @pl.when(place_ref[IS_END] == 0)
    def _():
        total = right_product(place_ref, False, rows, (before_ref, product_ref), right_ref)
        own_ref[...] = total
        sums_ref[1] = square_ref[0] + jnp.sum(folded(total))
        state(lambda c, row: (grad_a_ref, grad_b_ref)[c][pl.ds(row, MOMENT_TILE), :])

    @pl.when(place_ref[IS_END] == 1)
    def _():
        sums_ref[1] = 0.0
        base = pl.multiple_of(place_ref[SIDE] * rows, 64)
        nears, rests = (near_a_ref, near_b_ref), (rest_a_ref, rest_b_ref)
        state(
            lambda c, row: nears[c][pl.ds(pl.multiple_of(base + row, 16), MOMENT_TILE), :]
            + wide(rests[c], pl.ds(row, MOMENT_TILE))
        )


def update_kernel(
    place_ref, end_ref, own_ref, sums_ref, pair_ref, across_ref, mirror_ref, update_ref, held_ref, copied
):
    adam_sq = sums_ref[0] + pair_ref[0] + across_ref[0] + mirror_ref[0]
    pre_sq = sums_ref[1] + pair_ref[1]
    ones = jnp.ones((1, TILE), jnp.float32)
    scale = jnp.sqrt((adam_sq * ones) / (pre_sq * ones + norm_eps))[:, :1]
    tiles = copied.shape[0]
    rows = held_ref.shape[0] // tiles

    def write(value_of):
        copies = []
        for k in range(tiles):
            which = pl.ds(k * rows, rows)
            held_ref[which, :] = value_of(which) * scale
            copies.append(
                pltpu.make_async_copy(
                    held_ref.at[which, :], update_ref.at[0, which, :], copied.at[k]
                )
            )
            copies[-1].start()
        for copy in copies:
            copy.wait()

    @pl.when(place_ref[IS_END] == 0)
    def _():
        write(lambda which: own_ref[which, :])

    @pl.when(place_ref[IS_END] == 1)
    def _():
        write(lambda which: wide(end_ref, which))


def line_of_four(activations, key_grads, momentum, second_moment, left_roots, right_roots, owners):
    low = jnp.bfloat16
    group = lax.axis_index("groups")
    z = lax.axis_index("fsdp")
    tp_index = lax.axis_index("tp")
    side = z // 2
    is_end = (z == 0) | (z == 3)
    rows, columns = momentum.shape[1:]
    width = columns // 2
    stacked = lambda *values: jnp.stack(values).astype(jnp.int32)
    place = stacked(group, side, is_end.astype(jnp.int32), tp_index // 2, 1 - tp_index // 2)
    owner_row = owners[tp_index]
    near_owner = owner_row[side]
    far_owner = owner_row[1 - side]
    choice = stacked(
        jnp.where(far_owner == z, 0, 1),
        jnp.where(near_owner == z, 0, jnp.where(near_owner == jnp.where(side == 0, 0, 3), 1, 2)),
    )
    send = lambda value, perm: lax.ppermute(value, "fsdp", perm)
    shape = jax.ShapeDtypeStruct
    history = []

    def step(kernel, inputs, outputs, scalars=place, **kwargs):
        if history:
            inputs = [after(inputs[0], history[-1]), *inputs[1:]]
        flops = 1 + 115_000_000 * COSTS[len(history) - 1]
        out = on_device(kernel, scalars, inputs, outputs, flops=flops, **kwargs)
        history.append(out[0])
        return out

    left = left_roots[0, 0]
    right = right_roots[0, 0]
    lists = packing(left.shape[0], right.shape[0])
    count = len(lists[0])
    piece_shapes = [
        shape((tiles * TILE, TILE), low) for tiles in ((count + 1) // 2, count // 2)
    ]
    pieces = pl.pallas_call(
        functools.partial(pack_kernel, lists),
        in_specs=[IN_PLACE] * 2,
        out_specs=[pl.BlockSpec(memory_space=pltpu.VMEM)] * 2,
        out_shape=piece_shapes,
        scratch_shapes=[pltpu.SemaphoreType.DMA((count,))],
        compiler_params=pltpu.CompilerParams(vmem_limit_bytes=56 * MIB),
    )(left, right)
    history.append(pieces[0])
    root_end = [send(piece, END_TO_INNER) for piece in pieces]

    first_key = after(key_grads, history[-1])
    far_key = lax.ppermute(first_key, "tp", [(i, i ^ 2) for i in range(4)])
    core_key = lax.ppermute(first_key, "tp", [(i, i ^ 1) for i in range(4)])
    far_core_key = lax.ppermute(far_key, "tp", [(i, i ^ 1) for i in range(4)])
    odd = tp_index % 2 == 1
    joined = lambda one, two: jnp.where(
        odd, jnp.concatenate([two, one], 1), jnp.concatenate([one, two], 1)
    )
    keys_a, keys_b = joined(key_grads, core_key), joined(far_key, far_core_key)
    half = shape((rows, width), jnp.float32)
    block = shape((2 * rows, width), low)

    def partials(keys):
        return step(
            partial_kernel, [keys, activations], [block, shape(block.shape, jnp.float32), block]
        )

    def choose(which, *sources):
        rows = sum(options[0].shape[0] for options in sources)
        (out,) = step(
            functools.partial(choose_kernel, which, len(sources)),
            [array for options in sources for array in options],
            [shape((rows, TILE), low)],
            scalars=choice,
            scratch=[pltpu.SemaphoreType.DMA((len(sources),))],
            in_place=range(len(sources) * len(sources[0])),
        )
        return out

    def far_sum(from_end, keys):
        (out,) = step(far_kernel, [from_end, keys, activations], [block])
        return out

    def cross(k):
        return send(choose(ACROSS_OWN, [pieces[k], root_end[k]]), MIDDLE)

    other_group = lambda value: lax.ppermute(value, ("groups", "fsdp"), INNER_GROUPS)
    far_low_a, near_a, near_low_a = partials(keys_a)
    far_end_a = send(far_low_a, END_TO_INNER)
    far_low_b, near_b, near_low_b = partials(keys_b)
    across = [cross(0)]
    far_end_b = send(after(far_low_b, root_end[1]), END_TO_INNER)
    across.append(cross(1))
    far_sum_a = far_sum(far_end_a, keys_a)
    near_end_a = send(after(near_low_a, far_end_a), END_TO_INNER)
    arrived_a = send(far_sum_a, MIDDLE)
    picked = choose(PICK, *zip(pieces, root_end, across))
    other = other_group(picked)
    far_sum_b = far_sum(far_end_b, keys_b)
    near_end_b = send(after(near_low_b, far_end_b), END_TO_INNER)
    arrived_b = send(far_sum_b, MIDDLE)
    full = shape((rows, columns), jnp.float32)
    rest_shape = shape((rows, width), low)
    one = shape((1,), jnp.float32)
    rest_a, grad_a, low_a = step(
        gradient_kernel,
        [near_end_a, near_a, arrived_a],
        [rest_shape, half, block],
        resident=True,
    )
    rest_a = send(rest_a, INNER_TO_END)
    block_left, block_right = step(
        functools.partial(unpack_kernel, lists),
        [picked, other],
        [shape(left.shape, low), shape(right.shape, low)],
        resident=True,
    )
    (rest_b,) = step(
        rest_kernel, [arrived_b, near_b], [rest_shape], resident=True
    )
    rest_b = send(rest_b, INNER_TO_END)
    (left_a,) = step(
        left_kernel, [low_a, block_left], [block], resident=True
    )

    grad_b, product_b, end_product, end_square = step(
        end_kernel,
        [near_end_b, near_b, arrived_b, block_left, left_a, block_right],
        [half, block, shape((rows, columns), low), one],
        scratch=[pltpu.VMEM(block.shape, low)],
        resident=True,
    )
    end_product = send(end_product, INNER_TO_END)
    own_product, new_mom, new_sec, sums = step(
        finish_kernel,
        [
            product_b, left_a, block_right, grad_b, grad_a, rest_a, rest_b, near_a, near_b,
            momentum, second_moment, end_square,
        ],
        [full, *[shape(momentum.shape, jnp.float32)] * 2, shape((2,), jnp.float32)],
        resident=True,
    )
    received = [send(sums, PAIR), send(sums, ACROSS), send(sums, MIRROR)]
    update = pl.pallas_call(
        update_kernel,
        in_specs=[SCALARS, VECTORS, VECTORS] + [SCALARS] * 4,
        out_specs=IN_PLACE,
        out_shape=shape(momentum.shape, jnp.float32),
        scratch_shapes=[pltpu.VMEM((rows, columns), jnp.float32), pltpu.SemaphoreType.DMA((4,))],
        compiler_params=pltpu.CompilerParams(vmem_limit_bytes=8 * MIB),
    )(place, end_product, own_product, sums, *received)
    return (update, new_mom, new_sec)


def solution(mesh):
    def per_device(activations, key_grads, momentum, *rest):
        fits = (
            mesh.shape["fsdp"] == 4
            and mesh.shape["tp"] == 4
            and mesh.shape["groups"] == 2
            and momentum.shape[1] * 2 == BR
            and momentum.shape[2] == 4 * TILE
            and activations.shape[1] == 2 * BR
        )
        return (line_of_four if fits else general)(activations, key_grads, momentum, *rest)

    return jax.shard_map(
        per_device,
        mesh=mesh,
        in_specs=(
            P(("groups", "fsdp"), "tp"),
            P(("groups", "fsdp"), "tp"),
            P("tp", "fsdp", None),
            P("tp", "fsdp", None),
            P("fsdp", "tp", None, None),
            P("fsdp", "tp", None, None),
            P(),
        ),
        out_specs=(
            P(("groups", "tp"), "fsdp", None),
            P(("groups", "tp"), "fsdp", None),
            P(("groups", "tp"), "fsdp", None),
        ),
        check_vma=False,
    )
```

```python
import functools

import jax
import jax.numpy as jnp
from jax import lax
from jax.experimental import pallas as pl
from jax.experimental.pallas import tpu as pltpu
from jax.sharding import PartitionSpec as P

BR = 896
STEP = 20


beta_one = 0.9
beta_two = 0.99
adam_eps = 1e-08
norm_eps = 1e-06


def moments_scaled(momentum, second_moment, gradient):
    new_mom = beta_one * momentum + (1.0 - beta_one) * gradient
    new_sec = beta_two * second_moment + (1.0 - beta_two) * gradient * gradient
    adam_dir = (
        new_mom
        * (1.0 / (1.0 - beta_one**STEP))
        / (jnp.sqrt(new_sec * (1.0 / (1.0 - beta_two**STEP))) + adam_eps)
    )
    return new_mom, new_sec, adam_dir


def spread(value, axis, source):
    kept = jnp.where(lax.axis_index(axis) == source, value, 0).astype(value.dtype)
    return lax.psum(kept, axis)


def contract_tokens(left_side, right_side):
    return lax.dot_general(
        left_side, right_side, (((0,), (0,)), ((), ())), preferred_element_type=jnp.float32
    )


def moments(momentum, second_moment, gradient):
    new_mom = beta_one * momentum + (1.0 - beta_one) * gradient
    new_sec = beta_two * second_moment + (1.0 - beta_two) * gradient * gradient
    adam_dir = (
        new_mom / (1.0 - beta_one**STEP) / (jnp.sqrt(new_sec / (1.0 - beta_two**STEP)) + adam_eps)
    )
    return new_mom, new_sec, jnp.sum(adam_dir * adam_dir)


def general(activations, key_grads, momentum, second_moment, left_roots, right_roots, owners):
    all_heads = lax.all_gather(key_grads, "tp", axis=1, tiled=True)
    panel_rows = activations.shape[1]
    shard_rows = momentum.shape[1]
    columns = all_heads.shape[1]
    blocks = panel_rows // BR
    fsdp_index = lax.axis_index("fsdp")
    tp_index = lax.axis_index("tp")
    first_row = fsdp_index * shard_rows
    my_block = first_row // BR
    offset = first_row - my_block * BR
    summed = lax.psum(contract_tokens(activations, all_heads), "fsdp")
    gradient = lax.dynamic_slice_in_dim(summed, first_row, shard_rows, 0)
    panel_low = summed.astype(jnp.bfloat16)
    new_mom, new_sec, adam_sq = moments(momentum[0], second_moment[0], gradient)
    own_adam = lax.psum(adam_sq, "fsdp")
    owner_row = owners[tp_index]
    owned_slots = owner_row == fsdp_index
    own_block = jnp.sum(jnp.where(owned_slots, jnp.arange(blocks), 0))

    def precondition():
        grad_block = lax.dynamic_slice_in_dim(panel_low, own_block * BR, BR, 0)
        left_product = jnp.dot(
            left_roots[0, 0], grad_block, preferred_element_type=jnp.float32
        ).astype(jnp.bfloat16)
        return jnp.dot(left_product, right_roots[0, 0], preferred_element_type=jnp.float32).astype(
            jnp.bfloat16
        )

    def not_owner():
        return jnp.zeros((BR, columns), jnp.bfloat16)

    result_block = lax.cond(jnp.any(owned_slots), precondition, not_owner)
    update = jnp.zeros((shard_rows, columns), jnp.float32)
    for block_index in range(blocks):
        arrived = spread(result_block, "fsdp", owner_row[block_index])
        widened = lax.optimization_barrier(arrived).astype(jnp.float32)
        pre_sq = jnp.sum(widened * widened)
        my_rows = lax.dynamic_slice_in_dim(widened, offset, shard_rows, 0)
        scaled = my_rows * jnp.sqrt(own_adam / (pre_sq + norm_eps))
        update = jnp.where(my_block == block_index, scaled, update)
    return (update[None], new_mom[None], new_sec[None])


def after(value, *others):
    return lax.optimization_barrier((value, *others))[0]


END_TO_INNER = [(0, 1), (3, 2)]
INNER_TO_END = [(1, 0), (2, 3)]
MIDDLE = [(1, 2), (2, 1)]
PAIR = [(0, 1), (1, 0), (2, 3), (3, 2)]
ACROSS = [(0, 2), (2, 0), (1, 3), (3, 1)]
MIRROR = [(0, 3), (3, 0), (1, 2), (2, 1)]
INNER_GROUPS = [(1, 5), (5, 1), (2, 6), (6, 2)]

TILE = 128
MIB = 1024 * 1024
MOMENT_TILE = 64
COSTS = (0, 0, 0, 0, 0, 0, 0, 20, 0, 0, 0, 0, 40, 0)
SCALARS = pl.BlockSpec(memory_space=pltpu.SMEM)
VECTORS = pl.BlockSpec(memory_space=pltpu.VMEM)
IN_PLACE = pl.BlockSpec(memory_space=pl.ANY)
GROUP, SIDE, IS_END, CHUNK = 0, 1, 2, 3
ACROSS_OWN, PICK = 0, 1


def spec_of(array):
    if len(array.shape) == 1:
        return SCALARS
    return pl.BlockSpec(array.shape, lambda i: (0,) * len(array.shape))


def on_device(kernel, scalars, inputs, outputs, scratch=(), in_place=(), resident=False, flops=1):
    spec = lambda array: VECTORS if resident and len(array.shape) > 1 else spec_of(array)
    return pl.pallas_call(
        kernel,
        **({} if resident else {"grid": (1,)}),
        in_specs=[SCALARS]
        + [IN_PLACE if k in in_place else spec(array) for k, array in enumerate(inputs)],
        out_specs=[spec(shape) for shape in outputs],
        out_shape=list(outputs),
        scratch_shapes=list(scratch),
        cost_estimate=pl.CostEstimate(flops=flops, bytes_accessed=1, transcendentals=0),
        compiler_params=pltpu.CompilerParams(vmem_limit_bytes=(8 if resident else 32) * MIB),
    )(scalars, *inputs)


def packing(left_rows, right_rows):
    upper = lambda root, rows: [
        (root, i, j) for i in range(rows // TILE) for j in range(i, rows // TILE)
    ]
    lefts, rights = upper(0, left_rows), upper(1, right_rows)
    first, second = len(lefts) // 2, len(rights) // 2
    return [lefts[:first] + rights[:second], lefts[first:] + rights[second:]]


def spots(pieces):
    return [(piece, pl.ds(row, TILE)) for piece in pieces for row in range(0, piece.shape[0], TILE)]


def pack_kernel(lists, left_ref, right_ref, *refs):
    *pieces, copied = refs
    for group, places in enumerate(lists):

        @pl.when(lax.axis_index("groups") == group)
        def _():
            copies = [
                pltpu.make_async_copy(
                    (left_ref, right_ref)[root].at[
                        pl.ds(i * TILE, TILE), pl.ds(j * TILE, TILE)
                    ],
                    piece.at[rows, :],
                    copied.at[k],
                )
                for k, ((root, i, j), (piece, rows)) in enumerate(zip(places, spots(pieces)))
            ]
            for copy in copies:
                copy.start()
            for copy in copies:
                copy.wait()


def unpack_kernel(lists, place_ref, *refs):
    *pieces, left_ref, right_ref = refs
    count = len(pieces) // 2

    def fill(places, held):
        for (root, i, j), (piece, rows) in zip(places, spots(held)):
            target = (left_ref, right_ref)[root]
            tile = piece[rows, :]
            target[pl.ds(i * TILE, TILE), pl.ds(j * TILE, TILE)] = tile
            if i != j:
                target[pl.ds(j * TILE, TILE), pl.ds(i * TILE, TILE)] = tile.T

    for group in range(2):

        @pl.when((place_ref[GROUP] == group) & (place_ref[IS_END] == 0))
        def _():
            fill(lists[group], pieces[:count])
            fill(lists[1 - group], pieces[count:])


def choose_kernel(which, count, choice_ref, *refs):
    *sources, out_ref, copied = refs
    choices = len(sources) // count
    for k in range(choices):

        @pl.when(choice_ref[which] == k)
        def _():
            copies, row = [], 0
            for n, source in enumerate(sources[k::choices]):
                target = out_ref.at[pl.ds(row, source.shape[0]), :]
                copies.append(pltpu.make_async_copy(source, target, copied.at[n]))
                row += source.shape[0]
            for copy in copies:
                copy.start()
            for copy in copies:
                copy.wait()


def partial_kernel(place_ref, keys_ref, activations_ref, far_low_ref, near_ref, near_low_ref):
    def block_of(index):
        own = activations_ref[:, pl.ds(pl.multiple_of(index * BR, TILE), BR)]
        return contract_tokens(own, keys_ref[...])

    near = block_of(place_ref[SIDE])
    near_ref[...] = near

    @pl.when(place_ref[IS_END] == 1)
    def _():
        near_low_ref[...] = near.astype(jnp.bfloat16)
        far_low_ref[...] = block_of(1 - place_ref[SIDE]).astype(jnp.bfloat16)


def far_kernel(place_ref, from_end_ref, keys_ref, activations_ref, sum_ref):
    @pl.when(place_ref[IS_END] == 0)
    def _():
        columns = pl.ds(pl.multiple_of((1 - place_ref[SIDE]) * BR, TILE), BR)
        far = contract_tokens(activations_ref[:, columns], keys_ref[...])
        sum_ref[...] = (far + wide(from_end_ref)).astype(jnp.bfloat16)


def rows_of(place_ref, end, rows):
    index = place_ref[SIDE] if end else 1 - place_ref[SIDE]
    return pl.ds(pl.multiple_of(index * rows, 64), rows)


def wide(ref, which=slice(None)):
    return ref[which, :].astype(jnp.float32)


def rest_kernel(place_ref, arrived_ref, near_ref, rest_ref):
    @pl.when(place_ref[IS_END] == 0)
    def _():
        which = rows_of(place_ref, True, rest_ref.shape[0])
        rest_ref[...] = (near_ref[which, :] + wide(arrived_ref, which)).astype(jnp.bfloat16)


def near_gradient(place_ref, from_end_ref, near_ref, arrived_ref, grad_ref, low_ref):
    rows = grad_ref.shape[0]
    for end in (False, True):
        which = rows_of(place_ref, end, rows)
        grad = near_ref[which, :] + wide(from_end_ref, which) + wide(arrived_ref, which)
        low_ref[which, :] = grad.astype(jnp.bfloat16)
        if not end:
            grad_ref[...] = grad


def gradient_kernel(place_ref, from_end_ref, near_ref, arrived_ref, rest_ref, grad_ref, low_ref):
    rest_kernel(place_ref, arrived_ref, near_ref, rest_ref)

    @pl.when(place_ref[IS_END] == 0)
    def _():
        near_gradient(place_ref, from_end_ref, near_ref, arrived_ref, grad_ref, low_ref)


def left_product(low_ref, left_ref, product_ref):
    product_ref[...] = jnp.dot(
        left_ref[...], low_ref[...], preferred_element_type=jnp.float32
    ).astype(jnp.bfloat16)


def left_kernel(place_ref, low_ref, left_ref, product_ref):
    @pl.when(place_ref[IS_END] == 0)
    def _():
        left_product(low_ref, left_ref, product_ref)


def chunk_columns(place_ref, chunk, width):
    return pl.ds(pl.multiple_of(place_ref[CHUNK + chunk] * width, TILE), width)


def right_product(place_ref, end, rows, held_refs, right_ref):
    rows = rows_of(place_ref, end, rows)
    total = 0.0
    for c, ref in enumerate(held_refs):
        which = chunk_columns(place_ref, c, ref.shape[1])
        total = total + jnp.dot(
            ref[rows, :], right_ref[which, :], preferred_element_type=jnp.float32
        )
    return total


def end_kernel(
    place_ref, from_end_ref, near_ref, arrived_ref, left_ref, before_ref, right_ref,
    grad_ref, product_ref, end_ref, low_ref,
):
    @pl.when(place_ref[IS_END] == 0)
    def _():
        near_gradient(place_ref, from_end_ref, near_ref, arrived_ref, grad_ref, low_ref)
        left_product(low_ref, left_ref, product_ref)
        total = right_product(place_ref, True, end_ref.shape[0], (before_ref, product_ref), right_ref)
        end_ref[...] = total.astype(jnp.bfloat16)


def over_rows(rows, tile, body, start=None):
    step = lambda i, carried: body(pl.multiple_of(i * tile, tile), carried)
    return lax.fori_loop(0, rows // tile, step, start)


def folded(values):
    squares = values * values
    return jnp.sum(squares.reshape(-1, 8, squares.shape[1]), axis=0)


def gradient_of(place_ref, grads, nears, rests):
    inner = lambda c, row: grads[c][pl.ds(row, MOMENT_TILE), :]

    def end(c, row):
        first = pl.multiple_of(place_ref[SIDE] * rests[c].shape[0] + row, 16)
        return nears[c][pl.ds(first, MOMENT_TILE), :] + wide(rests[c], pl.ds(row, MOMENT_TILE))

    return inner, end


def spread_row(sums_ref, row, value):
    sums_ref[pl.ds(row, 1), :] = value * jnp.ones((1, sums_ref.shape[1]), jnp.float32)


def norms_kernel(
    place_ref, product_ref, before_ref, right_ref, end_ref, grad_a_ref, grad_b_ref, near_a_ref, near_b_ref,
    rest_a_ref, rest_b_ref, mom_ref, sec_ref, own_ref, sums_ref,
):
    rows, width = grad_a_ref.shape

    def adam(grad_of):
        def body(row, squares):
            which = pl.ds(row, MOMENT_TILE)
            for c in range(2):
                columns = chunk_columns(place_ref, c, width)
                _, _, adam_dir = moments_scaled(
                    mom_ref[0, which, columns], sec_ref[0, which, columns], grad_of(c, row)
                )
                squares = squares + folded(adam_dir)
            return squares

        squares = over_rows(rows, MOMENT_TILE, body, jnp.zeros((8, width), jnp.float32))
        spread_row(sums_ref, 0, jnp.sum(squares))

    inner, end = gradient_of(
        place_ref, (grad_a_ref, grad_b_ref), (near_a_ref, near_b_ref), (rest_a_ref, rest_b_ref)
    )

    @pl.when(place_ref[IS_END] == 0)
    def _():
        total = right_product(place_ref, False, rows, (before_ref, product_ref), right_ref)
        own_ref[...] = total
        spread_row(sums_ref, 1, jnp.sum(folded(total) + folded(wide(end_ref))))
        adam(inner)

    @pl.when(place_ref[IS_END] == 1)
    def _():
        spread_row(sums_ref, 1, 0.0)
        adam(end)


def state_kernel(
    place_ref, grad_a_ref, grad_b_ref, near_a_ref, near_b_ref, rest_a_ref, rest_b_ref, mom_ref, sec_ref,
    new_mom_ref, new_sec_ref,
):
    rows, width = grad_a_ref.shape

    def state(grad_of):
        def body(row, _):
            which = pl.ds(row, MOMENT_TILE)
            for c in range(2):
                columns = chunk_columns(place_ref, c, width)
                new_mom, new_sec, _ = moments_scaled(
                    mom_ref[0, which, columns], sec_ref[0, which, columns], grad_of(c, row)
                )
                new_mom_ref[0, which, columns] = new_mom
                new_sec_ref[0, which, columns] = new_sec

        over_rows(rows, MOMENT_TILE, body)

    inner, end = gradient_of(
        place_ref, (grad_a_ref, grad_b_ref), (near_a_ref, near_b_ref), (rest_a_ref, rest_b_ref)
    )

    @pl.when(place_ref[IS_END] == 0)
    def _():
        state(inner)

    @pl.when(place_ref[IS_END] == 1)
    def _():
        state(end)


def update_kernel(
    place_ref, end_ref, own_ref, sums_ref, pair_ref, across_ref, mirror_ref, update_ref, held_ref, copied
):
    adam_sq = sums_ref[0:1, :] + pair_ref[0:1, :] + across_ref[0:1, :] + mirror_ref[0:1, :]
    pre_sq = sums_ref[1:2, :] + pair_ref[1:2, :]
    scale = jnp.sqrt(adam_sq / (pre_sq + norm_eps))
    scale = jnp.concatenate([scale] * (held_ref.shape[1] // TILE), 1)
    tiles = copied.shape[0]
    rows = held_ref.shape[0] // tiles

    def write(value_of):
        copies = []
        for k in range(tiles):
            which = pl.ds(k * rows, rows)
            held_ref[which, :] = value_of(which) * scale
            copies.append(
                pltpu.make_async_copy(
                    held_ref.at[which, :], update_ref.at[0, which, :], copied.at[k]
                )
            )
            copies[-1].start()
        for copy in copies:
            copy.wait()

    @pl.when(place_ref[IS_END] == 0)
    def _():
        write(lambda which: own_ref[which, :])

    @pl.when(place_ref[IS_END] == 1)
    def _():
        write(lambda which: wide(end_ref, which))


def line_of_four(activations, key_grads, momentum, second_moment, left_roots, right_roots, owners):
    low = jnp.bfloat16
    group = lax.axis_index("groups")
    z = lax.axis_index("fsdp")
    tp_index = lax.axis_index("tp")
    side = z // 2
    is_end = (z == 0) | (z == 3)
    rows, columns = momentum.shape[1:]
    width = columns // 2
    stacked = lambda *values: jnp.stack(values).astype(jnp.int32)
    place = stacked(group, side, is_end.astype(jnp.int32), tp_index // 2, 1 - tp_index // 2)
    owner_row = owners[tp_index]
    near_owner = owner_row[side]
    far_owner = owner_row[1 - side]
    choice = stacked(
        jnp.where(far_owner == z, 0, 1),
        jnp.where(near_owner == z, 0, jnp.where(near_owner == jnp.where(side == 0, 0, 3), 1, 2)),
    )
    send = lambda value, perm: lax.ppermute(value, "fsdp", perm)
    shape = jax.ShapeDtypeStruct
    history = []

    def step(kernel, inputs, outputs, scalars=place, **kwargs):
        if history:
            inputs = [after(inputs[0], history[-1]), *inputs[1:]]
        flops = 1 + 115_000_000 * COSTS[len(history) - 1]
        out = on_device(kernel, scalars, inputs, outputs, flops=flops, **kwargs)
        history.append(out[0])
        return out

    left = left_roots[0, 0]
    right = right_roots[0, 0]
    lists = packing(left.shape[0], right.shape[0])
    count = len(lists[0])
    piece_shapes = [
        shape((tiles * TILE, TILE), low) for tiles in ((count + 1) // 2, count // 2)
    ]
    pieces = pl.pallas_call(
        functools.partial(pack_kernel, lists),
        in_specs=[IN_PLACE] * 2,
        out_specs=[pl.BlockSpec(memory_space=pltpu.VMEM)] * 2,
        out_shape=piece_shapes,
        scratch_shapes=[pltpu.SemaphoreType.DMA((count,))],
        compiler_params=pltpu.CompilerParams(vmem_limit_bytes=56 * MIB),
    )(left, right)
    history.append(pieces[0])
    root_end = [send(piece, END_TO_INNER) for piece in pieces]

    first_key = after(key_grads, history[-1])
    far_key = lax.ppermute(first_key, "tp", [(i, i ^ 2) for i in range(4)])
    core_key = lax.ppermute(first_key, "tp", [(i, i ^ 1) for i in range(4)])
    far_core_key = lax.ppermute(far_key, "tp", [(i, i ^ 1) for i in range(4)])
    odd = tp_index % 2 == 1
    joined = lambda one, two: jnp.where(
        odd, jnp.concatenate([two, one], 1), jnp.concatenate([one, two], 1)
    )
    keys_a, keys_b = joined(key_grads, core_key), joined(far_key, far_core_key)
    half = shape((rows, width), jnp.float32)
    block = shape((2 * rows, width), low)

    def partials(keys):
        return step(
            partial_kernel, [keys, activations], [block, shape(block.shape, jnp.float32), block]
        )

    def choose(which, *sources):
        rows = sum(options[0].shape[0] for options in sources)
        (out,) = step(
            functools.partial(choose_kernel, which, len(sources)),
            [array for options in sources for array in options],
            [shape((rows, TILE), low)],
            scalars=choice,
            scratch=[pltpu.SemaphoreType.DMA((len(sources),))],
            in_place=range(len(sources) * len(sources[0])),
        )
        return out

    def far_sum(from_end, keys):
        (out,) = step(far_kernel, [from_end, keys, activations], [block])
        return out

    def cross(k):
        return send(choose(ACROSS_OWN, [pieces[k], root_end[k]]), MIDDLE)

    other_group = lambda value: lax.ppermute(value, ("groups", "fsdp"), INNER_GROUPS)
    far_low_a, near_a, near_low_a = partials(keys_a)
    far_end_a = send(after(far_low_a, root_end[0]), END_TO_INNER)
    far_low_b, near_b, near_low_b = partials(keys_b)
    across = [cross(0)]
    far_end_b = send(after(far_low_b, root_end[1]), END_TO_INNER)
    across.append(cross(1))
    far_sum_a = far_sum(far_end_a, keys_a)
    near_end_a = send(after(near_low_a, far_end_a), END_TO_INNER)
    arrived_a = send(far_sum_a, MIDDLE)
    picked = choose(PICK, *zip(pieces, root_end, across))
    other = other_group(picked)
    far_sum_b = far_sum(far_end_b, keys_b)
    near_end_b = send(after(near_low_b, far_end_b), END_TO_INNER)
    arrived_b = send(far_sum_b, MIDDLE)
    full = shape((rows, columns), jnp.float32)
    rest_shape = shape((rows, width), low)
    rest_a, grad_a, low_a = step(
        gradient_kernel,
        [near_end_a, near_a, arrived_a],
        [rest_shape, half, block],
        resident=True,
    )
    rest_a = send(rest_a, INNER_TO_END)
    block_left, block_right = step(
        functools.partial(unpack_kernel, lists),
        [picked, other],
        [shape(left.shape, low), shape(right.shape, low)],
        resident=True,
    )
    (rest_b,) = step(
        rest_kernel, [arrived_b, near_b], [rest_shape], resident=True
    )
    rest_b = send(rest_b, INNER_TO_END)
    (left_a,) = step(
        left_kernel, [low_a, block_left], [block], resident=True
    )

    grad_b, product_b, end_product = step(
        end_kernel,
        [near_end_b, near_b, arrived_b, block_left, left_a, block_right],
        [half, block, shape((rows, columns), low)],
        scratch=[pltpu.VMEM(block.shape, low)],
        resident=True,
    )
    end_received = send(end_product, INNER_TO_END)
    gradients = [grad_a, grad_b, near_a, near_b, rest_a, rest_b, momentum, second_moment]
    own_product, sums = step(
        norms_kernel,
        [product_b, left_a, block_right, end_product, *gradients],
        [full, shape((8, TILE), jnp.float32)],
        resident=True,
    )
    received = [send(sums, perm) for perm in (PAIR, ACROSS, MIRROR)]
    new_mom, new_sec = step(
        state_kernel, gradients, [shape(momentum.shape, jnp.float32)] * 2, resident=True
    )
    update = pl.pallas_call(
        update_kernel,
        in_specs=[SCALARS] + [VECTORS] * 6,
        out_specs=IN_PLACE,
        out_shape=shape(momentum.shape, jnp.float32),
        scratch_shapes=[pltpu.VMEM((rows, columns), jnp.float32), pltpu.SemaphoreType.DMA((4,))],
        compiler_params=pltpu.CompilerParams(vmem_limit_bytes=8 * MIB),
    )(place, end_received, after(own_product, history[-1]), sums, *received)
    return (update, new_mom, new_sec)


def solution(mesh):
    def per_device(activations, key_grads, momentum, *rest):
        fits = (
            mesh.shape["fsdp"] == 4
            and mesh.shape["tp"] == 4
            and mesh.shape["groups"] == 2
            and momentum.shape[1] * 2 == BR
            and momentum.shape[2] == 4 * TILE
            and activations.shape[1] == 2 * BR
        )
        return (line_of_four if fits else general)(activations, key_grads, momentum, *rest)

    return jax.shard_map(
        per_device,
        mesh=mesh,
        in_specs=(
            P(("groups", "fsdp"), "tp"),
            P(("groups", "fsdp"), "tp"),
            P("tp", "fsdp", None),
            P("tp", "fsdp", None),
            P("fsdp", "tp", None, None),
            P("fsdp", "tp", None, None),
            P(),
        ),
        out_specs=(
            P(("groups", "tp"), "fsdp", None),
            P(("groups", "tp"), "fsdp", None),
            P(("groups", "tp"), "fsdp", None),
        ),
        check_vma=False,
    )
```

```python
import functools

import jax
import jax.numpy as jnp
from jax import lax
from jax.experimental import pallas as pl
from jax.experimental.pallas import tpu as pltpu
from jax.sharding import PartitionSpec as P

BR = 896
STEP = 20


beta_one = 0.9
beta_two = 0.99
adam_eps = 1e-08
norm_eps = 1e-06


def moments_scaled(momentum, second_moment, gradient):
    new_mom = beta_one * momentum + (1.0 - beta_one) * gradient
    new_sec = beta_two * second_moment + (1.0 - beta_two) * gradient * gradient
    adam_dir = (
        new_mom
        * (1.0 / (1.0 - beta_one**STEP))
        / (jnp.sqrt(new_sec * (1.0 / (1.0 - beta_two**STEP))) + adam_eps)
    )
    return new_mom, new_sec, adam_dir


def spread(value, axis, source):
    kept = jnp.where(lax.axis_index(axis) == source, value, 0).astype(value.dtype)
    return lax.psum(kept, axis)


def contract_tokens(left_side, right_side):
    return lax.dot_general(
        left_side, right_side, (((0,), (0,)), ((), ())), preferred_element_type=jnp.float32
    )


def moments(momentum, second_moment, gradient):
    new_mom = beta_one * momentum + (1.0 - beta_one) * gradient
    new_sec = beta_two * second_moment + (1.0 - beta_two) * gradient * gradient
    adam_dir = (
        new_mom / (1.0 - beta_one**STEP) / (jnp.sqrt(new_sec / (1.0 - beta_two**STEP)) + adam_eps)
    )
    return new_mom, new_sec, jnp.sum(adam_dir * adam_dir)


def general(activations, key_grads, momentum, second_moment, left_roots, right_roots, owners):
    all_heads = lax.all_gather(key_grads, "tp", axis=1, tiled=True)
    panel_rows = activations.shape[1]
    shard_rows = momentum.shape[1]
    columns = all_heads.shape[1]
    blocks = panel_rows // BR
    fsdp_index = lax.axis_index("fsdp")
    tp_index = lax.axis_index("tp")
    first_row = fsdp_index * shard_rows
    my_block = first_row // BR
    offset = first_row - my_block * BR
    summed = lax.psum(contract_tokens(activations, all_heads), "fsdp")
    gradient = lax.dynamic_slice_in_dim(summed, first_row, shard_rows, 0)
    panel_low = summed.astype(jnp.bfloat16)
    new_mom, new_sec, adam_sq = moments(momentum[0], second_moment[0], gradient)
    own_adam = lax.psum(adam_sq, "fsdp")
    owner_row = owners[tp_index]
    owned_slots = owner_row == fsdp_index
    own_block = jnp.sum(jnp.where(owned_slots, jnp.arange(blocks), 0))

    def precondition():
        grad_block = lax.dynamic_slice_in_dim(panel_low, own_block * BR, BR, 0)
        left_product = jnp.dot(
            left_roots[0, 0], grad_block, preferred_element_type=jnp.float32
        ).astype(jnp.bfloat16)
        return jnp.dot(left_product, right_roots[0, 0], preferred_element_type=jnp.float32).astype(
            jnp.bfloat16
        )

    def not_owner():
        return jnp.zeros((BR, columns), jnp.bfloat16)

    result_block = lax.cond(jnp.any(owned_slots), precondition, not_owner)
    update = jnp.zeros((shard_rows, columns), jnp.float32)
    for block_index in range(blocks):
        arrived = spread(result_block, "fsdp", owner_row[block_index])
        widened = lax.optimization_barrier(arrived).astype(jnp.float32)
        pre_sq = jnp.sum(widened * widened)
        my_rows = lax.dynamic_slice_in_dim(widened, offset, shard_rows, 0)
        scaled = my_rows * jnp.sqrt(own_adam / (pre_sq + norm_eps))
        update = jnp.where(my_block == block_index, scaled, update)
    return (update[None], new_mom[None], new_sec[None])


def after(value, *others):
    return lax.optimization_barrier((value, *others))[0]


END_TO_INNER = [(0, 1), (3, 2)]
INNER_TO_END = [(1, 0), (2, 3)]
MIDDLE = [(1, 2), (2, 1)]
PAIR = [(0, 1), (1, 0), (2, 3), (3, 2)]
ACROSS = [(0, 2), (2, 0), (1, 3), (3, 1)]
MIRROR = [(0, 3), (3, 0), (1, 2), (2, 1)]
INNER_GROUPS = [(1, 5), (5, 1), (2, 6), (6, 2)]

TILE = 128
MIB = 1024 * 1024
MOMENT_TILE = 64
CUT = 10
COSTS = (0, 0, 0, 0, 0, 0, 0, 20, 0, 0, 0, 0, 40, 0)
SCALARS = pl.BlockSpec(memory_space=pltpu.SMEM)
VECTORS = pl.BlockSpec(memory_space=pltpu.VMEM)
IN_PLACE = pl.BlockSpec(memory_space=pl.ANY)
GROUP, SIDE, IS_END, CHUNK = 0, 1, 2, 3
ACROSS_OWN, PICK = 0, 1


def spec_of(array):
    if len(array.shape) == 1:
        return SCALARS
    return pl.BlockSpec(array.shape, lambda i: (0,) * len(array.shape))


def on_device(kernel, scalars, inputs, outputs, scratch=(), in_place=(), resident=False, flops=1):
    spec = lambda array: VECTORS if resident and len(array.shape) > 1 else spec_of(array)
    return pl.pallas_call(
        kernel,
        **({} if resident else {"grid": (1,)}),
        in_specs=[SCALARS]
        + [IN_PLACE if k in in_place else spec(array) for k, array in enumerate(inputs)],
        out_specs=[spec(shape) for shape in outputs],
        out_shape=list(outputs),
        scratch_shapes=list(scratch),
        cost_estimate=pl.CostEstimate(flops=flops, bytes_accessed=1, transcendentals=0),
        compiler_params=pltpu.CompilerParams(vmem_limit_bytes=(8 if resident else 32) * MIB),
    )(scalars, *inputs)


def packing(left_tiles, right_tiles):
    sizes = (left_tiles, right_tiles)
    apart = [(r, i, j) for r in range(2) for i in range(sizes[r]) for j in range(i + 1, sizes[r])]
    middle = [(r, i) for r in range(2) for i in range(sizes[r])]
    shared = [tuple(middle[k : k + 2]) for k in range(0, len(middle), 2)]
    most = (len(shared) + 1) // 2
    first = (len(apart) + len(shared) + 1) // 2 - most
    return [apart[:first] + shared[:most], apart[first:] + shared[most:]]


def is_shared(entry):
    return isinstance(entry[0], tuple)


def halves_of(shape):
    row = lax.broadcasted_iota(jnp.int32, shape, 0)
    column = lax.broadcasted_iota(jnp.int32, shape, 1)
    return column > row, column == row


def pack_kernel(lists, first, left_ref, right_ref, piece_ref, *scratch):
    roots = (left_ref, right_ref)
    held_ref, copied = scratch if len(scratch) == 2 else (None, scratch[0])
    count = piece_ref.shape[0] // TILE

    def copy_of(root, i, j, target, semaphore):
        source = roots[root].at[pl.ds(i * TILE, TILE), pl.ds(j * TILE, TILE)]
        return pltpu.make_async_copy(source, target, semaphore)

    for group, entries in enumerate(lists):

        @pl.when(lax.axis_index("groups") == group)
        def _():
            copies, shared = [], []
            for k, entry in enumerate(entries[first : first + count]):
                spot = pl.ds(k * TILE, TILE)
                if not is_shared(entry):
                    copies.append(copy_of(*entry, piece_ref.at[spot, :], copied.at[len(copies)]))
                    continue
                shared.append((spot, len(entry)))
                for n, (root, i) in enumerate(entry):
                    target = held_ref.at[2 * len(shared) - 2 + n]
                    copies.append(copy_of(root, i, i, target, copied.at[len(copies)]))
            for copy in copies:
                copy.start()
            for copy in copies:
                copy.wait()
            if held_ref is None:
                return
            upper, diagonal = halves_of((TILE, TILE))
            apart = jnp.zeros((16, TILE), jnp.float32)
            line = lax.broadcasted_iota(jnp.int32, apart.shape, 0)
            for k, (spot, members) in enumerate(shared):
                one = wide(held_ref.at[2 * k])
                if members == 2:
                    two = wide(held_ref.at[2 * k + 1])
                    middle = jnp.sum(jnp.where(diagonal, two, 0.0), axis=0, keepdims=True)
                    apart = jnp.where(line == k, middle, apart)
                    one = jnp.where(upper | diagonal, one, two)
                piece_ref[spot, :] = one.astype(jnp.bfloat16)
            piece_ref[pl.ds(count * TILE, 16), :] = apart.astype(jnp.bfloat16)


def unpack_kernel(lists, count, place_ref, own_ref, other_ref, left_ref, right_ref):
    targets = (left_ref, right_ref)

    def fill(entries, held_ref):
        apart = wide(held_ref, pl.ds(count * TILE, 16))
        upper, diagonal = halves_of((TILE, TILE))
        shared = 0
        for k, entry in enumerate(entries):
            spot = pl.ds(k * TILE, TILE)
            if not is_shared(entry):
                root, i, j = entry
                tile = held_ref[spot, :]
                targets[root][pl.ds(i * TILE, TILE), pl.ds(j * TILE, TILE)] = tile
                targets[root][pl.ds(j * TILE, TILE), pl.ds(i * TILE, TILE)] = tile.T
                continue
            tile = wide(held_ref, spot)
            turned = tile.T
            middle = apart[shared : shared + 1, :]
            full = (
                jnp.where(upper | diagonal, tile, turned),
                jnp.where(upper, turned, jnp.where(diagonal, middle, tile)),
            )
            for (root, i), value in zip(entry, full):
                place = pl.ds(i * TILE, TILE)
                targets[root][place, place] = value.astype(jnp.bfloat16)
            shared += 1

    for group in range(2):

        @pl.when((place_ref[GROUP] == group) & (place_ref[IS_END] == 0))
        def _():
            fill(lists[group], own_ref)
            fill(lists[1 - group], other_ref)


def choose_kernel(which, count, choice_ref, *refs):
    *sources, out_ref, copied = refs
    choices = len(sources) // count
    for k in range(choices):

        @pl.when(choice_ref[which] == k)
        def _():
            copies, row = [], 0
            for n, source in enumerate(sources[k::choices]):
                target = out_ref.at[pl.ds(row, source.shape[0]), :]
                copies.append(pltpu.make_async_copy(source, target, copied.at[n]))
                row += source.shape[0]
            for copy in copies:
                copy.start()
            for copy in copies:
                copy.wait()


def partial_kernel(place_ref, keys_ref, activations_ref, far_low_ref, near_ref, near_low_ref):
    def block_of(index):
        own = activations_ref[:, pl.ds(pl.multiple_of(index * BR, TILE), BR)]
        return contract_tokens(own, keys_ref[...])

    near = block_of(place_ref[SIDE])
    near_ref[...] = near

    @pl.when(place_ref[IS_END] == 1)
    def _():
        near_low_ref[...] = near.astype(jnp.bfloat16)
        far_low_ref[...] = block_of(1 - place_ref[SIDE]).astype(jnp.bfloat16)


def far_kernel(place_ref, from_end_ref, keys_ref, activations_ref, sum_ref):
    @pl.when(place_ref[IS_END] == 0)
    def _():
        columns = pl.ds(pl.multiple_of((1 - place_ref[SIDE]) * BR, TILE), BR)
        far = contract_tokens(activations_ref[:, columns], keys_ref[...])
        sum_ref[...] = (far + wide(from_end_ref)).astype(jnp.bfloat16)


def rows_of(place_ref, end, rows):
    index = place_ref[SIDE] if end else 1 - place_ref[SIDE]
    return pl.ds(pl.multiple_of(index * rows, 64), rows)


def wide(ref, which=slice(None)):
    return ref[which, :].astype(jnp.float32)


def rest_kernel(place_ref, arrived_ref, near_ref, rest_ref):
    @pl.when(place_ref[IS_END] == 0)
    def _():
        which = rows_of(place_ref, True, rest_ref.shape[0])
        rest_ref[...] = (near_ref[which, :] + wide(arrived_ref, which)).astype(jnp.bfloat16)


def near_gradient(place_ref, from_end_ref, near_ref, arrived_ref, grad_ref, low_ref):
    rows = grad_ref.shape[0]
    for end in (False, True):
        which = rows_of(place_ref, end, rows)
        grad = near_ref[which, :] + wide(from_end_ref, which) + wide(arrived_ref, which)
        low_ref[which, :] = grad.astype(jnp.bfloat16)
        if not end:
            grad_ref[...] = grad


def gradient_kernel(place_ref, from_end_ref, near_ref, arrived_ref, rest_ref, grad_ref, low_ref):
    rest_kernel(place_ref, arrived_ref, near_ref, rest_ref)

    @pl.when(place_ref[IS_END] == 0)
    def _():
        near_gradient(place_ref, from_end_ref, near_ref, arrived_ref, grad_ref, low_ref)


def left_product(low_ref, left_ref, product_ref):
    product_ref[...] = jnp.dot(
        left_ref[...], low_ref[...], preferred_element_type=jnp.float32
    ).astype(jnp.bfloat16)


def left_kernel(place_ref, low_ref, left_ref, product_ref):
    @pl.when(place_ref[IS_END] == 0)
    def _():
        left_product(low_ref, left_ref, product_ref)


def chunk_columns(place_ref, chunk, width):
    return pl.ds(pl.multiple_of(place_ref[CHUNK + chunk] * width, TILE), width)


def right_product(place_ref, end, rows, held_refs, right_ref):
    rows = rows_of(place_ref, end, rows)
    total = 0.0
    for c, ref in enumerate(held_refs):
        which = chunk_columns(place_ref, c, ref.shape[1])
        total = total + jnp.dot(
            ref[rows, :], right_ref[which, :], preferred_element_type=jnp.float32
        )
    return total


def end_kernel(
    place_ref, from_end_ref, near_ref, arrived_ref, left_ref, before_ref, right_ref,
    grad_ref, product_ref, end_ref, low_ref,
):
    @pl.when(place_ref[IS_END] == 0)
    def _():
        near_gradient(place_ref, from_end_ref, near_ref, arrived_ref, grad_ref, low_ref)
        left_product(low_ref, left_ref, product_ref)
        total = right_product(place_ref, True, end_ref.shape[0], (before_ref, product_ref), right_ref)
        end_ref[...] = total.astype(jnp.bfloat16)


def over_rows(rows, tile, body, start=None):
    step = lambda i, carried: body(pl.multiple_of(i * tile, tile), carried)
    return lax.fori_loop(0, rows // tile, step, start)


def folded(values):
    squares = values * values
    return jnp.sum(squares.reshape(-1, 8, squares.shape[1]), axis=0)


def gradient_of(place_ref, grads, nears, rests):
    inner = lambda c, row: grads[c][pl.ds(row, MOMENT_TILE), :]

    def end(c, row):
        first = pl.multiple_of(place_ref[SIDE] * rests[c].shape[0] + row, 16)
        return nears[c][pl.ds(first, MOMENT_TILE), :] + wide(rests[c], pl.ds(row, MOMENT_TILE))

    return inner, end


def spread_row(sums_ref, row, value):
    sums_ref[pl.ds(row, 1), :] = value * jnp.ones((1, sums_ref.shape[1]), jnp.float32)


def norms_kernel(
    place_ref, product_ref, before_ref, right_ref, end_ref, grad_a_ref, grad_b_ref, near_a_ref, near_b_ref,
    rest_a_ref, rest_b_ref, mom_ref, sec_ref, own_ref, sums_ref,
):
    rows, width = grad_a_ref.shape

    def adam(grad_of):
        def body(row, squares):
            which = pl.ds(row, MOMENT_TILE)
            for c in range(2):
                columns = chunk_columns(place_ref, c, width)
                _, _, adam_dir = moments_scaled(
                    mom_ref[0, which, columns], sec_ref[0, which, columns], grad_of(c, row)
                )
                squares = squares + folded(adam_dir)
            return squares

        squares = over_rows(rows, MOMENT_TILE, body, jnp.zeros((8, width), jnp.float32))
        spread_row(sums_ref, 0, jnp.sum(squares))

    inner, end = gradient_of(
        place_ref, (grad_a_ref, grad_b_ref), (near_a_ref, near_b_ref), (rest_a_ref, rest_b_ref)
    )

    @pl.when(place_ref[IS_END] == 0)
    def _():
        total = right_product(place_ref, False, rows, (before_ref, product_ref), right_ref)
        own_ref[...] = total
        spread_row(sums_ref, 1, jnp.sum(folded(total) + folded(wide(end_ref))))
        adam(inner)

    @pl.when(place_ref[IS_END] == 1)
    def _():
        spread_row(sums_ref, 1, 0.0)
        adam(end)


def state_kernel(
    place_ref, grad_a_ref, grad_b_ref, near_a_ref, near_b_ref, rest_a_ref, rest_b_ref, mom_ref, sec_ref,
    new_mom_ref, new_sec_ref,
):
    rows, width = grad_a_ref.shape

    def state(grad_of):
        def body(row, _):
            which = pl.ds(row, MOMENT_TILE)
            for c in range(2):
                columns = chunk_columns(place_ref, c, width)
                new_mom, new_sec, _ = moments_scaled(
                    mom_ref[0, which, columns], sec_ref[0, which, columns], grad_of(c, row)
                )
                new_mom_ref[0, which, columns] = new_mom
                new_sec_ref[0, which, columns] = new_sec

        over_rows(rows, MOMENT_TILE, body)

    inner, end = gradient_of(
        place_ref, (grad_a_ref, grad_b_ref), (near_a_ref, near_b_ref), (rest_a_ref, rest_b_ref)
    )

    @pl.when(place_ref[IS_END] == 0)
    def _():
        state(inner)

    @pl.when(place_ref[IS_END] == 1)
    def _():
        state(end)


def update_kernel(
    place_ref, end_ref, own_ref, sums_ref, pair_ref, across_ref, mirror_ref, update_ref, held_ref, copied
):
    adam_sq = sums_ref[0:1, :] + pair_ref[0:1, :] + across_ref[0:1, :] + mirror_ref[0:1, :]
    pre_sq = sums_ref[1:2, :] + pair_ref[1:2, :]
    scale = jnp.sqrt(adam_sq / (pre_sq + norm_eps))
    scale = jnp.concatenate([scale] * (held_ref.shape[1] // TILE), 1)
    tiles = copied.shape[0]
    rows = held_ref.shape[0] // tiles

    def write(value_of):
        copies = []
        for k in range(tiles):
            which = pl.ds(k * rows, rows)
            held_ref[which, :] = value_of(which) * scale
            copies.append(
                pltpu.make_async_copy(
                    held_ref.at[which, :], update_ref.at[0, which, :], copied.at[k]
                )
            )
            copies[-1].start()
        for copy in copies:
            copy.wait()

    @pl.when(place_ref[IS_END] == 0)
    def _():
        write(lambda which: own_ref[which, :])

    @pl.when(place_ref[IS_END] == 1)
    def _():
        write(lambda which: wide(end_ref, which))


def line_of_four(activations, key_grads, momentum, second_moment, left_roots, right_roots, owners):
    low = jnp.bfloat16
    group = lax.axis_index("groups")
    z = lax.axis_index("fsdp")
    tp_index = lax.axis_index("tp")
    side = z // 2
    is_end = (z == 0) | (z == 3)
    rows, columns = momentum.shape[1:]
    width = columns // 2
    stacked = lambda *values: jnp.stack(values).astype(jnp.int32)
    place = stacked(group, side, is_end.astype(jnp.int32), tp_index // 2, 1 - tp_index // 2)
    owner_row = owners[tp_index]
    near_owner = owner_row[side]
    far_owner = owner_row[1 - side]
    choice = stacked(
        jnp.where(far_owner == z, 0, 1),
        jnp.where(near_owner == z, 0, jnp.where(near_owner == jnp.where(side == 0, 0, 3), 1, 2)),
    )
    send = lambda value, perm: lax.ppermute(value, "fsdp", perm)
    shape = jax.ShapeDtypeStruct
    history = []

    def step(kernel, inputs, outputs, scalars=place, **kwargs):
        if history:
            inputs = [after(inputs[0], history[-1]), *inputs[1:]]
        flops = 1 + 115_000_000 * COSTS[len(history) - 1]
        out = on_device(kernel, scalars, inputs, outputs, flops=flops, **kwargs)
        history.append(out[0])
        return out

    left = left_roots[0, 0]
    right = right_roots[0, 0]
    lists = packing(left.shape[0] // TILE, right.shape[0] // TILE)
    count = max(len(entries) for entries in lists)
    pieces = []
    for first, tiles in ((0, CUT), (CUT, count - CUT)):
        held = [] if first == 0 else [pltpu.VMEM((2 * tiles, TILE, TILE), low)]
        pieces.append(
            pl.pallas_call(
                functools.partial(pack_kernel, lists, first),
                in_specs=[IN_PLACE] * 2,
                out_specs=VECTORS,
                out_shape=shape((tiles * TILE + 16 * len(held), TILE), low),
                scratch_shapes=[*held, pltpu.SemaphoreType.DMA((2 * tiles,))],
                cost_estimate=pl.CostEstimate(flops=1, bytes_accessed=1, transcendentals=0),
                compiler_params=pltpu.CompilerParams(vmem_limit_bytes=56 * MIB),
            )(after(left, pieces[0]) if pieces else left, right)
        )
    history.append(pieces[1])
    root_end = [send(piece, END_TO_INNER) for piece in pieces]

    first_key = after(key_grads, history[-1])
    far_key = lax.ppermute(first_key, "tp", [(i, i ^ 2) for i in range(4)])
    core_key = lax.ppermute(first_key, "tp", [(i, i ^ 1) for i in range(4)])
    far_core_key = lax.ppermute(far_key, "tp", [(i, i ^ 1) for i in range(4)])
    odd = tp_index % 2 == 1
    joined = lambda one, two: jnp.where(
        odd, jnp.concatenate([two, one], 1), jnp.concatenate([one, two], 1)
    )
    keys_a, keys_b = joined(key_grads, core_key), joined(far_key, far_core_key)
    half = shape((rows, width), jnp.float32)
    block = shape((2 * rows, width), low)

    def partials(keys):
        return step(
            partial_kernel, [keys, activations], [block, shape(block.shape, jnp.float32), block]
        )

    def choose(which, *sources):
        rows = sum(options[0].shape[0] for options in sources)
        (out,) = step(
            functools.partial(choose_kernel, which, len(sources)),
            [array for options in sources for array in options],
            [shape((rows, TILE), low)],
            scalars=choice,
            scratch=[pltpu.SemaphoreType.DMA((len(sources),))],
            in_place=range(len(sources) * len(sources[0])),
        )
        return out

    def far_sum(from_end, keys):
        (out,) = step(far_kernel, [from_end, keys, activations], [block])
        return out

    def cross(k):
        return send(choose(ACROSS_OWN, [pieces[k], root_end[k]]), MIDDLE)

    other_group = lambda value: lax.ppermute(value, ("groups", "fsdp"), INNER_GROUPS)
    far_low_a, near_a, near_low_a = partials(after(keys_a, choice, place))
    far_end_a = send(after(far_low_a, root_end[0]), END_TO_INNER)
    across = [cross(0)]
    far_low_b, near_b, near_low_b = partials(keys_b)
    far_end_b = send(after(far_low_b, root_end[1]), END_TO_INNER)
    across.append(cross(1))
    far_sum_a = far_sum(far_end_a, keys_a)
    near_end_a = send(after(near_low_a, far_end_a), END_TO_INNER)
    arrived_a = send(far_sum_a, MIDDLE)
    picked = choose(PICK, *zip(pieces, root_end, across))
    other = other_group(picked)
    far_sum_b = far_sum(far_end_b, keys_b)
    near_end_b = send(after(near_low_b, far_end_b), END_TO_INNER)
    arrived_b = send(far_sum_b, MIDDLE)
    full = shape((rows, columns), jnp.float32)
    rest_shape = shape((rows, width), low)
    rest_a, grad_a, low_a = step(
        gradient_kernel,
        [near_end_a, near_a, arrived_a],
        [rest_shape, half, block],
        resident=True,
    )
    rest_a = send(rest_a, INNER_TO_END)
    block_left, block_right = step(
        functools.partial(unpack_kernel, lists, count),
        [picked, other],
        [shape(left.shape, low), shape(right.shape, low)],
        resident=True,
    )
    (left_a,) = step(left_kernel, [low_a, block_left], [block], resident=True)
    (rest_b,) = step(rest_kernel, [arrived_b, near_b], [rest_shape], resident=True)
    rest_b = send(rest_b, INNER_TO_END)

    grad_b, product_b, end_product = step(
        end_kernel,
        [near_end_b, near_b, arrived_b, block_left, left_a, block_right],
        [half, block, shape((rows, columns), low)],
        scratch=[pltpu.VMEM(block.shape, low)],
        resident=True,
    )
    end_received = send(end_product, INNER_TO_END)
    gradients = [grad_a, grad_b, near_a, near_b, rest_a, rest_b, momentum, second_moment]
    own_product, sums = step(
        norms_kernel,
        [product_b, left_a, block_right, end_product, *gradients],
        [full, shape((8, TILE), jnp.float32)],
        resident=True,
    )
    received = [send(sums, perm) for perm in (PAIR, ACROSS, MIRROR)]
    new_mom, new_sec = step(
        state_kernel, gradients, [shape(momentum.shape, jnp.float32)] * 2, resident=True
    )
    update = pl.pallas_call(
        update_kernel,
        in_specs=[SCALARS] + [VECTORS] * 6,
        out_specs=IN_PLACE,
        out_shape=shape(momentum.shape, jnp.float32),
        scratch_shapes=[pltpu.VMEM((rows, columns), jnp.float32), pltpu.SemaphoreType.DMA((4,))],
        compiler_params=pltpu.CompilerParams(vmem_limit_bytes=8 * MIB),
    )(place, end_received, after(own_product, history[-1]), sums, *received)
    return (update, new_mom, new_sec)


def solution(mesh):
    def per_device(activations, key_grads, momentum, *rest):
        fits = (
            mesh.shape["fsdp"] == 4
            and mesh.shape["tp"] == 4
            and mesh.shape["groups"] == 2
            and momentum.shape[1] * 2 == BR
            and momentum.shape[2] == 4 * TILE
            and activations.shape[1] == 2 * BR
        )
        return (line_of_four if fits else general)(activations, key_grads, momentum, *rest)

    return jax.shard_map(
        per_device,
        mesh=mesh,
        in_specs=(
            P(("groups", "fsdp"), "tp"),
            P(("groups", "fsdp"), "tp"),
            P("tp", "fsdp", None),
            P("tp", "fsdp", None),
            P("fsdp", "tp", None, None),
            P("fsdp", "tp", None, None),
            P(),
        ),
        out_specs=(
            P(("groups", "tp"), "fsdp", None),
            P(("groups", "tp"), "fsdp", None),
            P(("groups", "tp"), "fsdp", None),
        ),
        check_vma=False,
    )
```

```python
import functools

import jax
import jax.numpy as jnp
from jax import lax
from jax.experimental import pallas as pl
from jax.experimental.pallas import tpu as pltpu
from jax.sharding import PartitionSpec as P

BR = 896
STEP = 20


beta_one = 0.9
beta_two = 0.99
adam_eps = 1e-08
norm_eps = 1e-06


def moments_scaled(momentum, second_moment, gradient):
    new_mom = beta_one * momentum + (1.0 - beta_one) * gradient
    new_sec = beta_two * second_moment + (1.0 - beta_two) * gradient * gradient
    adam_dir = (
        new_mom
        * (1.0 / (1.0 - beta_one**STEP))
        / (jnp.sqrt(new_sec * (1.0 / (1.0 - beta_two**STEP))) + adam_eps)
    )
    return new_mom, new_sec, adam_dir


def spread(value, axis, source):
    kept = jnp.where(lax.axis_index(axis) == source, value, 0).astype(value.dtype)
    return lax.psum(kept, axis)


def contract_tokens(left_side, right_side):
    return lax.dot_general(
        left_side, right_side, (((0,), (0,)), ((), ())), preferred_element_type=jnp.float32
    )


def moments(momentum, second_moment, gradient):
    new_mom = beta_one * momentum + (1.0 - beta_one) * gradient
    new_sec = beta_two * second_moment + (1.0 - beta_two) * gradient * gradient
    adam_dir = (
        new_mom / (1.0 - beta_one**STEP) / (jnp.sqrt(new_sec / (1.0 - beta_two**STEP)) + adam_eps)
    )
    return new_mom, new_sec, jnp.sum(adam_dir * adam_dir)


def general(activations, key_grads, momentum, second_moment, left_roots, right_roots, owners):
    all_heads = lax.all_gather(key_grads, "tp", axis=1, tiled=True)
    panel_rows = activations.shape[1]
    shard_rows = momentum.shape[1]
    columns = all_heads.shape[1]
    blocks = panel_rows // BR
    fsdp_index = lax.axis_index("fsdp")
    tp_index = lax.axis_index("tp")
    first_row = fsdp_index * shard_rows
    my_block = first_row // BR
    offset = first_row - my_block * BR
    summed = lax.psum(contract_tokens(activations, all_heads), "fsdp")
    gradient = lax.dynamic_slice_in_dim(summed, first_row, shard_rows, 0)
    panel_low = summed.astype(jnp.bfloat16)
    new_mom, new_sec, adam_sq = moments(momentum[0], second_moment[0], gradient)
    own_adam = lax.psum(adam_sq, "fsdp")
    owner_row = owners[tp_index]
    owned_slots = owner_row == fsdp_index
    own_block = jnp.sum(jnp.where(owned_slots, jnp.arange(blocks), 0))

    def precondition():
        grad_block = lax.dynamic_slice_in_dim(panel_low, own_block * BR, BR, 0)
        left_product = jnp.dot(
            left_roots[0, 0], grad_block, preferred_element_type=jnp.float32
        ).astype(jnp.bfloat16)
        return jnp.dot(left_product, right_roots[0, 0], preferred_element_type=jnp.float32).astype(
            jnp.bfloat16
        )

    def not_owner():
        return jnp.zeros((BR, columns), jnp.bfloat16)

    result_block = lax.cond(jnp.any(owned_slots), precondition, not_owner)
    update = jnp.zeros((shard_rows, columns), jnp.float32)
    for block_index in range(blocks):
        arrived = spread(result_block, "fsdp", owner_row[block_index])
        widened = lax.optimization_barrier(arrived).astype(jnp.float32)
        pre_sq = jnp.sum(widened * widened)
        my_rows = lax.dynamic_slice_in_dim(widened, offset, shard_rows, 0)
        scaled = my_rows * jnp.sqrt(own_adam / (pre_sq + norm_eps))
        update = jnp.where(my_block == block_index, scaled, update)
    return (update[None], new_mom[None], new_sec[None])


def after(value, *others):
    return lax.optimization_barrier((value, *others))[0]


END_TO_INNER = [(0, 1), (3, 2)]
INNER_TO_END = [(1, 0), (2, 3)]
MIDDLE = [(1, 2), (2, 1)]
PAIR = [(0, 1), (1, 0), (2, 3), (3, 2)]
ACROSS = [(0, 2), (2, 0), (1, 3), (3, 1)]
MIRROR = [(0, 3), (3, 0), (1, 2), (2, 1)]
INNER_GROUPS = [(1, 5), (5, 1), (2, 6), (6, 2)]

TILE = 128
MIB = 1024 * 1024
MOMENT_TILE = 64
CUT = 10
COSTS = (0, 0, 0, 0, 0, 20, 0, 20, 0, 0, 0, 0, 40, 0)
SCALARS = pl.BlockSpec(memory_space=pltpu.SMEM)
VECTORS = pl.BlockSpec(memory_space=pltpu.VMEM)
IN_PLACE = pl.BlockSpec(memory_space=pl.ANY)
GROUP, SIDE, IS_END, CHUNK = 0, 1, 2, 3
ACROSS_OWN, PICK = 0, 1


def spec_of(array):
    if len(array.shape) == 1:
        return SCALARS
    return pl.BlockSpec(array.shape, lambda i: (0,) * len(array.shape))


def on_device(kernel, scalars, inputs, outputs, scratch=(), in_place=(), resident=False, flops=1):
    spec = lambda array: VECTORS if resident and len(array.shape) > 1 else spec_of(array)
    return pl.pallas_call(
        kernel,
        **({} if resident else {"grid": (1,)}),
        in_specs=[SCALARS]
        + [IN_PLACE if k in in_place else spec(array) for k, array in enumerate(inputs)],
        out_specs=[spec(shape) for shape in outputs],
        out_shape=list(outputs),
        scratch_shapes=list(scratch),
        cost_estimate=pl.CostEstimate(flops=flops, bytes_accessed=1, transcendentals=0),
        compiler_params=pltpu.CompilerParams(vmem_limit_bytes=(8 if resident else 32) * MIB),
    )(scalars, *inputs)


def packing(left_tiles, right_tiles):
    sizes = (left_tiles, right_tiles)
    apart = [(r, i, j) for r in range(2) for i in range(sizes[r]) for j in range(i + 1, sizes[r])]
    middle = [(r, i) for r in range(2) for i in range(sizes[r])]
    shared = [tuple(middle[k : k + 2]) for k in range(0, len(middle), 2)]
    most = (len(shared) + 1) // 2
    first = (len(apart) + len(shared) + 1) // 2 - most
    return [apart[:first] + shared[:most], apart[first:] + shared[most:]]


def is_shared(entry):
    return isinstance(entry[0], tuple)


def halves_of(shape):
    row = lax.broadcasted_iota(jnp.int32, shape, 0)
    column = lax.broadcasted_iota(jnp.int32, shape, 1)
    return column > row, column == row


def pack_kernel(lists, first, left_ref, right_ref, piece_ref, *scratch):
    roots = (left_ref, right_ref)
    held_ref, copied = scratch if len(scratch) == 2 else (None, scratch[0])
    count = piece_ref.shape[0] // TILE

    def copy_of(root, i, j, target, semaphore):
        source = roots[root].at[pl.ds(i * TILE, TILE), pl.ds(j * TILE, TILE)]
        return pltpu.make_async_copy(source, target, semaphore)

    for group, entries in enumerate(lists):

        @pl.when(lax.axis_index("groups") == group)
        def _():
            copies, shared = [], []
            for k, entry in enumerate(entries[first : first + count]):
                spot = pl.ds(k * TILE, TILE)
                if not is_shared(entry):
                    copies.append(copy_of(*entry, piece_ref.at[spot, :], copied.at[len(copies)]))
                    continue
                shared.append((spot, len(entry)))
                for n, (root, i) in enumerate(entry):
                    target = held_ref.at[2 * len(shared) - 2 + n]
                    copies.append(copy_of(root, i, i, target, copied.at[len(copies)]))
            for copy in copies:
                copy.start()
            for copy in copies:
                copy.wait()
            if held_ref is None:
                return
            upper, diagonal = halves_of((TILE, TILE))
            apart = jnp.zeros((16, TILE), jnp.float32)
            line = lax.broadcasted_iota(jnp.int32, apart.shape, 0)
            for k, (spot, members) in enumerate(shared):
                one = wide(held_ref.at[2 * k])
                if members == 2:
                    two = wide(held_ref.at[2 * k + 1])
                    middle = jnp.sum(jnp.where(diagonal, two, 0.0), axis=0, keepdims=True)
                    apart = jnp.where(line == k, middle, apart)
                    one = jnp.where(upper | diagonal, one, two)
                piece_ref[spot, :] = one.astype(jnp.bfloat16)
            piece_ref[pl.ds(count * TILE, 16), :] = apart.astype(jnp.bfloat16)


def unpack_kernel(lists, count, place_ref, own_ref, other_ref, left_ref, right_ref):
    targets = (left_ref, right_ref)

    def fill(entries, held_ref):
        apart = wide(held_ref, pl.ds(count * TILE, 16))
        upper, diagonal = halves_of((TILE, TILE))
        shared = 0
        for k, entry in enumerate(entries):
            spot = pl.ds(k * TILE, TILE)
            if not is_shared(entry):
                root, i, j = entry
                tile = held_ref[spot, :]
                targets[root][pl.ds(i * TILE, TILE), pl.ds(j * TILE, TILE)] = tile
                targets[root][pl.ds(j * TILE, TILE), pl.ds(i * TILE, TILE)] = tile.T
                continue
            tile = wide(held_ref, spot)
            turned = tile.T
            middle = apart[shared : shared + 1, :]
            full = (
                jnp.where(upper | diagonal, tile, turned),
                jnp.where(upper, turned, jnp.where(diagonal, middle, tile)),
            )
            for (root, i), value in zip(entry, full):
                place = pl.ds(i * TILE, TILE)
                targets[root][place, place] = value.astype(jnp.bfloat16)
            shared += 1

    for group in range(2):

        @pl.when((place_ref[GROUP] == group) & (place_ref[IS_END] == 0))
        def _():
            fill(lists[group], own_ref)
            fill(lists[1 - group], other_ref)


def choose_kernel(which, count, choice_ref, *refs):
    *sources, out_ref, copied = refs
    choices = len(sources) // count
    for k in range(choices):

        @pl.when(choice_ref[which] == k)
        def _():
            copies, row = [], 0
            for n, source in enumerate(sources[k::choices]):
                target = out_ref.at[pl.ds(row, source.shape[0]), :]
                copies.append(pltpu.make_async_copy(source, target, copied.at[n]))
                row += source.shape[0]
            for copy in copies:
                copy.start()
            for copy in copies:
                copy.wait()


def partial_kernel(place_ref, keys_ref, activations_ref, far_low_ref, near_ref, near_low_ref):
    def block_of(index):
        own = activations_ref[:, pl.ds(pl.multiple_of(index * BR, TILE), BR)]
        return contract_tokens(own, keys_ref[...])

    near = block_of(place_ref[SIDE])
    near_ref[...] = near

    @pl.when(place_ref[IS_END] == 1)
    def _():
        near_low_ref[...] = near.astype(jnp.bfloat16)
        far_low_ref[...] = block_of(1 - place_ref[SIDE]).astype(jnp.bfloat16)


def far_kernel(place_ref, from_end_ref, keys_ref, activations_ref, sum_ref):
    @pl.when(place_ref[IS_END] == 0)
    def _():
        columns = pl.ds(pl.multiple_of((1 - place_ref[SIDE]) * BR, TILE), BR)
        far = contract_tokens(activations_ref[:, columns], keys_ref[...])
        sum_ref[...] = (far + wide(from_end_ref)).astype(jnp.bfloat16)


def rows_of(place_ref, end, rows):
    index = place_ref[SIDE] if end else 1 - place_ref[SIDE]
    return pl.ds(pl.multiple_of(index * rows, 64), rows)


def wide(ref, which=slice(None)):
    return ref[which, :].astype(jnp.float32)


def rest_kernel(place_ref, arrived_ref, near_ref, rest_ref, sum_ref):
    @pl.when(place_ref[IS_END] == 0)
    def _():
        sum_ref[...] = near_ref[...] + wide(arrived_ref)
        rest_ref[...] = sum_ref[rows_of(place_ref, True, rest_ref.shape[0]), :].astype(jnp.bfloat16)


def near_gradient(place_ref, from_end_ref, sum_ref, grad_ref, low_ref):
    rows = grad_ref.shape[0]
    for end in (False, True):
        which = rows_of(place_ref, end, rows)
        grad = sum_ref[which, :] + wide(from_end_ref, which)
        low_ref[which, :] = grad.astype(jnp.bfloat16)
        if not end:
            grad_ref[...] = grad


def gradient_kernel(place_ref, from_end_ref, near_ref, arrived_ref, rest_ref, grad_ref, low_ref, sum_ref):
    rest_kernel(place_ref, arrived_ref, near_ref, rest_ref, sum_ref)

    @pl.when(place_ref[IS_END] == 0)
    def _():
        near_gradient(place_ref, from_end_ref, sum_ref, grad_ref, low_ref)


def left_product(low_ref, left_ref, which):
    return jnp.dot(
        left_ref[which, :], low_ref[...], preferred_element_type=jnp.float32
    ).astype(jnp.bfloat16)


def right_product(place_ref, chunk, product, right_ref):
    which = chunk_columns(place_ref, chunk, product.shape[1])
    return jnp.dot(product, right_ref[which, :], preferred_element_type=jnp.float32)


def left_kernel(place_ref, low_ref, left_ref, right_ref, end_ref, own_ref):
    @pl.when(place_ref[IS_END] == 0)
    def _():
        rows = own_ref.shape[0]
        own_ref[...] = left_product(low_ref, left_ref, rows_of(place_ref, False, rows))
        product = left_product(low_ref, left_ref, rows_of(place_ref, True, rows))
        end_ref[...] = right_product(place_ref, 0, product, right_ref)


def chunk_columns(place_ref, chunk, width):
    return pl.ds(pl.multiple_of(place_ref[CHUNK + chunk] * width, TILE), width)


def end_kernel(
    place_ref, from_end_ref, sum_ref, left_ref, right_ref, before_ref, grad_ref, low_ref, end_ref
):
    @pl.when(place_ref[IS_END] == 0)
    def _():
        near_gradient(place_ref, from_end_ref, sum_ref, grad_ref, low_ref)
        product = left_product(low_ref, left_ref, rows_of(place_ref, True, end_ref.shape[0]))
        total = before_ref[...] + right_product(place_ref, 1, product, right_ref)
        end_ref[...] = total.astype(jnp.bfloat16)


def over_rows(rows, tile, body, start=None):
    step = lambda i, carried: body(pl.multiple_of(i * tile, tile), carried)
    return lax.fori_loop(0, rows // tile, step, start)


def folded(values):
    squares = values * values
    return jnp.sum(squares.reshape(-1, 8, squares.shape[1]), axis=0)


def gradient_of(place_ref, grads, nears, rests):
    inner = lambda c, row: grads[c][pl.ds(row, MOMENT_TILE), :]

    def end(c, row):
        first = pl.multiple_of(place_ref[SIDE] * rests[c].shape[0] + row, 16)
        return nears[c][pl.ds(first, MOMENT_TILE), :] + wide(rests[c], pl.ds(row, MOMENT_TILE))

    return inner, end


def spread_row(sums_ref, row, value):
    sums_ref[pl.ds(row, 1), :] = value * jnp.ones((1, sums_ref.shape[1]), jnp.float32)


def norms_kernel(
    place_ref, low_ref, left_ref, right_ref, before_ref, end_ref, grad_a_ref, grad_b_ref, near_a_ref, near_b_ref,
    rest_a_ref, rest_b_ref, mom_ref, sec_ref, own_ref, sums_ref,
):
    rows, width = grad_a_ref.shape

    def adam(grad_of):
        def body(row, squares):
            which = pl.ds(row, MOMENT_TILE)
            for c in range(2):
                columns = chunk_columns(place_ref, c, width)
                _, _, adam_dir = moments_scaled(
                    mom_ref[0, which, columns], sec_ref[0, which, columns], grad_of(c, row)
                )
                squares = squares + folded(adam_dir)
            return squares

        squares = over_rows(rows, MOMENT_TILE, body, jnp.zeros((8, width), jnp.float32))
        spread_row(sums_ref, 0, jnp.sum(squares))

    inner, end = gradient_of(
        place_ref, (grad_a_ref, grad_b_ref), (near_a_ref, near_b_ref), (rest_a_ref, rest_b_ref)
    )

    @pl.when(place_ref[IS_END] == 0)
    def _():
        product = left_product(low_ref, left_ref, rows_of(place_ref, False, rows))
        total = right_product(place_ref, 0, before_ref[...], right_ref)
        total = total + right_product(place_ref, 1, product, right_ref)
        own_ref[...] = total
        spread_row(sums_ref, 1, jnp.sum(folded(total) + folded(wide(end_ref))))
        adam(inner)

    @pl.when(place_ref[IS_END] == 1)
    def _():
        spread_row(sums_ref, 1, 0.0)
        adam(end)


def state_kernel(
    place_ref, grad_a_ref, grad_b_ref, near_a_ref, near_b_ref, rest_a_ref, rest_b_ref, mom_ref, sec_ref,
    new_mom_ref, new_sec_ref,
):
    rows, width = grad_a_ref.shape

    def state(grad_of):
        def body(row, _):
            which = pl.ds(row, MOMENT_TILE)
            for c in range(2):
                columns = chunk_columns(place_ref, c, width)
                new_mom, new_sec, _ = moments_scaled(
                    mom_ref[0, which, columns], sec_ref[0, which, columns], grad_of(c, row)
                )
                new_mom_ref[0, which, columns] = new_mom
                new_sec_ref[0, which, columns] = new_sec

        over_rows(rows, MOMENT_TILE, body)

    inner, end = gradient_of(
        place_ref, (grad_a_ref, grad_b_ref), (near_a_ref, near_b_ref), (rest_a_ref, rest_b_ref)
    )

    @pl.when(place_ref[IS_END] == 0)
    def _():
        state(inner)

    @pl.when(place_ref[IS_END] == 1)
    def _():
        state(end)


def update_kernel(
    place_ref, end_ref, own_ref, sums_ref, pair_ref, across_ref, mirror_ref, update_ref, held_ref, copied
):
    adam_sq = sums_ref[0:1, :] + pair_ref[0:1, :] + across_ref[0:1, :] + mirror_ref[0:1, :]
    pre_sq = sums_ref[1:2, :] + pair_ref[1:2, :]
    scale = jnp.sqrt(adam_sq / (pre_sq + norm_eps))
    scale = jnp.concatenate([scale] * (held_ref.shape[1] // TILE), 1)
    tiles = copied.shape[0]
    rows = held_ref.shape[0] // tiles

    def write(value_of):
        copies = []
        for k in range(tiles):
            which = pl.ds(k * rows, rows)
            held_ref[which, :] = value_of(which) * scale
            copies.append(
                pltpu.make_async_copy(
                    held_ref.at[which, :], update_ref.at[0, which, :], copied.at[k]
                )
            )
            copies[-1].start()
        for copy in copies:
            copy.wait()

    @pl.when(place_ref[IS_END] == 0)
    def _():
        write(lambda which: own_ref[which, :])

    @pl.when(place_ref[IS_END] == 1)
    def _():
        write(lambda which: wide(end_ref, which))


def line_of_four(activations, key_grads, momentum, second_moment, left_roots, right_roots, owners):
    low = jnp.bfloat16
    group = lax.axis_index("groups")
    z = lax.axis_index("fsdp")
    tp_index = lax.axis_index("tp")
    side = z // 2
    is_end = (z == 0) | (z == 3)
    rows, columns = momentum.shape[1:]
    width = columns // 2
    stacked = lambda *values: jnp.stack(values).astype(jnp.int32)
    place = stacked(group, side, is_end.astype(jnp.int32), tp_index // 2, 1 - tp_index // 2)
    owner_row = owners[tp_index]
    near_owner = owner_row[side]
    far_owner = owner_row[1 - side]
    choice = stacked(
        jnp.where(far_owner == z, 0, 1),
        jnp.where(near_owner == z, 0, jnp.where(near_owner == jnp.where(side == 0, 0, 3), 1, 2)),
    )
    send = lambda value, perm: lax.ppermute(value, "fsdp", perm)
    shape = jax.ShapeDtypeStruct
    history = []

    def step(kernel, inputs, outputs, scalars=place, **kwargs):
        if history:
            inputs = [after(inputs[0], history[-1]), *inputs[1:]]
        flops = 1 + 115_000_000 * COSTS[len(history) - 1]
        out = on_device(kernel, scalars, inputs, outputs, flops=flops, **kwargs)
        history.append(out[0])
        return out

    left = left_roots[0, 0]
    right = right_roots[0, 0]
    lists = packing(left.shape[0] // TILE, right.shape[0] // TILE)
    count = max(len(entries) for entries in lists)
    pieces = []
    for first, tiles in ((0, CUT), (CUT, count - CUT)):
        held = [] if first == 0 else [pltpu.VMEM((2 * tiles, TILE, TILE), low)]
        pieces.append(
            pl.pallas_call(
                functools.partial(pack_kernel, lists, first),
                in_specs=[IN_PLACE] * 2,
                out_specs=VECTORS,
                out_shape=shape((tiles * TILE + 16 * len(held), TILE), low),
                scratch_shapes=[*held, pltpu.SemaphoreType.DMA((2 * tiles,))],
                cost_estimate=pl.CostEstimate(flops=1, bytes_accessed=1, transcendentals=0),
                compiler_params=pltpu.CompilerParams(vmem_limit_bytes=56 * MIB),
            )(after(left, pieces[0]) if pieces else left, right)
        )
    history.append(pieces[1])
    root_end = [send(piece, END_TO_INNER) for piece in pieces]

    first_key = after(key_grads, history[-1])
    far_key = lax.ppermute(first_key, "tp", [(i, i ^ 2) for i in range(4)])
    core_key = lax.ppermute(first_key, "tp", [(i, i ^ 1) for i in range(4)])
    far_core_key = lax.ppermute(far_key, "tp", [(i, i ^ 1) for i in range(4)])
    odd = tp_index % 2 == 1
    joined = lambda one, two: jnp.where(
        odd, jnp.concatenate([two, one], 1), jnp.concatenate([one, two], 1)
    )
    keys_a, keys_b = joined(key_grads, core_key), joined(far_key, far_core_key)
    half = shape((rows, width), jnp.float32)
    block = shape((2 * rows, width), low)

    def partials(keys):
        return step(
            partial_kernel, [keys, activations], [block, shape(block.shape, jnp.float32), block]
        )

    def choose(which, *sources):
        rows = sum(options[0].shape[0] for options in sources)
        (out,) = step(
            functools.partial(choose_kernel, which, len(sources)),
            [array for options in sources for array in options],
            [shape((rows, TILE), low)],
            scalars=choice,
            scratch=[pltpu.SemaphoreType.DMA((len(sources),))],
            in_place=range(len(sources) * len(sources[0])),
        )
        return out

    def far_sum(from_end, keys):
        (out,) = step(far_kernel, [from_end, keys, activations], [block])
        return out

    def cross(k):
        return send(choose(ACROSS_OWN, [pieces[k], root_end[k]]), MIDDLE)

    other_group = lambda value: lax.ppermute(value, ("groups", "fsdp"), INNER_GROUPS)
    far_low_a, near_a, near_low_a = partials(after(keys_a, choice, place))
    far_end_a = send(after(far_low_a, root_end[0]), END_TO_INNER)
    across = [cross(0)]
    far_low_b, near_b, near_low_b = partials(keys_b)
    far_end_b = send(after(far_low_b, root_end[1]), END_TO_INNER)
    across.append(cross(1))
    near_end_a = send(after(near_low_a, history[-1]), END_TO_INNER)
    far_sum_a = far_sum(far_end_a, keys_a)
    arrived_a = send(far_sum_a, MIDDLE)
    picked = choose(PICK, *zip(pieces, root_end, across))
    other = other_group(picked)
    far_sum_b = far_sum(far_end_b, keys_b)
    near_end_b = send(after(near_low_b, far_end_b), END_TO_INNER)
    arrived_b = send(far_sum_b, MIDDLE)
    full = shape((rows, columns), jnp.float32)
    rest_shape = shape((rows, width), low)
    near_shape = shape(block.shape, jnp.float32)
    rest_a, grad_a, low_a = step(
        gradient_kernel,
        [near_end_a, near_a, arrived_a],
        [rest_shape, half, block],
        scratch=[pltpu.VMEM(near_shape.shape, jnp.float32)],
        resident=True,
    )
    rest_a = send(rest_a, INNER_TO_END)
    block_left, block_right = step(
        functools.partial(unpack_kernel, lists, count),
        [picked, other],
        [shape(left.shape, low), shape(right.shape, low)],
        resident=True,
    )
    rest_b, near_sum = step(
        rest_kernel, [arrived_b, near_b], [rest_shape, near_shape], resident=True
    )
    rest_b = send(rest_b, INNER_TO_END)
    end_before, own_before = step(
        left_kernel, [low_a, block_left, block_right], [full, rest_shape], resident=True
    )
    grad_b, low_b, end_product = step(
        end_kernel,
        [near_end_b, near_sum, block_left, block_right, end_before],
        [half, block, shape((rows, columns), low)],
        resident=True,
    )
    end_received = send(end_product, INNER_TO_END)
    gradients = [grad_a, grad_b, near_a, near_b, rest_a, rest_b, momentum, second_moment]
    own_product, sums = step(
        norms_kernel,
        [low_b, block_left, block_right, own_before, end_product, *gradients],
        [full, shape((8, TILE), jnp.float32)],
        resident=True,
    )
    received = [send(sums, perm) for perm in (PAIR, ACROSS, MIRROR)]
    new_mom, new_sec = step(
        state_kernel, gradients, [shape(momentum.shape, jnp.float32)] * 2, resident=True
    )
    update = pl.pallas_call(
        update_kernel,
        in_specs=[SCALARS] + [VECTORS] * 6,
        out_specs=IN_PLACE,
        out_shape=shape(momentum.shape, jnp.float32),
        scratch_shapes=[pltpu.VMEM((rows, columns), jnp.float32), pltpu.SemaphoreType.DMA((4,))],
        compiler_params=pltpu.CompilerParams(vmem_limit_bytes=8 * MIB),
    )(place, end_received, after(own_product, history[-1]), sums, *received)
    return (update, new_mom, new_sec)


def solution(mesh):
    def per_device(activations, key_grads, momentum, *rest):
        fits = (
            mesh.shape["fsdp"] == 4
            and mesh.shape["tp"] == 4
            and mesh.shape["groups"] == 2
            and momentum.shape[1] * 2 == BR
            and momentum.shape[2] == 4 * TILE
            and activations.shape[1] == 2 * BR
        )
        return (line_of_four if fits else general)(activations, key_grads, momentum, *rest)

    return jax.shard_map(
        per_device,
        mesh=mesh,
        in_specs=(
            P(("groups", "fsdp"), "tp"),
            P(("groups", "fsdp"), "tp"),
            P("tp", "fsdp", None),
            P("tp", "fsdp", None),
            P("fsdp", "tp", None, None),
            P("fsdp", "tp", None, None),
            P(),
        ),
        out_specs=(
            P(("groups", "tp"), "fsdp", None),
            P(("groups", "tp"), "fsdp", None),
            P(("groups", "tp"), "fsdp", None),
        ),
        check_vma=False,
    )
```

```python
import functools

import jax
import jax.numpy as jnp
from jax import lax
from jax.experimental import pallas as pl
from jax.experimental.pallas import tpu as pltpu
from jax.sharding import PartitionSpec as P

BR = 896
STEP = 20


beta_one = 0.9
beta_two = 0.99
adam_eps = 1e-08
norm_eps = 1e-06


def moments_scaled(momentum, second_moment, gradient):
    new_mom = beta_one * momentum + (1.0 - beta_one) * gradient
    new_sec = beta_two * second_moment + (1.0 - beta_two) * gradient * gradient
    adam_dir = (
        new_mom
        * (1.0 / (1.0 - beta_one**STEP))
        / (jnp.sqrt(new_sec * (1.0 / (1.0 - beta_two**STEP))) + adam_eps)
    )
    return new_mom, new_sec, adam_dir


def spread(value, axis, source):
    kept = jnp.where(lax.axis_index(axis) == source, value, 0).astype(value.dtype)
    return lax.psum(kept, axis)


def contract_tokens(left_side, right_side):
    return lax.dot_general(
        left_side, right_side, (((0,), (0,)), ((), ())), preferred_element_type=jnp.float32
    )


def moments(momentum, second_moment, gradient):
    new_mom = beta_one * momentum + (1.0 - beta_one) * gradient
    new_sec = beta_two * second_moment + (1.0 - beta_two) * gradient * gradient
    adam_dir = (
        new_mom / (1.0 - beta_one**STEP) / (jnp.sqrt(new_sec / (1.0 - beta_two**STEP)) + adam_eps)
    )
    return new_mom, new_sec, jnp.sum(adam_dir * adam_dir)


def general(activations, key_grads, momentum, second_moment, left_roots, right_roots, owners):
    all_heads = lax.all_gather(key_grads, "tp", axis=1, tiled=True)
    panel_rows = activations.shape[1]
    shard_rows = momentum.shape[1]
    columns = all_heads.shape[1]
    blocks = panel_rows // BR
    fsdp_index = lax.axis_index("fsdp")
    tp_index = lax.axis_index("tp")
    first_row = fsdp_index * shard_rows
    my_block = first_row // BR
    offset = first_row - my_block * BR
    summed = lax.psum(contract_tokens(activations, all_heads), "fsdp")
    gradient = lax.dynamic_slice_in_dim(summed, first_row, shard_rows, 0)
    panel_low = summed.astype(jnp.bfloat16)
    new_mom, new_sec, adam_sq = moments(momentum[0], second_moment[0], gradient)
    own_adam = lax.psum(adam_sq, "fsdp")
    owner_row = owners[tp_index]
    owned_slots = owner_row == fsdp_index
    own_block = jnp.sum(jnp.where(owned_slots, jnp.arange(blocks), 0))

    def precondition():
        grad_block = lax.dynamic_slice_in_dim(panel_low, own_block * BR, BR, 0)
        left_product = jnp.dot(
            left_roots[0, 0], grad_block, preferred_element_type=jnp.float32
        ).astype(jnp.bfloat16)
        return jnp.dot(left_product, right_roots[0, 0], preferred_element_type=jnp.float32).astype(
            jnp.bfloat16
        )

    def not_owner():
        return jnp.zeros((BR, columns), jnp.bfloat16)

    result_block = lax.cond(jnp.any(owned_slots), precondition, not_owner)
    update = jnp.zeros((shard_rows, columns), jnp.float32)
    for block_index in range(blocks):
        arrived = spread(result_block, "fsdp", owner_row[block_index])
        widened = lax.optimization_barrier(arrived).astype(jnp.float32)
        pre_sq = jnp.sum(widened * widened)
        my_rows = lax.dynamic_slice_in_dim(widened, offset, shard_rows, 0)
        scaled = my_rows * jnp.sqrt(own_adam / (pre_sq + norm_eps))
        update = jnp.where(my_block == block_index, scaled, update)
    return (update[None], new_mom[None], new_sec[None])


def after(value, *others):
    return lax.optimization_barrier((value, *others))[0]


END_TO_INNER = [(0, 1), (3, 2)]
INNER_TO_END = [(1, 0), (2, 3)]
MIDDLE = [(1, 2), (2, 1)]
PAIR = [(0, 1), (1, 0), (2, 3), (3, 2)]
ACROSS = [(0, 2), (2, 0), (1, 3), (3, 1)]
MIRROR = [(0, 3), (3, 0), (1, 2), (2, 1)]
INNER_GROUPS = [(1, 5), (5, 1), (2, 6), (6, 2)]

TILE = 128
MIB = 1024 * 1024
MOMENT_TILE = 64
CUT = 10
COSTS = (0, 30, 0, 0, 0, 20, 0, 20, 0, 0, 0, 0, 40, 0)
SCALARS = pl.BlockSpec(memory_space=pltpu.SMEM)
VECTORS = pl.BlockSpec(memory_space=pltpu.VMEM)
IN_PLACE = pl.BlockSpec(memory_space=pl.ANY)
GROUP, SIDE, IS_END, CHUNK = 0, 1, 2, 3
ACROSS_OWN, PICK = 0, 1


def spec_of(array):
    if len(array.shape) == 1:
        return SCALARS
    return pl.BlockSpec(array.shape, lambda i: (0,) * len(array.shape))


def on_device(kernel, scalars, inputs, outputs, scratch=(), in_place=(), resident=False, flops=1):
    spec = lambda array: VECTORS if resident and len(array.shape) > 1 else spec_of(array)
    return pl.pallas_call(
        kernel,
        **({} if resident else {"grid": (1,)}),
        in_specs=[SCALARS]
        + [IN_PLACE if k in in_place else spec(array) for k, array in enumerate(inputs)],
        out_specs=[spec(shape) for shape in outputs],
        out_shape=list(outputs),
        scratch_shapes=list(scratch),
        cost_estimate=pl.CostEstimate(flops=flops, bytes_accessed=1, transcendentals=0),
        compiler_params=pltpu.CompilerParams(vmem_limit_bytes=(8 if resident else 32) * MIB),
    )(scalars, *inputs)


def packing(left_tiles, right_tiles):
    sizes = (left_tiles, right_tiles)
    apart = [(r, i, j) for r in range(2) for i in range(sizes[r]) for j in range(i + 1, sizes[r])]
    middle = [(r, i) for r in range(2) for i in range(sizes[r])]
    shared = [tuple(middle[k : k + 2]) for k in range(0, len(middle), 2)]
    most = (len(shared) + 1) // 2
    first = (len(apart) + len(shared) + 1) // 2 - most
    return [apart[:first] + shared[:most], apart[first:] + shared[most:]]


def is_shared(entry):
    return isinstance(entry[0], tuple)


def halves_of(shape):
    row = lax.broadcasted_iota(jnp.int32, shape, 0)
    column = lax.broadcasted_iota(jnp.int32, shape, 1)
    return column > row, column == row


def pack_kernel(lists, first, left_ref, right_ref, piece_ref, *scratch):
    roots = (left_ref, right_ref)
    held_ref, copied = scratch if len(scratch) == 2 else (None, scratch[0])
    count = piece_ref.shape[0] // TILE

    def copy_of(root, i, j, target, semaphore):
        source = roots[root].at[pl.ds(i * TILE, TILE), pl.ds(j * TILE, TILE)]
        return pltpu.make_async_copy(source, target, semaphore)

    for group, entries in enumerate(lists):

        @pl.when(lax.axis_index("groups") == group)
        def _():
            copies, shared = [], []
            for k, entry in enumerate(entries[first : first + count]):
                spot = pl.ds(k * TILE, TILE)
                if not is_shared(entry):
                    copies.append(copy_of(*entry, piece_ref.at[spot, :], copied.at[len(copies)]))
                    continue
                shared.append((spot, len(entry)))
                for n, (root, i) in enumerate(entry):
                    target = held_ref.at[2 * len(shared) - 2 + n]
                    copies.append(copy_of(root, i, i, target, copied.at[len(copies)]))
            for copy in copies:
                copy.start()
            for copy in copies:
                copy.wait()
            if held_ref is None:
                return
            upper, diagonal = halves_of((TILE, TILE))
            apart = jnp.zeros((16, TILE), jnp.float32)
            line = lax.broadcasted_iota(jnp.int32, apart.shape, 0)
            for k, (spot, members) in enumerate(shared):
                one = wide(held_ref.at[2 * k])
                if members == 2:
                    two = wide(held_ref.at[2 * k + 1])
                    middle = jnp.sum(jnp.where(diagonal, two, 0.0), axis=0, keepdims=True)
                    apart = jnp.where(line == k, middle, apart)
                    one = jnp.where(upper | diagonal, one, two)
                piece_ref[spot, :] = one.astype(jnp.bfloat16)
            piece_ref[pl.ds(count * TILE, 16), :] = apart.astype(jnp.bfloat16)


def unpack_kernel(lists, count, place_ref, own_ref, other_ref, left_ref, right_ref):
    targets = (left_ref, right_ref)

    def fill(entries, held_ref):
        apart = wide(held_ref, pl.ds(count * TILE, 16))
        upper, diagonal = halves_of((TILE, TILE))
        shared = 0
        for k, entry in enumerate(entries):
            spot = pl.ds(k * TILE, TILE)
            if not is_shared(entry):
                root, i, j = entry
                tile = held_ref[spot, :]
                targets[root][pl.ds(i * TILE, TILE), pl.ds(j * TILE, TILE)] = tile
                targets[root][pl.ds(j * TILE, TILE), pl.ds(i * TILE, TILE)] = tile.T
                continue
            tile = wide(held_ref, spot)
            turned = tile.T
            middle = apart[shared : shared + 1, :]
            full = (
                jnp.where(upper | diagonal, tile, turned),
                jnp.where(upper, turned, jnp.where(diagonal, middle, tile)),
            )
            for (root, i), value in zip(entry, full):
                place = pl.ds(i * TILE, TILE)
                targets[root][place, place] = value.astype(jnp.bfloat16)
            shared += 1

    for group in range(2):

        @pl.when((place_ref[GROUP] == group) & (place_ref[IS_END] == 0))
        def _():
            fill(lists[group], own_ref)
            fill(lists[1 - group], other_ref)


def choose_kernel(which, count, choice_ref, *refs):
    *sources, out_ref, copied = refs
    choices = len(sources) // count
    for k in range(choices):

        @pl.when(choice_ref[which] == k)
        def _():
            copies, row = [], 0
            for n, source in enumerate(sources[k::choices]):
                target = out_ref.at[pl.ds(row, source.shape[0]), :]
                copies.append(pltpu.make_async_copy(source, target, copied.at[n]))
                row += source.shape[0]
            for copy in copies:
                copy.start()
            for copy in copies:
                copy.wait()


def partial_kernel(place_ref, keys_ref, activations_ref, far_low_ref, near_ref, near_low_ref):
    def block_of(index):
        own = activations_ref[:, pl.ds(pl.multiple_of(index * BR, TILE), BR)]
        return contract_tokens(own, keys_ref[...])

    near = block_of(place_ref[SIDE])
    near_ref[...] = near

    @pl.when(place_ref[IS_END] == 1)
    def _():
        near_low_ref[...] = near.astype(jnp.bfloat16)
        far_low_ref[...] = block_of(1 - place_ref[SIDE]).astype(jnp.bfloat16)


def far_kernel(place_ref, from_end_ref, keys_ref, activations_ref, sum_ref):
    @pl.when(place_ref[IS_END] == 0)
    def _():
        columns = pl.ds(pl.multiple_of((1 - place_ref[SIDE]) * BR, TILE), BR)
        far = contract_tokens(activations_ref[:, columns], keys_ref[...])
        sum_ref[...] = (far + wide(from_end_ref)).astype(jnp.bfloat16)


def rows_of(place_ref, end, rows):
    index = place_ref[SIDE] if end else 1 - place_ref[SIDE]
    return pl.ds(pl.multiple_of(index * rows, 64), rows)


def wide(ref, which=slice(None)):
    return ref[which, :].astype(jnp.float32)


def rest_kernel(place_ref, arrived_ref, near_ref, rest_ref, sum_ref):
    @pl.when(place_ref[IS_END] == 0)
    def _():
        sum_ref[...] = near_ref[...] + wide(arrived_ref)
        rest_ref[...] = sum_ref[rows_of(place_ref, True, rest_ref.shape[0]), :].astype(jnp.bfloat16)


def near_gradient(place_ref, from_end_ref, sum_ref, grad_ref, low_ref):
    rows = grad_ref.shape[0]
    for end in (False, True):
        which = rows_of(place_ref, end, rows)
        grad = sum_ref[which, :] + wide(from_end_ref, which)
        low_ref[which, :] = grad.astype(jnp.bfloat16)
        if not end:
            grad_ref[...] = grad


def gradient_kernel(place_ref, from_end_ref, near_ref, arrived_ref, rest_ref, grad_ref, low_ref, sum_ref):
    rest_kernel(place_ref, arrived_ref, near_ref, rest_ref, sum_ref)

    @pl.when(place_ref[IS_END] == 0)
    def _():
        near_gradient(place_ref, from_end_ref, sum_ref, grad_ref, low_ref)


def left_product(low_ref, left_ref, which):
    return jnp.dot(
        left_ref[which, :], low_ref[...], preferred_element_type=jnp.float32
    ).astype(jnp.bfloat16)


def right_product(place_ref, chunk, product, right_ref):
    which = chunk_columns(place_ref, chunk, product.shape[1])
    return jnp.dot(product, right_ref[which, :], preferred_element_type=jnp.float32)


def left_kernel(place_ref, low_ref, left_ref, right_ref, end_ref, own_ref):
    @pl.when(place_ref[IS_END] == 0)
    def _():
        rows = own_ref.shape[0]
        own_ref[...] = left_product(low_ref, left_ref, rows_of(place_ref, False, rows))
        product = left_product(low_ref, left_ref, rows_of(place_ref, True, rows))
        end_ref[...] = right_product(place_ref, 0, product, right_ref)


def chunk_columns(place_ref, chunk, width):
    return pl.ds(pl.multiple_of(place_ref[CHUNK + chunk] * width, TILE), width)


def end_kernel(
    place_ref, from_end_ref, sum_ref, left_ref, right_ref, before_ref, grad_ref, low_ref, end_ref
):
    @pl.when(place_ref[IS_END] == 0)
    def _():
        near_gradient(place_ref, from_end_ref, sum_ref, grad_ref, low_ref)
        product = left_product(low_ref, left_ref, rows_of(place_ref, True, end_ref.shape[0]))
        total = before_ref[...] + right_product(place_ref, 1, product, right_ref)
        end_ref[...] = total.astype(jnp.bfloat16)


def over_rows(rows, tile, body, start=None):
    step = lambda i, carried: body(pl.multiple_of(i * tile, tile), carried)
    return lax.fori_loop(0, rows // tile, step, start)


def folded(values):
    squares = values * values
    return jnp.sum(squares.reshape(-1, 8, squares.shape[1]), axis=0)


def gradient_of(place_ref, grads, nears, rests):
    inner = lambda c, row: grads[c][pl.ds(row, MOMENT_TILE), :]

    def end(c, row):
        first = pl.multiple_of(place_ref[SIDE] * rests[c].shape[0] + row, 16)
        return nears[c][pl.ds(first, MOMENT_TILE), :] + wide(rests[c], pl.ds(row, MOMENT_TILE))

    return inner, end


def spread_row(sums_ref, row, value):
    sums_ref[pl.ds(row, 1), :] = value * jnp.ones((1, sums_ref.shape[1]), jnp.float32)


def norms_kernel(
    place_ref, low_ref, left_ref, right_ref, before_ref, end_ref, grad_a_ref, grad_b_ref, near_a_ref, near_b_ref,
    rest_a_ref, rest_b_ref, mom_ref, sec_ref, own_ref, sums_ref,
):
    rows, width = grad_a_ref.shape

    def adam(grad_of):
        def body(row, squares):
            which = pl.ds(row, MOMENT_TILE)
            for c in range(2):
                columns = chunk_columns(place_ref, c, width)
                _, _, adam_dir = moments_scaled(
                    mom_ref[0, which, columns], sec_ref[0, which, columns], grad_of(c, row)
                )
                squares = squares + folded(adam_dir)
            return squares

        squares = over_rows(rows, MOMENT_TILE, body, jnp.zeros((8, width), jnp.float32))
        spread_row(sums_ref, 0, jnp.sum(squares))

    inner, end = gradient_of(
        place_ref, (grad_a_ref, grad_b_ref), (near_a_ref, near_b_ref), (rest_a_ref, rest_b_ref)
    )

    @pl.when(place_ref[IS_END] == 0)
    def _():
        product = left_product(low_ref, left_ref, rows_of(place_ref, False, rows))
        total = right_product(place_ref, 0, before_ref[...], right_ref)
        total = total + right_product(place_ref, 1, product, right_ref)
        own_ref[...] = total
        spread_row(sums_ref, 1, jnp.sum(folded(total) + folded(wide(end_ref))))
        adam(inner)

    @pl.when(place_ref[IS_END] == 1)
    def _():
        spread_row(sums_ref, 1, 0.0)
        adam(end)


def state_kernel(
    place_ref, grad_a_ref, grad_b_ref, near_a_ref, near_b_ref, rest_a_ref, rest_b_ref, mom_ref, sec_ref,
    new_mom_ref, new_sec_ref,
):
    rows, width = grad_a_ref.shape

    def state(grad_of):
        def body(row, _):
            which = pl.ds(row, MOMENT_TILE)
            for c in range(2):
                columns = chunk_columns(place_ref, c, width)
                new_mom, new_sec, _ = moments_scaled(
                    mom_ref[0, which, columns], sec_ref[0, which, columns], grad_of(c, row)
                )
                new_mom_ref[0, which, columns] = new_mom
                new_sec_ref[0, which, columns] = new_sec

        over_rows(rows, MOMENT_TILE, body)

    inner, end = gradient_of(
        place_ref, (grad_a_ref, grad_b_ref), (near_a_ref, near_b_ref), (rest_a_ref, rest_b_ref)
    )

    @pl.when(place_ref[IS_END] == 0)
    def _():
        state(inner)

    @pl.when(place_ref[IS_END] == 1)
    def _():
        state(end)


def update_kernel(
    place_ref, end_ref, own_ref, sums_ref, pair_ref, across_ref, mirror_ref, update_ref, held_ref, copied
):
    adam_sq = sums_ref[0:1, :] + pair_ref[0:1, :] + across_ref[0:1, :] + mirror_ref[0:1, :]
    pre_sq = sums_ref[1:2, :] + pair_ref[1:2, :]
    scale = jnp.sqrt(adam_sq / (pre_sq + norm_eps))
    scale = jnp.concatenate([scale] * (held_ref.shape[1] // TILE), 1)
    tiles = copied.shape[0]
    rows = held_ref.shape[0] // tiles

    def write(value_of):
        copies = []
        for k in range(tiles):
            which = pl.ds(k * rows, rows)
            held_ref[which, :] = value_of(which) * scale
            copies.append(
                pltpu.make_async_copy(
                    held_ref.at[which, :], update_ref.at[0, which, :], copied.at[k]
                )
            )
            copies[-1].start()
        for copy in copies:
            copy.wait()

    @pl.when(place_ref[IS_END] == 0)
    def _():
        write(lambda which: own_ref[which, :])

    @pl.when(place_ref[IS_END] == 1)
    def _():
        write(lambda which: wide(end_ref, which))


def line_of_four(activations, key_grads, momentum, second_moment, left_roots, right_roots, owners):
    low = jnp.bfloat16
    group = lax.axis_index("groups")
    z = lax.axis_index("fsdp")
    tp_index = lax.axis_index("tp")
    side = z // 2
    is_end = (z == 0) | (z == 3)
    rows, columns = momentum.shape[1:]
    width = columns // 2
    stacked = lambda *values: jnp.stack(values).astype(jnp.int32)
    place = stacked(group, side, is_end.astype(jnp.int32), tp_index // 2, 1 - tp_index // 2)
    owner_row = owners[tp_index]
    near_owner = owner_row[side]
    far_owner = owner_row[1 - side]
    choice = stacked(
        jnp.where(far_owner == z, 0, 1),
        jnp.where(near_owner == z, 0, jnp.where(near_owner == jnp.where(side == 0, 0, 3), 1, 2)),
    )
    send = lambda value, perm: lax.ppermute(value, "fsdp", perm)
    shape = jax.ShapeDtypeStruct
    history = []

    def step(kernel, inputs, outputs, scalars=place, **kwargs):
        if history:
            inputs = [after(inputs[0], history[-1]), *inputs[1:]]
        flops = 1 + 115_000_000 * COSTS[len(history) - 1]
        out = on_device(kernel, scalars, inputs, outputs, flops=flops, **kwargs)
        history.append(out[0])
        return out

    left = left_roots[0, 0]
    right = right_roots[0, 0]
    lists = packing(left.shape[0] // TILE, right.shape[0] // TILE)
    count = max(len(entries) for entries in lists)
    pieces = []
    for first, tiles in ((0, CUT), (CUT, count - CUT)):
        held = [] if first == 0 else [pltpu.VMEM((2 * tiles, TILE, TILE), low)]
        pieces.append(
            pl.pallas_call(
                functools.partial(pack_kernel, lists, first),
                in_specs=[IN_PLACE] * 2,
                out_specs=VECTORS,
                out_shape=shape((tiles * TILE + 16 * len(held), TILE), low),
                scratch_shapes=[*held, pltpu.SemaphoreType.DMA((2 * tiles,))],
                cost_estimate=pl.CostEstimate(flops=1, bytes_accessed=1, transcendentals=0),
                compiler_params=pltpu.CompilerParams(vmem_limit_bytes=56 * MIB),
            )(after(left, pieces[0]) if pieces else left, right)
        )
    history.append(pieces[1])
    root_end = [send(piece, END_TO_INNER) for piece in pieces]

    first_key = after(key_grads, history[-1])
    far_key = lax.ppermute(first_key, "tp", [(i, i ^ 2) for i in range(4)])
    core_key = lax.ppermute(first_key, "tp", [(i, i ^ 1) for i in range(4)])
    far_core_key = lax.ppermute(far_key, "tp", [(i, i ^ 1) for i in range(4)])
    odd = tp_index % 2 == 1
    joined = lambda one, two: jnp.where(
        odd, jnp.concatenate([two, one], 1), jnp.concatenate([one, two], 1)
    )
    keys_a, keys_b = joined(key_grads, core_key), joined(far_key, far_core_key)
    half = shape((rows, width), jnp.float32)
    block = shape((2 * rows, width), low)

    def partials(keys):
        return step(
            partial_kernel, [keys, activations], [block, shape(block.shape, jnp.float32), block]
        )

    def choose(which, *sources):
        rows = sum(options[0].shape[0] for options in sources)
        (out,) = step(
            functools.partial(choose_kernel, which, len(sources)),
            [array for options in sources for array in options],
            [shape((rows, TILE), low)],
            scalars=choice,
            scratch=[pltpu.SemaphoreType.DMA((len(sources),))],
            in_place=range(len(sources) * len(sources[0])),
        )
        return out

    def far_sum(from_end, keys):
        (out,) = step(far_kernel, [from_end, keys, activations], [block])
        return out

    def cross(k):
        return send(choose(ACROSS_OWN, [pieces[k], root_end[k]]), MIDDLE)

    other_group = lambda value: lax.ppermute(value, ("groups", "fsdp"), INNER_GROUPS)
    far_low_a, near_a, near_low_a = partials(after(keys_a, choice, place))
    far_end_a = send(after(far_low_a, root_end[0]), END_TO_INNER)
    across = [cross(0)]
    far_low_b, near_b, near_low_b = partials(keys_b)
    far_end_b = send(after(far_low_b, root_end[1]), END_TO_INNER)
    across.append(cross(1))
    near_end_a = send(after(near_low_a, history[-1]), END_TO_INNER)
    far_sum_a = far_sum(far_end_a, keys_a)
    arrived_a = send(far_sum_a, MIDDLE)
    picked = choose(PICK, *zip(pieces, root_end, across))
    other = other_group(picked)
    far_sum_b = far_sum(far_end_b, keys_b)
    near_end_b = send(near_low_b, END_TO_INNER)
    arrived_b = send(far_sum_b, MIDDLE)
    full = shape((rows, columns), jnp.float32)
    rest_shape = shape((rows, width), low)
    near_shape = shape(block.shape, jnp.float32)
    rest_a, grad_a, low_a = step(
        gradient_kernel,
        [near_end_a, near_a, arrived_a],
        [rest_shape, half, block],
        scratch=[pltpu.VMEM(near_shape.shape, jnp.float32)],
        resident=True,
    )
    rest_a = send(rest_a, INNER_TO_END)
    block_left, block_right = step(
        functools.partial(unpack_kernel, lists, count),
        [picked, other],
        [shape(left.shape, low), shape(right.shape, low)],
        resident=True,
    )
    rest_b, near_sum = step(
        rest_kernel, [arrived_b, near_b], [rest_shape, near_shape], resident=True
    )
    rest_b = send(rest_b, INNER_TO_END)
    end_before, own_before = step(
        left_kernel, [low_a, block_left, block_right], [full, rest_shape], resident=True
    )
    grad_b, low_b, end_product = step(
        end_kernel,
        [near_end_b, near_sum, block_left, block_right, end_before],
        [half, block, shape((rows, columns), low)],
        resident=True,
    )
    end_received = send(end_product, INNER_TO_END)
    gradients = [grad_a, grad_b, near_a, near_b, rest_a, rest_b, momentum, second_moment]
    own_product, sums = step(
        norms_kernel,
        [low_b, block_left, block_right, own_before, end_product, *gradients],
        [full, shape((8, TILE), jnp.float32)],
        resident=True,
    )
    received = [send(sums, perm) for perm in (PAIR, ACROSS, MIRROR)]
    new_mom, new_sec = step(
        state_kernel, gradients, [shape(momentum.shape, jnp.float32)] * 2, resident=True
    )
    update = pl.pallas_call(
        update_kernel,
        in_specs=[SCALARS] + [VECTORS] * 6,
        out_specs=IN_PLACE,
        out_shape=shape(momentum.shape, jnp.float32),
        scratch_shapes=[pltpu.VMEM((rows, columns), jnp.float32), pltpu.SemaphoreType.DMA((4,))],
        compiler_params=pltpu.CompilerParams(vmem_limit_bytes=8 * MIB),
    )(place, end_received, after(own_product, history[-1]), sums, *received)
    return (update, new_mom, new_sec)


def solution(mesh):
    def per_device(activations, key_grads, momentum, *rest):
        fits = (
            mesh.shape["fsdp"] == 4
            and mesh.shape["tp"] == 4
            and mesh.shape["groups"] == 2
            and momentum.shape[1] * 2 == BR
            and momentum.shape[2] == 4 * TILE
            and activations.shape[1] == 2 * BR
        )
        return (line_of_four if fits else general)(activations, key_grads, momentum, *rest)

    return jax.shard_map(
        per_device,
        mesh=mesh,
        in_specs=(
            P(("groups", "fsdp"), "tp"),
            P(("groups", "fsdp"), "tp"),
            P("tp", "fsdp", None),
            P("tp", "fsdp", None),
            P("fsdp", "tp", None, None),
            P("fsdp", "tp", None, None),
            P(),
        ),
        out_specs=(
            P(("groups", "tp"), "fsdp", None),
            P(("groups", "tp"), "fsdp", None),
            P(("groups", "tp"), "fsdp", None),
        ),
        check_vma=False,
    )
```

```python
import functools

import jax
import jax.numpy as jnp
from jax import lax
from jax.experimental import pallas as pl
from jax.experimental.pallas import tpu as pltpu
from jax.sharding import PartitionSpec as P

BR = 896
STEP = 20


beta_one = 0.9
beta_two = 0.99
adam_eps = 1e-08
norm_eps = 1e-06


def moments_scaled(momentum, second_moment, gradient):
    new_mom = beta_one * momentum + (1.0 - beta_one) * gradient
    new_sec = beta_two * second_moment + (1.0 - beta_two) * gradient * gradient
    adam_dir = (
        new_mom
        * (1.0 / (1.0 - beta_one**STEP))
        / (jnp.sqrt(new_sec * (1.0 / (1.0 - beta_two**STEP))) + adam_eps)
    )
    return new_mom, new_sec, adam_dir


def spread(value, axis, source):
    kept = jnp.where(lax.axis_index(axis) == source, value, 0).astype(value.dtype)
    return lax.psum(kept, axis)


def contract_tokens(left_side, right_side):
    return lax.dot_general(
        left_side, right_side, (((0,), (0,)), ((), ())), preferred_element_type=jnp.float32
    )


def moments(momentum, second_moment, gradient):
    new_mom = beta_one * momentum + (1.0 - beta_one) * gradient
    new_sec = beta_two * second_moment + (1.0 - beta_two) * gradient * gradient
    adam_dir = (
        new_mom / (1.0 - beta_one**STEP) / (jnp.sqrt(new_sec / (1.0 - beta_two**STEP)) + adam_eps)
    )
    return new_mom, new_sec, jnp.sum(adam_dir * adam_dir)


def general(activations, key_grads, momentum, second_moment, left_roots, right_roots, owners):
    all_heads = lax.all_gather(key_grads, "tp", axis=1, tiled=True)
    panel_rows = activations.shape[1]
    shard_rows = momentum.shape[1]
    columns = all_heads.shape[1]
    blocks = panel_rows // BR
    fsdp_index = lax.axis_index("fsdp")
    tp_index = lax.axis_index("tp")
    first_row = fsdp_index * shard_rows
    my_block = first_row // BR
    offset = first_row - my_block * BR
    summed = lax.psum(contract_tokens(activations, all_heads), "fsdp")
    gradient = lax.dynamic_slice_in_dim(summed, first_row, shard_rows, 0)
    panel_low = summed.astype(jnp.bfloat16)
    new_mom, new_sec, adam_sq = moments(momentum[0], second_moment[0], gradient)
    own_adam = lax.psum(adam_sq, "fsdp")
    owner_row = owners[tp_index]
    owned_slots = owner_row == fsdp_index
    own_block = jnp.sum(jnp.where(owned_slots, jnp.arange(blocks), 0))

    def precondition():
        grad_block = lax.dynamic_slice_in_dim(panel_low, own_block * BR, BR, 0)
        left_product = jnp.dot(
            left_roots[0, 0], grad_block, preferred_element_type=jnp.float32
        ).astype(jnp.bfloat16)
        return jnp.dot(left_product, right_roots[0, 0], preferred_element_type=jnp.float32).astype(
            jnp.bfloat16
        )

    def not_owner():
        return jnp.zeros((BR, columns), jnp.bfloat16)

    result_block = lax.cond(jnp.any(owned_slots), precondition, not_owner)
    update = jnp.zeros((shard_rows, columns), jnp.float32)
    for block_index in range(blocks):
        arrived = spread(result_block, "fsdp", owner_row[block_index])
        widened = lax.optimization_barrier(arrived).astype(jnp.float32)
        pre_sq = jnp.sum(widened * widened)
        my_rows = lax.dynamic_slice_in_dim(widened, offset, shard_rows, 0)
        scaled = my_rows * jnp.sqrt(own_adam / (pre_sq + norm_eps))
        update = jnp.where(my_block == block_index, scaled, update)
    return (update[None], new_mom[None], new_sec[None])


def after(value, *others):
    return lax.optimization_barrier((value, *others))[0]


END_TO_INNER = [(0, 1), (3, 2)]
INNER_TO_END = [(1, 0), (2, 3)]
MIDDLE = [(1, 2), (2, 1)]
PAIR = [(0, 1), (1, 0), (2, 3), (3, 2)]
ACROSS = [(0, 2), (2, 0), (1, 3), (3, 1)]
MIRROR = [(0, 3), (3, 0), (1, 2), (2, 1)]
INNER_GROUPS = [(1, 5), (5, 1), (2, 6), (6, 2)]

TILE = 128
MIB = 1024 * 1024
MOMENT_TILE = 64
CUT = 10
COSTS = (0, 30, 0, 0, 0, 20, 0, 20, 0, 0, 0, 0, 40, 0)
SCALARS = pl.BlockSpec(memory_space=pltpu.SMEM)
VECTORS = pl.BlockSpec(memory_space=pltpu.VMEM)
IN_PLACE = pl.BlockSpec(memory_space=pl.ANY)
GROUP, SIDE, IS_END, CHUNK = 0, 1, 2, 3
ACROSS_OWN, PICK = 0, 1


def spec_of(array):
    if len(array.shape) == 1:
        return SCALARS
    return pl.BlockSpec(array.shape, lambda i: (0,) * len(array.shape))


def on_device(kernel, scalars, inputs, outputs, scratch=(), in_place=(), resident=False, flops=1):
    spec = lambda array: VECTORS if resident and len(array.shape) > 1 else spec_of(array)
    return pl.pallas_call(
        kernel,
        **({} if resident else {"grid": (1,)}),
        in_specs=[SCALARS]
        + [IN_PLACE if k in in_place else spec(array) for k, array in enumerate(inputs)],
        out_specs=[spec(shape) for shape in outputs],
        out_shape=list(outputs),
        scratch_shapes=list(scratch),
        cost_estimate=pl.CostEstimate(flops=flops, bytes_accessed=1, transcendentals=0),
        compiler_params=pltpu.CompilerParams(vmem_limit_bytes=(8 if resident else 32) * MIB),
    )(scalars, *inputs)


def packing(left_tiles, right_tiles):
    sizes = (left_tiles, right_tiles)
    apart = [(r, i, j) for r in range(2) for i in range(sizes[r]) for j in range(i + 1, sizes[r])]
    middle = [(r, i) for r in range(2) for i in range(sizes[r])]
    shared = [tuple(middle[k : k + 2]) for k in range(0, len(middle), 2)]
    most = (len(shared) + 1) // 2
    first = (len(apart) + len(shared) + 1) // 2 - most
    return [apart[:first] + shared[:most], apart[first:] + shared[most:]]


def is_shared(entry):
    return isinstance(entry[0], tuple)


def halves_of(shape):
    row = lax.broadcasted_iota(jnp.int32, shape, 0)
    column = lax.broadcasted_iota(jnp.int32, shape, 1)
    return column > row, column == row


def pack_kernel(lists, first, left_ref, right_ref, piece_ref, *scratch):
    roots = (left_ref, right_ref)
    held_ref, copied = scratch if len(scratch) == 2 else (None, scratch[0])
    count = piece_ref.shape[0] // TILE

    def copy_of(root, i, j, target, semaphore):
        source = roots[root].at[pl.ds(i * TILE, TILE), pl.ds(j * TILE, TILE)]
        return pltpu.make_async_copy(source, target, semaphore)

    for group, entries in enumerate(lists):

        @pl.when(lax.axis_index("groups") == group)
        def _():
            copies, shared = [], []
            for k, entry in enumerate(entries[first : first + count]):
                spot = pl.ds(k * TILE, TILE)
                if not is_shared(entry):
                    copies.append(copy_of(*entry, piece_ref.at[spot, :], copied.at[len(copies)]))
                    continue
                shared.append((spot, len(entry)))
                for n, (root, i) in enumerate(entry):
                    target = held_ref.at[2 * len(shared) - 2 + n]
                    copies.append(copy_of(root, i, i, target, copied.at[len(copies)]))
            for copy in copies:
                copy.start()
            for copy in copies:
                copy.wait()
            if held_ref is None:
                return
            upper, diagonal = halves_of((TILE, TILE))
            apart = jnp.zeros((16, TILE), jnp.float32)
            line = lax.broadcasted_iota(jnp.int32, apart.shape, 0)
            for k, (spot, members) in enumerate(shared):
                one = wide(held_ref.at[2 * k])
                if members == 2:
                    two = wide(held_ref.at[2 * k + 1])
                    middle = jnp.sum(jnp.where(diagonal, two, 0.0), axis=0, keepdims=True)
                    apart = jnp.where(line == k, middle, apart)
                    one = jnp.where(upper | diagonal, one, two)
                piece_ref[spot, :] = one.astype(jnp.bfloat16)
            piece_ref[pl.ds(count * TILE, 16), :] = apart.astype(jnp.bfloat16)


def unpack_kernel(lists, count, place_ref, own_ref, other_ref, left_ref, right_ref):
    targets = (left_ref, right_ref)

    def fill(entries, held_ref):
        apart = wide(held_ref, pl.ds(count * TILE, 16))
        upper, diagonal = halves_of((TILE, TILE))
        shared = 0
        for k, entry in enumerate(entries):
            spot = pl.ds(k * TILE, TILE)
            if not is_shared(entry):
                root, i, j = entry
                tile = held_ref[spot, :]
                targets[root][pl.ds(i * TILE, TILE), pl.ds(j * TILE, TILE)] = tile
                targets[root][pl.ds(j * TILE, TILE), pl.ds(i * TILE, TILE)] = tile.T
                continue
            tile = wide(held_ref, spot)
            turned = tile.T
            middle = apart[shared : shared + 1, :]
            full = (
                jnp.where(upper | diagonal, tile, turned),
                jnp.where(upper, turned, jnp.where(diagonal, middle, tile)),
            )
            for (root, i), value in zip(entry, full):
                place = pl.ds(i * TILE, TILE)
                targets[root][place, place] = value.astype(jnp.bfloat16)
            shared += 1

    for group in range(2):

        @pl.when((place_ref[GROUP] == group) & (place_ref[IS_END] == 0))
        def _():
            fill(lists[group], own_ref)
            fill(lists[1 - group], other_ref)


def choose_kernel(which, count, choice_ref, *refs):
    *sources, out_ref, copied = refs
    choices = len(sources) // count
    for k in range(choices):

        @pl.when(choice_ref[which] == k)
        def _():
            copies, row = [], 0
            for n, source in enumerate(sources[k::choices]):
                target = out_ref.at[pl.ds(row, source.shape[0]), :]
                copies.append(pltpu.make_async_copy(source, target, copied.at[n]))
                row += source.shape[0]
            for copy in copies:
                copy.start()
            for copy in copies:
                copy.wait()


def partial_kernel(place_ref, keys_ref, activations_ref, far_low_ref, near_ref, near_low_ref):
    def block_of(index):
        own = activations_ref[:, pl.ds(pl.multiple_of(index * BR, TILE), BR)]
        return contract_tokens(own, keys_ref[...])

    near = block_of(place_ref[SIDE])
    near_ref[...] = near

    @pl.when(place_ref[IS_END] == 1)
    def _():
        near_low_ref[...] = near.astype(jnp.bfloat16)
        far_low_ref[...] = block_of(1 - place_ref[SIDE]).astype(jnp.bfloat16)


def far_kernel(place_ref, from_end_ref, keys_ref, activations_ref, sum_ref):
    @pl.when(place_ref[IS_END] == 0)
    def _():
        columns = pl.ds(pl.multiple_of((1 - place_ref[SIDE]) * BR, TILE), BR)
        far = contract_tokens(activations_ref[:, columns], keys_ref[...])
        sum_ref[...] = (far + wide(from_end_ref)).astype(jnp.bfloat16)


def rows_of(place_ref, end, rows):
    index = place_ref[SIDE] if end else 1 - place_ref[SIDE]
    return pl.ds(pl.multiple_of(index * rows, 64), rows)


def wide(ref, which=slice(None)):
    return ref[which, :].astype(jnp.float32)


def rest_kernel(place_ref, arrived_ref, near_ref, rest_ref, sum_ref):
    @pl.when(place_ref[IS_END] == 0)
    def _():
        sum_ref[...] = near_ref[...] + wide(arrived_ref)
        rest_ref[...] = sum_ref[rows_of(place_ref, True, rest_ref.shape[0]), :].astype(jnp.bfloat16)


def near_gradient(place_ref, from_end_ref, sum_ref, grad_ref, low_ref):
    rows = low_ref.shape[0] // 2
    for end in (False, True):
        which = rows_of(place_ref, end, rows)
        grad = sum_ref[which, :] + wide(from_end_ref, which)
        low_ref[which, :] = grad.astype(jnp.bfloat16)
        if not end and grad_ref is not None:
            grad_ref[...] = grad


def gradient_kernel(place_ref, from_end_ref, near_ref, arrived_ref, rest_ref, grad_ref, low_ref, sum_ref):
    rest_kernel(place_ref, arrived_ref, near_ref, rest_ref, sum_ref)

    @pl.when(place_ref[IS_END] == 0)
    def _():
        near_gradient(place_ref, from_end_ref, sum_ref, grad_ref, low_ref)


def left_product(low_ref, left_ref, which):
    return jnp.dot(
        left_ref[which, :], low_ref[...], preferred_element_type=jnp.float32
    ).astype(jnp.bfloat16)


def right_product(place_ref, chunk, product, right_ref):
    which = chunk_columns(place_ref, chunk, product.shape[1])
    return jnp.dot(product, right_ref[which, :], preferred_element_type=jnp.float32)


def left_kernel(place_ref, low_ref, left_ref, right_ref, end_ref, own_ref):
    @pl.when(place_ref[IS_END] == 0)
    def _():
        rows = own_ref.shape[0]
        own_ref[...] = left_product(low_ref, left_ref, rows_of(place_ref, False, rows))
        product = left_product(low_ref, left_ref, rows_of(place_ref, True, rows))
        end_ref[...] = right_product(place_ref, 0, product, right_ref)


def chunk_columns(place_ref, chunk, width):
    return pl.ds(pl.multiple_of(place_ref[CHUNK + chunk] * width, TILE), width)


def end_kernel(
    place_ref, from_end_ref, sum_ref, left_ref, right_ref, before_ref, low_ref, end_ref
):
    @pl.when(place_ref[IS_END] == 0)
    def _():
        near_gradient(place_ref, from_end_ref, sum_ref, None, low_ref)
        product = left_product(low_ref, left_ref, rows_of(place_ref, True, end_ref.shape[0]))
        total = before_ref[...] + right_product(place_ref, 1, product, right_ref)
        end_ref[...] = total.astype(jnp.bfloat16)


def over_rows(rows, tile, body, start=None):
    step = lambda i, carried: body(pl.multiple_of(i * tile, tile), carried)
    return lax.fori_loop(0, rows // tile, step, start)


def folded(values):
    squares = values * values
    return jnp.sum(squares.reshape(-1, 8, squares.shape[1]), axis=0)


def gradient_of(place_ref, grads, nears, rests):
    inner = lambda c, row: grads[c][pl.ds(row, MOMENT_TILE), :]

    def end(c, row):
        first = pl.multiple_of(place_ref[SIDE] * rests[c].shape[0] + row, 16)
        return nears[c][pl.ds(first, MOMENT_TILE), :] + wide(rests[c], pl.ds(row, MOMENT_TILE))

    return inner, end


def spread_row(sums_ref, row, value):
    sums_ref[pl.ds(row, 1), :] = value * jnp.ones((1, sums_ref.shape[1]), jnp.float32)


def norms_kernel(
    place_ref, low_ref, left_ref, right_ref, before_ref, end_ref, from_end_ref, sum_ref, grad_a_ref, near_a_ref, near_b_ref,
    rest_a_ref, rest_b_ref, mom_ref, sec_ref, own_ref, sums_ref, grad_b_ref,
):
    rows, width = grad_a_ref.shape

    def adam(grad_of):
        def body(row, squares):
            which = pl.ds(row, MOMENT_TILE)
            for c in range(2):
                columns = chunk_columns(place_ref, c, width)
                _, _, adam_dir = moments_scaled(
                    mom_ref[0, which, columns], sec_ref[0, which, columns], grad_of(c, row)
                )
                squares = squares + folded(adam_dir)
            return squares

        squares = over_rows(rows, MOMENT_TILE, body, jnp.zeros((8, width), jnp.float32))
        spread_row(sums_ref, 0, jnp.sum(squares))

    inner, end = gradient_of(
        place_ref, (grad_a_ref, grad_b_ref), (near_a_ref, near_b_ref), (rest_a_ref, rest_b_ref)
    )

    @pl.when(place_ref[IS_END] == 0)
    def _():
        which = rows_of(place_ref, False, rows)
        grad_b_ref[...] = sum_ref[which, :] + wide(from_end_ref, which)
        product = left_product(low_ref, left_ref, rows_of(place_ref, False, rows))
        total = right_product(place_ref, 0, before_ref[...], right_ref)
        total = total + right_product(place_ref, 1, product, right_ref)
        own_ref[...] = total
        spread_row(sums_ref, 1, jnp.sum(folded(total) + folded(wide(end_ref))))
        adam(inner)

    @pl.when(place_ref[IS_END] == 1)
    def _():
        spread_row(sums_ref, 1, 0.0)
        adam(end)


def state_kernel(
    place_ref, grad_a_ref, grad_b_ref, near_a_ref, near_b_ref, rest_a_ref, rest_b_ref, mom_ref, sec_ref,
    new_mom_ref, new_sec_ref,
):
    rows, width = grad_a_ref.shape

    def state(grad_of):
        def body(row, _):
            which = pl.ds(row, MOMENT_TILE)
            for c in range(2):
                columns = chunk_columns(place_ref, c, width)
                new_mom, new_sec, _ = moments_scaled(
                    mom_ref[0, which, columns], sec_ref[0, which, columns], grad_of(c, row)
                )
                new_mom_ref[0, which, columns] = new_mom
                new_sec_ref[0, which, columns] = new_sec

        over_rows(rows, MOMENT_TILE, body)

    inner, end = gradient_of(
        place_ref, (grad_a_ref, grad_b_ref), (near_a_ref, near_b_ref), (rest_a_ref, rest_b_ref)
    )

    @pl.when(place_ref[IS_END] == 0)
    def _():
        state(inner)

    @pl.when(place_ref[IS_END] == 1)
    def _():
        state(end)


def update_kernel(
    place_ref, end_ref, own_ref, sums_ref, pair_ref, across_ref, mirror_ref, update_ref, held_ref, copied
):
    adam_sq = sums_ref[0:1, :] + pair_ref[0:1, :] + across_ref[0:1, :] + mirror_ref[0:1, :]
    pre_sq = sums_ref[1:2, :] + pair_ref[1:2, :]
    scale = jnp.sqrt(adam_sq / (pre_sq + norm_eps))
    scale = jnp.concatenate([scale] * (held_ref.shape[1] // TILE), 1)
    tiles = copied.shape[0]
    rows = held_ref.shape[0] // tiles

    def write(value_of):
        copies = []
        for k in range(tiles):
            which = pl.ds(k * rows, rows)
            held_ref[which, :] = value_of(which) * scale
            copies.append(
                pltpu.make_async_copy(
                    held_ref.at[which, :], update_ref.at[0, which, :], copied.at[k]
                )
            )
            copies[-1].start()
        for copy in copies:
            copy.wait()

    @pl.when(place_ref[IS_END] == 0)
    def _():
        write(lambda which: own_ref[which, :])

    @pl.when(place_ref[IS_END] == 1)
    def _():
        write(lambda which: wide(end_ref, which))


def line_of_four(activations, key_grads, momentum, second_moment, left_roots, right_roots, owners):
    low = jnp.bfloat16
    group = lax.axis_index("groups")
    z = lax.axis_index("fsdp")
    tp_index = lax.axis_index("tp")
    side = z // 2
    is_end = (z == 0) | (z == 3)
    rows, columns = momentum.shape[1:]
    width = columns // 2
    stacked = lambda *values: jnp.stack(values).astype(jnp.int32)
    place = stacked(group, side, is_end.astype(jnp.int32), tp_index // 2, 1 - tp_index // 2)
    owner_row = owners[tp_index]
    near_owner = owner_row[side]
    far_owner = owner_row[1 - side]
    choice = stacked(
        jnp.where(far_owner == z, 0, 1),
        jnp.where(near_owner == z, 0, jnp.where(near_owner == jnp.where(side == 0, 0, 3), 1, 2)),
    )
    send = lambda value, perm: lax.ppermute(value, "fsdp", perm)
    shape = jax.ShapeDtypeStruct
    history = []

    def step(kernel, inputs, outputs, scalars=place, **kwargs):
        if history:
            inputs = [after(inputs[0], history[-1]), *inputs[1:]]
        flops = 1 + 115_000_000 * COSTS[len(history) - 1]
        out = on_device(kernel, scalars, inputs, outputs, flops=flops, **kwargs)
        history.append(out[0])
        return out

    left = left_roots[0, 0]
    right = right_roots[0, 0]
    lists = packing(left.shape[0] // TILE, right.shape[0] // TILE)
    count = max(len(entries) for entries in lists)
    pieces = []
    for first, tiles in ((0, CUT), (CUT, count - CUT)):
        held = [] if first == 0 else [pltpu.VMEM((2 * tiles, TILE, TILE), low)]
        pieces.append(
            pl.pallas_call(
                functools.partial(pack_kernel, lists, first),
                in_specs=[IN_PLACE] * 2,
                out_specs=VECTORS,
                out_shape=shape((tiles * TILE + 16 * len(held), TILE), low),
                scratch_shapes=[*held, pltpu.SemaphoreType.DMA((2 * tiles,))],
                cost_estimate=pl.CostEstimate(flops=1, bytes_accessed=1, transcendentals=0),
                compiler_params=pltpu.CompilerParams(vmem_limit_bytes=56 * MIB),
            )(after(left, pieces[0]) if pieces else left, right)
        )
    history.append(pieces[1])
    root_end = [send(piece, END_TO_INNER) for piece in pieces]

    first_key = after(key_grads, history[-1])
    far_key = lax.ppermute(first_key, "tp", [(i, i ^ 2) for i in range(4)])
    core_key = lax.ppermute(first_key, "tp", [(i, i ^ 1) for i in range(4)])
    far_core_key = lax.ppermute(far_key, "tp", [(i, i ^ 1) for i in range(4)])
    odd = tp_index % 2 == 1
    joined = lambda one, two: jnp.where(
        odd, jnp.concatenate([two, one], 1), jnp.concatenate([one, two], 1)
    )
    keys_a, keys_b = joined(key_grads, core_key), joined(far_key, far_core_key)
    half = shape((rows, width), jnp.float32)
    block = shape((2 * rows, width), low)

    def partials(keys):
        return step(
            partial_kernel, [keys, activations], [block, shape(block.shape, jnp.float32), block]
        )

    def choose(which, *sources):
        rows = sum(options[0].shape[0] for options in sources)
        (out,) = step(
            functools.partial(choose_kernel, which, len(sources)),
            [array for options in sources for array in options],
            [shape((rows, TILE), low)],
            scalars=choice,
            scratch=[pltpu.SemaphoreType.DMA((len(sources),))],
            in_place=range(len(sources) * len(sources[0])),
        )
        return out

    def far_sum(from_end, keys):
        (out,) = step(far_kernel, [from_end, keys, activations], [block])
        return out

    def cross(k):
        return send(choose(ACROSS_OWN, [pieces[k], root_end[k]]), MIDDLE)

    other_group = lambda value: lax.ppermute(value, ("groups", "fsdp"), INNER_GROUPS)
    far_low_a, near_a, near_low_a = partials(after(keys_a, choice, place))
    far_end_a = send(after(far_low_a, root_end[0]), END_TO_INNER)
    across = [cross(0)]
    far_low_b, near_b, near_low_b = partials(keys_b)
    far_end_b = send(after(far_low_b, root_end[1]), END_TO_INNER)
    across.append(cross(1))
    near_end_a = send(after(near_low_a, history[-1]), END_TO_INNER)
    far_sum_a = far_sum(far_end_a, keys_a)
    arrived_a = send(far_sum_a, MIDDLE)
    picked = choose(PICK, *zip(pieces, root_end, across))
    other = other_group(picked)
    far_sum_b = far_sum(far_end_b, keys_b)
    near_end_b = send(near_low_b, END_TO_INNER)
    arrived_b = send(far_sum_b, MIDDLE)
    full = shape((rows, columns), jnp.float32)
    rest_shape = shape((rows, width), low)
    near_shape = shape(block.shape, jnp.float32)
    rest_a, grad_a, low_a = step(
        gradient_kernel,
        [near_end_a, near_a, arrived_a],
        [rest_shape, half, block],
        scratch=[pltpu.VMEM(near_shape.shape, jnp.float32)],
        resident=True,
    )
    rest_a = send(rest_a, INNER_TO_END)
    block_left, block_right = step(
        functools.partial(unpack_kernel, lists, count),
        [picked, other],
        [shape(left.shape, low), shape(right.shape, low)],
        resident=True,
    )
    rest_b, near_sum = step(
        rest_kernel, [arrived_b, near_b], [rest_shape, near_shape], resident=True
    )
    rest_b = send(rest_b, INNER_TO_END)
    end_before, own_before = step(
        left_kernel, [low_a, block_left, block_right], [full, rest_shape], resident=True
    )
    low_b, end_product = step(
        end_kernel,
        [near_end_b, near_sum, block_left, block_right, end_before],
        [block, shape((rows, columns), low)],
        resident=True,
    )
    end_received = send(end_product, INNER_TO_END)
    others = [near_a, near_b, rest_a, rest_b, momentum, second_moment]
    own_product, sums, grad_b = step(
        norms_kernel,
        [low_b, block_left, block_right, own_before, end_product, near_end_b, near_sum, grad_a, *others],
        [full, shape((8, TILE), jnp.float32), half],
        resident=True,
    )
    received = [send(sums, perm) for perm in (PAIR, ACROSS, MIRROR)]
    new_mom, new_sec = step(
        state_kernel, [grad_a, grad_b, *others], [shape(momentum.shape, jnp.float32)] * 2, resident=True
    )
    update = pl.pallas_call(
        update_kernel,
        in_specs=[SCALARS] + [VECTORS] * 6,
        out_specs=IN_PLACE,
        out_shape=shape(momentum.shape, jnp.float32),
        scratch_shapes=[pltpu.VMEM((rows, columns), jnp.float32), pltpu.SemaphoreType.DMA((4,))],
        compiler_params=pltpu.CompilerParams(vmem_limit_bytes=8 * MIB),
    )(place, end_received, after(own_product, history[-1]), sums, *received)
    return (update, new_mom, new_sec)


def solution(mesh):
    def per_device(activations, key_grads, momentum, *rest):
        fits = (
            mesh.shape["fsdp"] == 4
            and mesh.shape["tp"] == 4
            and mesh.shape["groups"] == 2
            and momentum.shape[1] * 2 == BR
            and momentum.shape[2] == 4 * TILE
            and activations.shape[1] == 2 * BR
        )
        return (line_of_four if fits else general)(activations, key_grads, momentum, *rest)

    return jax.shard_map(
        per_device,
        mesh=mesh,
        in_specs=(
            P(("groups", "fsdp"), "tp"),
            P(("groups", "fsdp"), "tp"),
            P("tp", "fsdp", None),
            P("tp", "fsdp", None),
            P("fsdp", "tp", None, None),
            P("fsdp", "tp", None, None),
            P(),
        ),
        out_specs=(
            P(("groups", "tp"), "fsdp", None),
            P(("groups", "tp"), "fsdp", None),
            P(("groups", "tp"), "fsdp", None),
        ),
        check_vma=False,
    )
```
